32 devices in a mesh: fsdp: 8 (over y, x, core), tp: 4 (over z).
Axes of the slice: x: 2, y: 2, z: 4, core: 2. Of those that a mesh axis runs over, the one named last changes fastest.
Arguments:
- tokens: bfloat16 [32768, 1024], P(('fsdp', 'tp')), may hold values from -6 to 6
- segments: int32 [32, 1024], P('fsdp'), may hold values from 0 to 6, as said below
- attn_gain: bfloat16 [1024], replicated, may hold values from 0.099609375 to 1.8984375
- attn_shift: bfloat16 [1024], replicated, may hold values from -1.75 to 1.75
- mlp_gain: bfloat16 [1024], replicated, may hold values from 0.099609375 to 1.8984375
- mlp_shift: bfloat16 [1024], replicated, may hold values from -1.75 to 1.75
- qkv_weight: bfloat16 [1024, 3, 1024], P('fsdp', None, 'tp'), may hold values from -0.1875 to 0.1875
- qkv_bias: bfloat16 [3, 1024], replicated, may hold values from -3 to 3
- out_weight: bfloat16 [1024, 1024], P('tp', 'fsdp'), may hold values from -0.75 to 0.75
- out_bias: bfloat16 [1024], replicated, may hold values from -1.75 to 1.75
- up_weight: bfloat16 [1024, 4096], P('fsdp', 'tp'), may hold values from -0.1875 to 0.1875
- up_bias: bfloat16 [4096], replicated, may hold values from -3 to 3
- down_weight: bfloat16 [4096, 1024], P('tp', 'fsdp'), may hold values from -0.09375 to 0.09375
- down_bias: bfloat16 [1024], replicated, may hold values from -1.75 to 1.75
- cotangent: bfloat16 [32768, 1024], P(('fsdp', 'tp')), may hold values from -6 to 6
Outputs:
- output: bfloat16 [32768, 1024], P(('fsdp', 'tp'))
- input_grad: float32 [32768, 1024], P(('fsdp', 'tp'))
- attn_gain_grad: float32 [1024], replicated
- attn_shift_grad: float32 [1024], replicated
- mlp_gain_grad: float32 [1024], replicated
- mlp_shift_grad: float32 [1024], replicated
- qkv_weight_grad: float32 [1024, 3, 1024], P('fsdp', None, 'tp')
- qkv_bias_grad: float32 [3, 1024], replicated
- out_weight_grad: float32 [1024, 1024], P('tp', 'fsdp')
- out_bias_grad: float32 [1024], replicated
- up_weight_grad: float32 [1024, 4096], P('fsdp', 'tp')
- up_bias_grad: float32 [4096], replicated
- down_weight_grad: float32 [4096, 1024], P('tp', 'fsdp')
- down_bias_grad: float32 [1024], replicated
The draws below stay inside these ranges and needn't reach their ends.
Inputs may be any that keep to these rules, and one draw needn't show every extreme that they name: `segments`: each packed sequence is a window of 1024 tokens cut from a stream of documents whose lengths lie between about 0.2 * 1024 and 2048; a sequence's segment numbers count its pieces from 0 and never fall, and only its first and last piece can be shorter than a whole document.
All inputs are finite; a program needn't handle non-finite values.
Results may differ from the reference program's by a relative error of at most 0.012.
Values may be sent and summed in bfloat16 or wider, within the bound.
No kernel may reach another device: no remote copies, remote signals or barrier semaphores. Data moves between devices by JAX's collectives and lax.ppermute only.
A program may use at most 256 MiB of HBM per device.

```python
import math
import jax
import jax.numpy as jnp
from jax import lax

D = 1024
H = 16
HD = 64
FF = 4096
ROT = 16
LEN = 1024
TOK_DEV = 1024
TOKENS = 32768
NSEQ = 32
N_FSDP = 8
N_TP = 4


def draw_segments(key, part):
    key = jax.random.fold_in(key, 11)
    shortest = max(2, LEN * 25 // 128)
    longest = max(shortest + 1, LEN * 125 // 64)
    pieces = LEN // shortest + 2
    first_key, rest_key, pick_key = jax.random.split(key, 3)
    first_piece = jax.random.randint(first_key, (NSEQ, 1), 1, longest + 1, dtype=jnp.int32)
    later = jax.random.randint(rest_key, (NSEQ, pieces - 1), shortest, longest + 1, dtype=jnp.int32)
    chosen = jax.random.randint(pick_key, (), 0, NSEQ, dtype=jnp.int32)
    row_ids = jnp.arange(NSEQ, dtype=jnp.int32)[:, None]
    first_piece = jnp.where(row_ids == chosen, 1, first_piece).astype(jnp.int32)
    later = jnp.where(row_ids == chosen, shortest, later).astype(jnp.int32)
    bounds = jnp.cumsum(jnp.concatenate([first_piece, later], axis=1), axis=1)
    column = jnp.arange(LEN, dtype=jnp.int32)
    passed = (bounds[:, None, :] <= column[None, :, None]).astype(jnp.int32)
    return jnp.sum(passed, axis=-1).astype(jnp.int32)


def levels(rng, dims, cuts, least, top_value):
    loudness = 1.0
    for axis_at, blocks in cuts:
        heights = jax.random.uniform(jax.random.fold_in(jax.random.fold_in(rng, 6), axis_at), (blocks,), jnp.float32, least / len(cuts), top_value / len(cuts))
        loudness = loudness * jnp.repeat(jnp.exp(heights), dims[axis_at] // blocks).reshape((-1,) + (1,) * (len(dims) - 1 - axis_at))
    return loudness


def gaussian(rng, shape, scale, most, cuts=(), kind=jnp.bfloat16):
    values = scale * jax.random.normal(rng, shape, jnp.float32)
    if cuts:
        values = values * levels(rng, shape, cuts, -0.22, 0.18)
    return jnp.clip(values, -most, most).astype(kind)


def setup_inputs(seed: int = 0) -> dict:
    streams_of = jax.random.split(jax.random.key(seed), 16)
    tokens = gaussian(streams_of[0], (TOKENS, D), 1.0, 6.0, ((0, 32),))
    segments = draw_segments(jax.random.fold_in(streams_of[15], 71), 0)
    attn_gain = jnp.clip(1.0 + 0.18 * jax.random.normal(streams_of[2], (D,), jnp.float32), 0.099609375, 1.8984375).astype(jnp.bfloat16)
    attn_shift = gaussian(streams_of[3], (D,), 0.3, 1.75)
    mlp_gain = jnp.clip(1.0 + 0.18 * jax.random.normal(streams_of[4], (D,), jnp.float32), 0.099609375, 1.8984375).astype(jnp.bfloat16)
    mlp_shift = gaussian(streams_of[5], (D,), 0.3, 1.75)
    qkv_weight = gaussian(streams_of[6], (D, 3, H * HD), D ** -0.5, 0.1875, ((0, 8), (2, 4)))
    qkv_bias = gaussian(streams_of[7], (3, H * HD), 0.5, 3.0)
    out_weight = gaussian(streams_of[8], (H * HD, D), (H * HD // 16) ** -0.5, 0.75, ((0, 4), (1, 8)))
    out_bias = gaussian(streams_of[9], (D,), 0.3, 1.75)
    up_weight = gaussian(streams_of[10], (D, FF), D ** -0.5, 0.1875, ((0, 8), (1, 4)))
    up_bias = gaussian(streams_of[11], (FF,), 0.5, 3.0)
    down_weight = gaussian(streams_of[12], (FF, D), FF ** -0.5, 0.09375, ((0, 4), (1, 8)))
    down_bias = gaussian(streams_of[13], (D,), 0.3, 1.75)
    cotangent = gaussian(streams_of[14], (TOKENS, D), 1.0, 6.0, ((0, 32),))
    return {"tokens": tokens, "segments": segments, "attn_gain": attn_gain, "attn_shift": attn_shift, "mlp_gain": mlp_gain, "mlp_shift": mlp_shift, "qkv_weight": qkv_weight, "qkv_bias": qkv_bias, "out_weight": out_weight, "out_bias": out_bias, "up_weight": up_weight, "up_bias": up_bias, "down_weight": down_weight, "down_bias": down_bias, "cotangent": cotangent}


@jax.custom_vjp
def low(v):
    return lax.optimization_barrier(v.astype(jnp.bfloat16)).astype(jnp.float32)

@jax.custom_vjp
def low_back(v):
    return v

def low_keep(v):
    return (low(v), None)

def low_pass(kept, grad):
    return (grad,)

def back_keep(v):
    return (v, None)

def back_low(kept, grad):
    return (low(grad),)
low.defvjp(low_keep, low_pass)
low_back.defvjp(back_keep, back_low)
EPS = 1e-05
NEG = -1000000000.0
PRECISE = lax.Precision.HIGHEST

def layer_norm(values, gain_row, shift_row):
    centre = values - lax.optimization_barrier(jnp.mean(values, axis=-1, keepdims=True))
    spread = lax.optimization_barrier(jnp.mean(centre * centre, axis=-1, keepdims=True))
    return centre * lax.rsqrt(spread + EPS) * gain_row + shift_row

def doc_positions(segment_ids):
    length = segment_ids.shape[-1]
    column = jnp.arange(length, dtype=jnp.int32)
    before = jnp.concatenate([jnp.full(segment_ids.shape[:-1] + (1,), -1, jnp.int32), segment_ids[..., :-1]], axis=-1)
    starts = lax.cummax(jnp.where(segment_ids != before, column, 0), axis=segment_ids.ndim - 1)
    return column - starts

def rotary_tables(segment_ids):
    inverse_freq = jnp.power(10000.0, -jnp.arange(0, ROT, 2, dtype=jnp.float32) / ROT)
    places = doc_positions(segment_ids).reshape(-1).astype(jnp.float32)
    angles = places[:, None] * inverse_freq[None, :]
    return (jnp.cos(angles)[:, None, :], jnp.sin(angles)[:, None, :])

def rotate(head_values, cos_table, sine_table):
    half_dims = ROT // 2
    first_half = head_values[..., :half_dims]
    second = head_values[..., half_dims:ROT]
    return jnp.concatenate([first_half * cos_table - second * sine_table, second * cos_table + first_half * sine_table, head_values[..., ROT:]], axis=-1)

def allowed(segment_ids):
    column = jnp.arange(segment_ids.shape[0], dtype=jnp.int32)
    return (column[:, None] >= column[None, :]) & (segment_ids[:, None] == segment_ids[None, :])

def attend_seq(inputs):
    queries, key_rows, values, segment_ids = inputs
    score_scale = 1.0 / math.sqrt(HD)
    scores = low_back(jnp.einsum('qhd,khd->hqk', queries, key_rows, precision=PRECISE) * score_scale)
    scores = jnp.where(allowed(segment_ids), scores, NEG)
    maxima = lax.optimization_barrier(jnp.max(scores, axis=-1, keepdims=True))
    exponent = jnp.exp(scores - maxima)
    softmax_rows = low(exponent / lax.optimization_barrier(jnp.sum(exponent, axis=-1, keepdims=True)))
    return jnp.einsum('hqk,khd->qhd', softmax_rows, values, precision=PRECISE)

def forward(inputs, params, segment_ids):
    attn_gain, attn_shift, mlp_gain, mlp_shift, qkv_weight, qkv_bias, out_weight, out_bias, up_weight, up_bias, down_weight, down_bias = params
    row_count = inputs.shape[0]
    seq_count = segment_ids.shape[0]
    attn_normed = low(layer_norm(inputs, attn_gain, attn_shift))
    mlp_normed = low(layer_norm(inputs, mlp_gain, mlp_shift))
    mixed_rows = low_back(jnp.einsum('rd,dcw->rcw', attn_normed, qkv_weight, precision=PRECISE) + qkv_bias)
    head_values = mixed_rows.reshape(row_count, 3, H, HD)
    cos_table, sine_table = rotary_tables(segment_ids)
    queries = low(rotate(head_values[:, 0], cos_table, sine_table))
    key_rows = low(rotate(head_values[:, 1], cos_table, sine_table))
    values = low(head_values[:, 2])
    seq_shape = (seq_count, LEN, H, HD)
    attended = lax.map(jax.checkpoint(attend_seq), (queries.reshape(seq_shape), key_rows.reshape(seq_shape), values.reshape(seq_shape), segment_ids))
    attended = low(low_back(attended.reshape(row_count, H * HD)))
    branch_attn = jnp.dot(attended, out_weight, precision=PRECISE) + out_bias
    gate_rows = low_back(jnp.dot(mlp_normed, up_weight, precision=PRECISE) + up_bias)
    active = low(jax.nn.gelu(gate_rows, approximate=False))
    branch_mlp = jnp.dot(active, down_weight, precision=PRECISE) + down_bias
    return inputs + branch_attn + branch_mlp

def reference(tokens, segments, attn_gain, attn_shift, mlp_gain, mlp_shift, qkv_weight, qkv_bias, out_weight, out_bias, up_weight, up_bias, down_weight, down_bias, cotangent):
    params = tuple((member.astype(jnp.float32) for member in (attn_gain, attn_shift, mlp_gain, mlp_shift, qkv_weight, qkv_bias, out_weight, out_bias, up_weight, up_bias, down_weight, down_bias)))
    group_rows = N_TP * TOK_DEV
    group_seqs = group_rows // LEN
    inputs = tokens.astype(jnp.float32).reshape(N_FSDP, group_rows, D)
    grads_in = cotangent.astype(jnp.float32).reshape(N_FSDP, group_rows, D)
    seg_groups = segments.reshape(N_FSDP, group_seqs, LEN)

    def one_group(totals, block_items):
        block_in, block_grad, block_seg = block_items
        result, pull_back = jax.vjp(lambda values, weights: forward(values, weights, block_seg), block_in, params)
        grad_block, grad_params = pull_back(block_grad)
        return (jax.tree.map(jnp.add, totals, grad_params), (result, grad_block))
    zero_grads = tuple((jnp.zeros_like(member) for member in params))
    totals, (results, grad_blocks) = lax.scan(one_group, zero_grads, (inputs, grads_in, seg_groups))
    output = results.reshape(-1, D).astype(jnp.bfloat16)
    input_grad = grad_blocks.reshape(-1, D)
    return (output, input_grad, totals[0], totals[1], totals[2], totals[3], totals[4], totals[5], totals[6], totals[7], totals[8], totals[9], totals[10], totals[11])
```

```python
from functools import partial
import math

import jax
import jax.numpy as jnp
from jax import lax
from jax.experimental import pallas as pl
from jax.experimental.pallas import tpu as pltpu
from jax.sharding import PartitionSpec as P

HD = 64
ROT = 16
EPS = 1e-05
MASKED = 1e30
F32 = jnp.float32
BF16 = jnp.bfloat16
VMEM_BYTES = 56 * 1024 * 1024
NT = (((1,), (1,)), ((), ()))
TN = (((0,), (0,)), ((), ()))
NN = (((1,), (0,)), ((), ()))

dot32 = partial(lax.dot_general, preferred_element_type=F32)


def attention_kernel(
    mixed_ref, dout_ref, cos_ref, sa_ref, sb_ref, qf_ref, kf_ref, att_ref, dmix_ref, dk_scr, dv_scr, *, bq
):
    length = mixed_ref.shape[0]
    width = 2 * HD
    cos, sa, sb = cos_ref[...], sa_ref[...], sb_ref[...]
    scale = 1.0 / math.sqrt(HD)
    half = ROT // 2

    def turn(v, c, a, b, sign):
        side = pltpu.roll(v, width - half, 1) * a + pltpu.roll(v, half, 1) * b
        return v * c + side if sign > 0 else v * c - side

    q = turn(mixed_ref[:, 0:width], cos, sa, sb, 1).astype(BF16)
    k = turn(mixed_ref[:, width : 2 * width], cos, sa, sb, 1).astype(BF16)
    v = mixed_ref[:, 2 * width : 3 * width].astype(BF16)
    do = dout_ref[...]
    lane = lax.broadcasted_iota(jnp.int32, (length, width), 1)
    zero = jnp.zeros((), BF16)
    qs = (q.astype(F32) * scale).astype(BF16)
    qf = qf_ref[...]
    kaug = jnp.concatenate([k, kf_ref[...]], axis=1)
    heads = []
    for h in range(2):
        m = (lane // HD) == h
        qm = jnp.where(m, qs, zero)
        heads.append(
            (
                jnp.concatenate([qm, qf], axis=1),
                qm,
                jnp.where(m, k, zero),
                jnp.where(m, v, zero),
                jnp.where(m, do, zero),
            )
        )
    causal = lax.broadcasted_iota(jnp.int32, (bq, bq), 1) <= lax.broadcasted_iota(jnp.int32, (bq, bq), 0)
    blocks = length // bq
    for i in range(blocks):
        r0 = i * bq
        w = r0 + bq
        att = dq = dkp = dvp = None
        for qaug, qm, km, vm, dom in heads:
            s = dot32(qaug[r0:w], kaug[:w], NT)
            diagonal = jnp.where(causal, s[:, r0:], -MASKED)
            s = diagonal if i == 0 else jnp.concatenate([s[:, :r0], diagonal], axis=1)
            e = jnp.exp(s - jnp.max(s, axis=1, keepdims=True))
            p = e * (1.0 / jnp.sum(e, axis=1, keepdims=True))
            pb = p.astype(BF16)
            o = dot32(pb, vm[:w], NN)
            dp = dot32(dom[r0:w], v[:w], NT)
            delta = jnp.sum(p * dp, axis=1, keepdims=True)
            ds = (p * (dp - delta)).astype(BF16)
            x = dot32(ds, km[:w], NN)
            a = dot32(pb, dom[r0:w], TN)
            b = dot32(ds, qm[r0:w], TN)
            if att is None:
                att, dq, dvp, dkp = o, x, a, b
            else:
                att, dq, dvp, dkp = att + o, dq + x, dvp + a, dkp + b
        att_ref[r0:w, :] = att.astype(BF16)
        dmix_ref[r0:w, 0:width] = turn(dq * scale, cos[r0:w], sa[r0:w], sb[r0:w], -1).astype(BF16)
        if i > 0:
            dk_scr[:r0] += dkp[:r0]
            dv_scr[:r0] += dvp[:r0]
        dk_scr[r0:w] = dkp[r0:]
        dv_scr[r0:w] = dvp[r0:]
    dmix_ref[:, width : 2 * width] = turn(dk_scr[...], cos, sa, sb, -1).astype(BF16)
    dmix_ref[:, 2 * width : 3 * width] = dv_scr[...].astype(BF16)


def attention(mixed, dout, tables, length):
    rows = mixed.shape[0]
    width = 2 * HD
    pairs = dout.shape[1] // width
    seqs = rows // length
    bq = min(512, length)
    table = pl.BlockSpec((length, width), lambda s, j: (s, 0))
    units = seqs * pairs
    return pl.pallas_call(
        partial(attention_kernel, bq=bq),
        grid=(seqs, pairs),
        in_specs=[
            pl.BlockSpec((length, 3 * width), lambda s, j: (s, j)),
            pl.BlockSpec((length, width), lambda s, j: (s, j)),
        ]
        + [table] * 5,
        out_specs=[
            pl.BlockSpec((length, width), lambda s, j: (s, j)),
            pl.BlockSpec((length, 3 * width), lambda s, j: (s, j)),
        ],
        out_shape=[
            jax.ShapeDtypeStruct((rows, pairs * width), BF16),
            jax.ShapeDtypeStruct((rows, pairs * 3 * width), BF16),
        ],
        scratch_shapes=[pltpu.VMEM((length, width), F32), pltpu.VMEM((length, width), F32)],
        compiler_params=pltpu.CompilerParams(vmem_limit_bytes=VMEM_BYTES),
        cost_estimate=pl.CostEstimate(
            flops=units * 24 * length * length * width,
            bytes_accessed=units * length * width * 40,
            transcendentals=units * 2 * length * length,
        ),
        name="attention",
    )(mixed, dout, *tables)


def mlp_kernel(mn_ref, dy_ref, up_ref, bias_ref, down_ref, act_ref, dgate_ref, sum_ref):
    gate = dot32(mn_ref[...], up_ref[...], NN) + bias_ref[...]
    dact = dot32(dy_ref[...], down_ref[...], NT)
    cdf = 0.5 + 0.5 * lax.erf(gate * math.sqrt(0.5))
    pdf = jnp.exp(gate * gate * -0.5) * (1.0 / math.sqrt(2.0 * math.pi))
    act_ref[...] = (gate * cdf).astype(BF16)
    dgate = (dact * (cdf + gate * pdf)).astype(BF16)
    dgate_ref[...] = dgate
    part = jnp.sum(dgate.astype(F32), axis=0, keepdims=True)

    @pl.when(pl.program_id(1) == 0)
    def _():
        sum_ref[...] = part

    @pl.when(pl.program_id(1) > 0)
    def _():
        sum_ref[...] += part


def mlp_front(mn, dy, up, bias, down):
    rows, depth = mn.shape
    units = up.shape[1]
    br, bc = min(512, rows), min(512, units)
    row = pl.BlockSpec((br, depth), lambda c, r: (r, 0))
    tile = pl.BlockSpec((br, bc), lambda c, r: (r, c))
    return pl.pallas_call(
        mlp_kernel,
        grid=(units // bc, rows // br),
        in_specs=[
            row,
            row,
            pl.BlockSpec((depth, bc), lambda c, r: (0, c)),
            pl.BlockSpec((1, bc), lambda c, r: (0, c)),
            pl.BlockSpec((bc, depth), lambda c, r: (c, 0)),
        ],
        out_specs=[tile, tile, pl.BlockSpec((1, bc), lambda c, r: (0, c))],
        out_shape=[
            jax.ShapeDtypeStruct((rows, units), BF16),
            jax.ShapeDtypeStruct((rows, units), BF16),
            jax.ShapeDtypeStruct((1, units), F32),
        ],
        compiler_params=pltpu.CompilerParams(vmem_limit_bytes=VMEM_BYTES),
        cost_estimate=pl.CostEstimate(
            flops=4 * rows * depth * units,
            bytes_accessed=(units // bc) * rows * depth * 4 + units * depth * 4 + rows * units * 4,
            transcendentals=2 * rows * units,
        ),
        name="mlp_front",
    )(mn, dy, up, bias, down)


class Links:
    def __init__(self):
        self.fsdp = lax.axis_size("fsdp")
        self.tp = lax.axis_size("tp")
        index = lax.axis_index("fsdp")
        self.core = index % 2
        self.place = index // 2
        self.lane = lax.axis_index("tp")
        self.places = self.fsdp // 2
        self.cores = [list(range(c, self.fsdp, 2)) for c in range(2)]
        self.bits = [1 << b for b in range((self.places - 1).bit_length())]

    def swap(self, value):
        return lax.ppermute(value, "fsdp", [(i, i ^ 1) for i in range(self.fsdp)])

    def hop(self, value, bit):
        return lax.ppermute(value, "fsdp", [(i, i ^ (2 * bit)) for i in range(self.fsdp)])

    def ring(self, value):
        return lax.ppermute(value, "tp", [(i, (i + 1) % self.tp) for i in range(self.tp)])

    def gather_places(self, piece, axis):
        size = piece.shape[axis]
        found = {0: piece}
        if self.places == 4:
            found[1] = self.hop(piece, 1)
            found[2] = self.hop(piece, 2)
            cut = piece.shape[1 - axis] // 2
            first = lax.slice_in_dim(found[2], 0, cut, axis=1 - axis)
            second = lax.slice_in_dim(found[1], cut, 2 * cut, axis=1 - axis)
            found[3] = (self.hop(first, 1), self.hop(second, 2))
        else:
            return lax.all_gather(piece, "fsdp", axis=axis, tiled=True, axis_index_groups=self.cores)
        shape = list(piece.shape)
        shape[axis] = size * self.places
        whole = jnp.zeros(shape, piece.dtype)
        for key, block in found.items():
            start = (self.place ^ key) * size
            at = [0, 0]
            at[axis] = start
            if isinstance(block, tuple):
                whole = lax.dynamic_update_slice(whole, block[0], tuple(at))
                at[1 - axis] = block[0].shape[1 - axis]
                whole = lax.dynamic_update_slice(whole, block[1], tuple(at))
            else:
                whole = lax.dynamic_update_slice(whole, block, tuple(at))
        return whole

    def scatter_places(self, whole, axis):
        size = whole.shape[axis] // self.places

        def block(key):
            return lax.dynamic_slice_in_dim(whole, (self.place ^ key) * size, size, axis)

        if self.places == 4:
            cut = whole.shape[1 - axis] // 2
            far = block(3)
            first = self.hop(lax.slice_in_dim(far, 0, cut, axis=1 - axis), 2)
            second = self.hop(lax.slice_in_dim(far, cut, 2 * cut, axis=1 - axis), 1)
            near = block(1)
            left = lax.slice_in_dim(near, 0, cut, axis=1 - axis).astype(F32) + first.astype(F32)
            one = jnp.concatenate(
                [left.astype(BF16), lax.slice_in_dim(near, cut, 2 * cut, axis=1 - axis)], axis=1 - axis
            )
            near = block(2)
            right = lax.slice_in_dim(near, cut, 2 * cut, axis=1 - axis).astype(F32) + second.astype(F32)
            two = jnp.concatenate(
                [lax.slice_in_dim(near, 0, cut, axis=1 - axis), right.astype(BF16)], axis=1 - axis
            )
            return block(0).astype(F32) + self.hop(one, 1).astype(F32) + self.hop(two, 2).astype(F32)
        return lax.psum_scatter(
            whole, "fsdp", scatter_dimension=axis, tiled=True, axis_index_groups=self.cores
        ).astype(F32)

    def scatter_lanes(self, slots):
        total = None
        for step in range(1, self.tp):
            total = slots[step] if total is None else total + slots[step]
            total = self.ring(total.astype(BF16)).astype(F32)
        return slots[0] if total is None else total + slots[0]

    def total(self, value):
        for bit in [1] + [2 * b for b in self.bits]:
            value = value + lax.ppermute(value, "fsdp", [(i, i ^ bit) for i in range(self.fsdp)])
        bit = 1
        while bit < self.tp:
            value = value + lax.ppermute(value, "tp", [(i, i ^ bit) for i in range(self.tp)])
            bit *= 2
        return value


def pick(value, index, axis):
    return lax.dynamic_index_in_dim(value, index, axis, keepdims=False)


def pair_blocks(links, shard, split_axis, join_axis):
    half = shard.shape[split_axis] // 2
    mine = lax.dynamic_slice_in_dim(shard, links.core * half, half, split_axis)
    other = links.swap(lax.dynamic_slice_in_dim(shard, (1 - links.core) * half, half, split_axis))
    first = jnp.where(links.core == 0, mine, other)
    second = jnp.where(links.core == 0, other, mine)
    return jnp.concatenate([first, second], axis=join_axis)


def unpair_blocks(links, block, split_axis, join_axis):
    half = block.shape[join_axis] // 2
    mine = lax.dynamic_slice_in_dim(block, links.core * half, half, join_axis)
    other = links.swap(lax.dynamic_slice_in_dim(block, (1 - links.core) * half, half, join_axis))
    first = jnp.where(links.core == 0, mine, other)
    second = jnp.where(links.core == 0, other, mine)
    return jnp.concatenate([first, second], axis=split_axis)


def tables_of(segment_rows):
    seqs, length = segment_rows.shape
    width = 2 * HD
    starts = jnp.sum((segment_rows[:, None, :] < segment_rows[:, :, None]).astype(jnp.int32), axis=-1)
    places = (jnp.arange(length, dtype=jnp.int32)[None] - starts).reshape(-1).astype(F32)
    inverse_freq = jnp.power(10000.0, -jnp.arange(0, ROT, 2, dtype=F32) / ROT)
    angles = places[:, None] * jnp.tile(inverse_freq, width // (ROT // 2))[None, :]
    lane = jnp.arange(width, dtype=jnp.int32)[None, :]
    turn = lane % HD
    cos = jnp.where(turn < ROT, jnp.cos(angles), 1.0)
    sine = jnp.sin(angles)
    sa = jnp.where(turn < ROT // 2, -sine, 0.0)
    sb = jnp.where((turn >= ROT // 2) & (turn < ROT), sine, 0.0)
    same = segment_rows.reshape(-1, 1) == lane
    key_mark = jnp.where(same, 1.0, 0.0).astype(BF16)
    query_mark = jnp.where(same | (lane >= 8), 0.0, -MASKED).astype(BF16)
    return cos, sa, sb, query_mark, key_mark


def body(
    tokens,
    segments,
    attn_gain,
    attn_shift,
    mlp_gain,
    mlp_shift,
    qkv_weight,
    qkv_bias,
    out_weight,
    out_bias,
    up_weight,
    up_bias,
    down_weight,
    down_bias,
    cotangent,
):
    links = Links()
    tp = links.tp
    rows, depth = tokens.shape
    length = segments.shape[1]
    head_cols = qkv_weight.shape[2] // 2
    unit_cols = up_weight.shape[1] // 2

    x2 = jnp.concatenate([tokens, links.swap(tokens)], axis=0)
    dy2 = jnp.concatenate([cotangent, links.swap(cotangent)], axis=0)
    own_segments = lax.dynamic_slice_in_dim(segments, links.lane * rows // length, rows // length, 0)
    tables = tables_of(jnp.concatenate([own_segments, links.swap(own_segments)], axis=0))

    qkv_piece = pair_blocks(links, qkv_weight, 2, 0)
    qkv_piece = qkv_piece.reshape(qkv_piece.shape[0], 3 * head_cols)
    out_piece = pair_blocks(links, out_weight, 0, 1)
    up_piece = pair_blocks(links, up_weight, 1, 0)
    down_piece = pair_blocks(links, down_weight, 0, 1)
    qkv_slots = [links.gather_places(qkv_piece, 0)]
    out_slots = [links.gather_places(out_piece, 1)]
    up_slots, down_slots = [up_piece], [down_piece]
    for _ in range(tp - 1):
        qkv_slots.append(links.ring(qkv_slots[-1]))
        out_slots.append(links.ring(out_slots[-1]))
        up_slots.append(links.ring(up_slots[-1]))
        down_slots.append(links.ring(down_slots[-1]))
    half = tp // 2
    per = max(1, 2 * HD // head_cols)

    def join_heads(slots):
        if per == 1:
            return jnp.concatenate(slots, axis=1)
        lead = slots[0].shape[0]
        blocks = [
            jnp.concatenate([v.reshape(lead, 3, head_cols) for v in slots[i : i + per]], axis=2).reshape(lead, -1)
            for i in range(0, len(slots), per)
        ]
        return jnp.concatenate(blocks, axis=1)

    def split_heads(joined):
        lead = joined.shape[0]
        blocks = joined.reshape(lead, -1, 3, per, head_cols)
        return [blocks[:, i, :, j] for i in range(blocks.shape[1]) for j in range(per)]

    groups = [list(range(0, half)), list(range(half, tp))]
    qkv_groups = [join_heads([qkv_slots[s] for s in g]) for g in groups]
    out_groups = [jnp.concatenate([out_slots[s] for s in g], axis=0) for g in groups]
    up_groups = [links.gather_places(jnp.concatenate([up_slots[s] for s in g], axis=1), 0) for g in groups]
    down_groups = [links.gather_places(jnp.concatenate([down_slots[s] for s in g], axis=0), 1) for g in groups]

    lane_of = [(links.lane - s) % tp for s in range(tp)]
    qkv_bias_lanes = pick(qkv_bias.reshape(3, tp, 2, head_cols), links.core, 2)
    up_bias_lanes = pick(up_bias.reshape(tp, 2, unit_cols), links.core, 1)
    qkv_bias_groups = [
        join_heads([pick(qkv_bias_lanes, lane_of[s], 1).reshape(1, -1) for s in g]).astype(F32) for g in groups
    ]
    up_bias_groups = [
        jnp.concatenate([pick(up_bias_lanes, lane_of[s], 0) for s in g]).astype(F32)[None] for g in groups
    ]

    x = x2.astype(F32)
    centre = x - jnp.mean(x, axis=-1, keepdims=True)
    rstd = lax.rsqrt(jnp.mean(centre * centre, axis=-1, keepdims=True) + EPS)
    xhat = centre * rstd
    gains = [v.astype(F32) for v in (attn_gain, attn_shift, mlp_gain, mlp_shift)]
    attn_normed = (xhat * gains[0] + gains[1]).astype(BF16)
    mlp_normed = (xhat * gains[2] + gains[3]).astype(BF16)

    def attention_part(g, normed, dy):
        mixed = dot32(normed, qkv_groups[g], NN) + qkv_bias_groups[g]
        dout = dot32(dy, out_groups[g], NT).astype(BF16)
        attended, dmixed = attention(mixed, dout, tables, length)
        return attended, dmixed

    def mlp_part(g, normed, dy):
        active, dgate, gate_sum = mlp_front(normed, dy, up_groups[g], up_bias_groups[g], down_groups[g])
        grad_up = dot32(normed, dgate, TN).astype(BF16)
        grad_down = dot32(active, dy, TN).astype(BF16)
        return active, dgate, gate_sum, grad_up, grad_down

    att0, dmix0 = attention_part(0, attn_normed, dy2)
    mlp_in, dy_mlp, att0, dmix0 = lax.optimization_barrier((mlp_normed, dy2, att0, dmix0))
    mlp = [mlp_part(g, mlp_in, dy_mlp) for g in range(2)]
    grad_qkv0 = dot32(attn_normed, dmix0, TN).astype(BF16)
    grad_out0 = dot32(att0, dy2, TN).astype(BF16)
    normed1, dy1, mlp = lax.optimization_barrier((attn_normed, dy2, mlp))
    att1, dmix1 = attention_part(1, normed1, dy1)
    grad_qkv1 = dot32(attn_normed, dmix1, TN).astype(BF16)
    grad_out1 = dot32(att1, dy2, TN).astype(BF16)

    def finish(parts, axis, split):
        slots = []
        for part in parts:
            slots += split(links.scatter_places(part, axis))
        return links.scatter_lanes(slots)

    def split_cols(piece):
        return jnp.split(piece, half, axis=1)

    def split_rows(piece):
        return jnp.split(piece, half, axis=0)

    up_grad = unpair_blocks(links, finish([mlp[0][3], mlp[1][3]], 0, split_cols), 1, 0)
    down_grad = unpair_blocks(links, finish([mlp[0][4], mlp[1][4]], 1, split_rows), 0, 1)
    qkv_grad = unpair_blocks(links, finish([grad_qkv0, grad_qkv1], 0, split_heads), 2, 0)
    out_grad = unpair_blocks(links, finish([grad_out0, grad_out1], 1, split_rows), 0, 1)

    partial_out = (
        dot32(mlp[0][0], down_groups[0], NN)
        + dot32(mlp[1][0], down_groups[1], NN)
        + dot32(jnp.concatenate([att0, att1], axis=1), jnp.concatenate(out_groups, axis=0), NN)
    )
    other_out = links.swap(partial_out[rows:].astype(BF16))
    output = (
        tokens.astype(F32)
        + partial_out[:rows]
        + other_out.astype(F32)
        + out_bias.astype(F32)
        + down_bias.astype(F32)
    ).astype(BF16)

    n_mlp = dot32(mlp[0][1], up_groups[0], NT) + dot32(mlp[1][1], up_groups[1], NT)
    n_attn = dot32(dmix0, qkv_groups[0], NT) + dot32(dmix1, qkv_groups[1], NT)
    pulled = n_attn * gains[0] + n_mlp * gains[2]
    other_pull = links.swap(pulled[rows:].astype(BF16))
    whole = pulled[:rows] + other_pull.astype(F32)
    own_hat = xhat[:rows]
    input_grad = cotangent.astype(F32) + rstd[:rows] * (
        whole
        - jnp.mean(whole, axis=-1, keepdims=True)
        - own_hat * jnp.mean(whole * own_hat, axis=-1, keepdims=True)
    )

    def spread(values):
        lead, cols = values[0].shape
        full = jnp.zeros((lead, tp, 2, cols), F32)
        for s, value in enumerate(values):
            full = lax.dynamic_update_slice(full, value.reshape(lead, 1, 1, cols), (0, lane_of[s], links.core, 0))
        return full.reshape(-1)

    qkv_sums = [jnp.sum(d.astype(F32), axis=0, keepdims=True) for d in (dmix0, dmix1)]
    qkv_bias_part = spread([v[0] for d in qkv_sums for v in split_heads(d)])
    up_bias_part = spread([v for part in mlp for v in jnp.split(part[2], half, axis=1)])
    bias_part = jnp.sum(cotangent.astype(F32), axis=0)
    pieces = [
        jnp.sum(n_attn * xhat, axis=0),
        jnp.sum(n_attn, axis=0),
        jnp.sum(n_mlp * xhat, axis=0),
        jnp.sum(n_mlp, axis=0),
        qkv_bias_part,
        bias_part,
        up_bias_part,
    ]
    sizes = [v.shape[0] for v in pieces]
    summed = links.total(jnp.concatenate(pieces).reshape(-1, 128)).reshape(-1)
    sums = []
    at = 0
    for size in sizes:
        sums.append(summed[at : at + size])
        at += size
    return (
        output,
        input_grad,
        sums[0],
        sums[1],
        sums[2],
        sums[3],
        qkv_grad,
        sums[4].reshape(qkv_bias.shape),
        out_grad,
        sums[5],
        up_grad,
        sums[6],
        down_grad,
        sums[5],
    )


def solution(mesh):
    placed = (
        P(("fsdp", "tp"), None),
        P("fsdp", None),
        P(),
        P(),
        P(),
        P(),
        P("fsdp", None, "tp"),
        P(),
        P("tp", "fsdp"),
        P(),
        P("fsdp", "tp"),
        P(),
        P("tp", "fsdp"),
        P(),
        P(("fsdp", "tp"), None),
    )
    return jax.shard_map(
        body,
        mesh=mesh,
        in_specs=placed,
        out_specs=(
            P(("fsdp", "tp"), None),
            P(("fsdp", "tp"), None),
            P(),
            P(),
            P(),
            P(),
            P("fsdp", None, "tp"),
            P(),
            P("tp", "fsdp"),
            P(),
            P("fsdp", "tp"),
            P(),
            P("tp", "fsdp"),
            P(),
        ),
        check_vma=False,
    )
```

```python
from functools import partial
import math

import jax
import jax.numpy as jnp
from jax import lax
from jax.experimental import pallas as pl
from jax.experimental.pallas import tpu as pltpu
from jax.sharding import PartitionSpec as P

HD = 64
ROT = 16
EPS = 1e-05
MASKED = 1e30
F32 = jnp.float32
BF16 = jnp.bfloat16
VMEM_BYTES = 56 * 1024 * 1024
NT = (((1,), (1,)), ((), ()))
TN = (((0,), (0,)), ((), ()))
NN = (((1,), (0,)), ((), ()))

dot32 = partial(lax.dot_general, preferred_element_type=F32)


def whole_spec(value):
    return pl.BlockSpec(value.shape, lambda *_: (0,) * value.ndim)


def put_rows(into, pieces, place):
    for ref, key in pieces:
        rows = ref.shape[0]
        if rows == into.shape[0]:
            into[...] = ref[...]
        else:
            into[pl.ds(pl.multiple_of((place ^ key) * rows, rows), rows), :] = ref[...]


def prepare_kernel(x_own, x_other, dy_own, dy_other, gain_ref, an_ref, mn_ref, dy_ref, ant_ref, mnt_ref, dyt_ref):
    step = pl.program_id(0)
    half = pl.num_programs(0) // 2

    def work(x_ref, grad_ref):
        xhat, _ = row_norm(x_ref[...].astype(F32))
        an = (xhat * gain_ref[0:1, :] + gain_ref[1:2, :]).astype(BF16)
        mn = (xhat * gain_ref[2:3, :] + gain_ref[3:4, :]).astype(BF16)
        dy = grad_ref[...]
        an_ref[...], mn_ref[...], dy_ref[...] = an, mn, dy
        ant_ref[...], mnt_ref[...], dyt_ref[...] = an.T, mn.T, dy.T

    @pl.when(step < half)
    def _():
        work(x_own, dy_own)

    @pl.when(step >= half)
    def _():
        work(x_other, dy_other)


def prepare(x_own, x_other, dy_own, dy_other, gains):
    rows, depth = x_own.shape
    br = min(256, rows)
    half = rows // br
    own = pl.BlockSpec((br, depth), lambda i: (jnp.minimum(i, half - 1), 0))
    other = pl.BlockSpec((br, depth), lambda i: (jnp.maximum(i - half, 0), 0))
    tall = pl.BlockSpec((br, depth), lambda i: (i, 0))
    wide = pl.BlockSpec((depth, br), lambda i: (0, i))
    return pl.pallas_call(
        prepare_kernel,
        grid=(2 * half,),
        in_specs=[own, other, own, other, whole_spec(gains)],
        out_specs=[tall] * 3 + [wide] * 3,
        out_shape=[jax.ShapeDtypeStruct((2 * rows, depth), BF16)] * 3
        + [jax.ShapeDtypeStruct((depth, 2 * rows), BF16)] * 3,
        compiler_params=pltpu.CompilerParams(vmem_limit_bytes=VMEM_BYTES),
        cost_estimate=pl.CostEstimate(
            flops=40 * rows * depth, bytes_accessed=32 * rows * depth, transcendentals=2 * rows
        ),
        name="prepare",
    )(x_own, x_other, dy_own, dy_other, gains)


def attention_kernel(place_ref, an_ref, dy_ref, bias_ref, cos_ref, sa_ref, sb_ref, qf_ref, kf_ref, *refs, keys, bq):
    length = an_ref.shape[0]
    width = 2 * HD
    piece_refs, refs = refs[: sum(map(len, keys))], refs[sum(map(len, keys)) :]
    att_ref, dmix_ref, qkv_ref, out_ref, packed, dk_scr, dv_scr = refs
    at = 0
    for j, pair_keys in enumerate(keys):
        pieces = list(zip(piece_refs[at : at + len(pair_keys)], pair_keys))
        at += len(pair_keys)

        @pl.when((pl.program_id(0) == j) & (pl.program_id(1) == 0))
        def _():
            put_rows(packed, pieces, place_ref[0])
            qkv_ref[...] = packed[:, : 3 * width]
            out_ref[...] = packed[:, 3 * width :]

    mixed = dot32(an_ref[...], packed[:, : 3 * width], NN) + bias_ref[...]
    cos, sa, sb = cos_ref[...], sa_ref[...], sb_ref[...]
    scale = 1.0 / math.sqrt(HD)
    half = ROT // 2

    def turn(v, c, a, b, sign):
        side = pltpu.roll(v, width - half, 1) * a + pltpu.roll(v, half, 1) * b
        return v * c + side if sign > 0 else v * c - side

    q = turn(mixed[:, 0:width], cos, sa, sb, 1).astype(BF16)
    k = turn(mixed[:, width : 2 * width], cos, sa, sb, 1).astype(BF16)
    v = mixed[:, 2 * width : 3 * width].astype(BF16)
    do = dot32(dy_ref[...], packed[:, 3 * width :], NN).astype(BF16)
    lane = lax.broadcasted_iota(jnp.int32, (length, width), 1)
    zero = jnp.zeros((), BF16)
    qs = (q.astype(F32) * scale).astype(BF16)
    qf = qf_ref[...]
    kaug = jnp.concatenate([k, kf_ref[...]], axis=1)
    heads = []
    for h in range(2):
        m = (lane // HD) == h
        qm = jnp.where(m, qs, zero)
        heads.append(
            (
                jnp.concatenate([qm, qf], axis=1),
                qm,
                jnp.where(m, k, zero),
                jnp.where(m, v, zero),
                jnp.where(m, do, zero),
            )
        )
    causal = lax.broadcasted_iota(jnp.int32, (bq, bq), 1) <= lax.broadcasted_iota(jnp.int32, (bq, bq), 0)
    blocks = length // bq
    for i in range(blocks):
        r0 = i * bq
        w = r0 + bq
        att = dq = dkp = dvp = None
        for qaug, qm, km, vm, dom in heads:
            s = dot32(qaug[r0:w], kaug[:w], NT)
            diagonal = jnp.where(causal, s[:, r0:], -MASKED)
            s = diagonal if i == 0 else jnp.concatenate([s[:, :r0], diagonal], axis=1)
            e = jnp.exp(s - jnp.max(s, axis=1, keepdims=True))
            p = e * (1.0 / jnp.sum(e, axis=1, keepdims=True))
            pb = p.astype(BF16)
            o = dot32(pb, vm[:w], NN)
            dp = dot32(dom[r0:w], v[:w], NT)
            delta = jnp.sum(p * dp, axis=1, keepdims=True)
            ds = (p * (dp - delta)).astype(BF16)
            x = dot32(ds, km[:w], NN)
            a = dot32(pb, dom[r0:w], TN)
            b = dot32(ds, qm[r0:w], TN)
            if att is None:
                att, dq, dvp, dkp = o, x, a, b
            else:
                att, dq, dvp, dkp = att + o, dq + x, dvp + a, dkp + b
        att_ref[r0:w, :] = att.astype(BF16)
        dmix_ref[r0:w, 0:width] = turn(dq * scale, cos[r0:w], sa[r0:w], sb[r0:w], -1).astype(BF16)
        if i > 0:
            dk_scr[:r0] += dkp[:r0]
            dv_scr[:r0] += dvp[:r0]
        dk_scr[r0:w] = dkp[r0:]
        dv_scr[r0:w] = dvp[r0:]
    dmix_ref[:, width : 2 * width] = turn(dk_scr[...], cos, sa, sb, -1).astype(BF16)
    dmix_ref[:, 2 * width : 3 * width] = dv_scr[...].astype(BF16)


def attention(pairs, place, an, dy, bias, tables, length):
    rows, depth = an.shape
    width = 2 * HD
    seqs = rows // length
    count = len(pairs)
    row = pl.BlockSpec((length, depth), lambda j, s, p: (s, 0))
    table = pl.BlockSpec((length, width), lambda j, s, p: (s, 0))
    pieces = [piece for pair in pairs for piece in pair.values()]
    units = seqs * count
    return pl.pallas_call(
        partial(attention_kernel, keys=[list(pair) for pair in pairs], bq=min(512, length)),
        grid_spec=pltpu.PrefetchScalarGridSpec(
            num_scalar_prefetch=1,
            grid=(count, seqs),
            in_specs=[row, row, pl.BlockSpec((1, 3 * width), lambda j, s, p: (0, j))]
            + [table] * 5
            + [whole_spec(v) for v in pieces],
            out_specs=[
                pl.BlockSpec((length, width), lambda j, s, p: (s, j)),
                pl.BlockSpec((length, 3 * width), lambda j, s, p: (s, j)),
                pl.BlockSpec((depth, 3 * width), lambda j, s, p: (0, j)),
                pl.BlockSpec((depth, width), lambda j, s, p: (0, j)),
            ],
            scratch_shapes=[
                pltpu.VMEM((depth, 4 * width), BF16),
                pltpu.VMEM((length, width), F32),
                pltpu.VMEM((length, width), F32),
            ],
        ),
        out_shape=[
            jax.ShapeDtypeStruct((rows, count * width), BF16),
            jax.ShapeDtypeStruct((rows, count * 3 * width), BF16),
            jax.ShapeDtypeStruct((depth, count * 3 * width), BF16),
            jax.ShapeDtypeStruct((depth, count * width), BF16),
        ],
        compiler_params=pltpu.CompilerParams(vmem_limit_bytes=VMEM_BYTES),
        cost_estimate=pl.CostEstimate(
            flops=units * (32 * length * length * width + 8 * length * depth * width),
            bytes_accessed=units * length * (depth * 4 + width * 40),
            transcendentals=units * 2 * length * length,
        ),
        name="attention",
    )(place, an, dy, bias, *tables, *pieces)


def mlp_kernel(place_ref, mn_ref, dy_ref, bias_ref, *refs, keys):
    piece_refs, refs = refs[: sum(map(len, keys))], refs[sum(map(len, keys)) :]
    act_ref, dgate_ref, sum_ref, up_ref, down_ref, packed = refs
    units = up_ref.shape[1]
    at = 0
    for j, slot_keys in enumerate(keys):
        pieces = list(zip(piece_refs[at : at + len(slot_keys)], slot_keys))
        at += len(slot_keys)

        @pl.when((pl.program_id(0) == j) & (pl.program_id(1) == 0))
        def _():
            put_rows(packed, pieces, place_ref[0])
            up_ref[...] = packed[:, :units]
            down_ref[...] = packed[:, units:]

    gate = dot32(mn_ref[...], packed[:, :units], NN) + bias_ref[...]
    dact = dot32(dy_ref[...], packed[:, units:], NN)
    cdf = 0.5 + 0.5 * lax.erf(gate * math.sqrt(0.5))
    pdf = jnp.exp(gate * gate * -0.5) * (1.0 / math.sqrt(2.0 * math.pi))
    act_ref[...] = (gate * cdf).astype(BF16)
    dgate = (dact * (cdf + gate * pdf)).astype(BF16)
    dgate_ref[...] = dgate
    part = jnp.sum(dgate.astype(F32), axis=0, keepdims=True)

    @pl.when(pl.program_id(1) == 0)
    def _():
        sum_ref[...] = part

    @pl.when(pl.program_id(1) > 0)
    def _():
        sum_ref[...] += part


def mlp_front(slots, place, mn, dy, bias):
    rows, depth = mn.shape
    units = slots[0][0].shape[1] // 2
    count = len(slots)
    br = min(512, rows)
    row = pl.BlockSpec((br, depth), lambda c, r, p: (r, 0))
    tile = pl.BlockSpec((br, units), lambda c, r, p: (r, c))
    top = pl.BlockSpec((1, units), lambda c, r, p: (0, c))
    tall = pl.BlockSpec((depth, units), lambda c, r, p: (0, c))
    pieces = [piece for slot in slots for piece in slot.values()]
    return pl.pallas_call(
        partial(mlp_kernel, keys=[list(slot) for slot in slots]),
        grid_spec=pltpu.PrefetchScalarGridSpec(
            num_scalar_prefetch=1,
            grid=(count, rows // br),
            in_specs=[row, row, top] + [whole_spec(v) for v in pieces],
            out_specs=[tile, tile, top, tall, tall],
            scratch_shapes=[pltpu.VMEM((depth, 2 * units), BF16)],
        ),
        out_shape=[
            jax.ShapeDtypeStruct((rows, count * units), BF16),
            jax.ShapeDtypeStruct((rows, count * units), BF16),
            jax.ShapeDtypeStruct((1, count * units), F32),
            jax.ShapeDtypeStruct((depth, count * units), BF16),
            jax.ShapeDtypeStruct((depth, count * units), BF16),
        ],
        compiler_params=pltpu.CompilerParams(vmem_limit_bytes=VMEM_BYTES),
        cost_estimate=pl.CostEstimate(
            flops=4 * rows * depth * count * units,
            bytes_accessed=count * (rows * depth * 4 + units * depth * 8 + rows * units * 4),
            transcendentals=2 * rows * count * units,
        ),
        name="mlp_front",
    )(place, mn, dy, bias, *pieces)


def grads_kernel(place_ref, left_a, left_b, right_a, right_b, *outs, count, keys):
    a = dot32(left_a[...], right_a[...], NN)
    b = dot32(left_b[...], right_b[...], NN)
    wa, wb = a.shape[1] // count, b.shape[1] // count
    for n, _ in enumerate(keys):

        @pl.when(pl.program_id(0) == n)
        def _():
            for j in range(count):
                out = outs[j * len(keys) + n]
                out[:, :wa] = a[:, j * wa : (j + 1) * wa].astype(out.dtype)
                out[:, wa:] = b[:, j * wb : (j + 1) * wb].astype(out.dtype)


def weight_grads(place, places, left_a, right_a, left_b, right_b, count):
    depth, rows = left_a.shape
    keys = (3, 1, 2, 0) if places == 4 else (0,)
    size = depth // len(keys)

    def left_at(i, p):
        key = keys[0]
        for n in range(1, len(keys)):
            key = jnp.where(i == n, keys[n], key)
        return (p[0] ^ key, 0)

    left = pl.BlockSpec((size, rows), left_at)
    width = (right_a.shape[1] + right_b.shape[1]) // count
    out = pl.BlockSpec((size, width), lambda i, p: (0, 0))
    found = pl.pallas_call(
        partial(grads_kernel, count=count, keys=keys),
        grid_spec=pltpu.PrefetchScalarGridSpec(
            num_scalar_prefetch=1,
            grid=(len(keys),),
            in_specs=[left, left, whole_spec(right_a), whole_spec(right_b)],
            out_specs=[out] * (count * len(keys)),
        ),
        out_shape=[jax.ShapeDtypeStruct((size, width), BF16)] * (count * len(keys)),
        compiler_params=pltpu.CompilerParams(vmem_limit_bytes=VMEM_BYTES),
        cost_estimate=pl.CostEstimate(
            flops=2 * rows * depth * count * width,
            bytes_accessed=4 * rows * depth + 2 * count * width * (rows + depth),
            transcendentals=0,
        ),
        name="weight_grads",
    )(place, left_a, left_b, right_a, right_b)
    return [dict(zip(keys, found[j * len(keys) : (j + 1) * len(keys)])) for j in range(count)]


def row_norm(x):
    centre = x - jnp.mean(x, axis=-1, keepdims=True)
    rstd = lax.rsqrt(jnp.mean(centre * centre, axis=-1, keepdims=True) + EPS)
    return centre * rstd, rstd


def pull_kernel(*refs):
    dg0, up0, dg1, up1, dm0, qkv0, dm1, qkv1, x_ref, gain_ref = refs[:10]
    out_ref, sum_ref = refs[-2:]
    n_mlp = dot32(dg0[...], up0[...], NT) + dot32(dg1[...], up1[...], NT)
    n_attn = dot32(dm0[...], qkv0[...], NT) + dot32(dm1[...], qkv1[...], NT)
    xhat, rstd = row_norm(x_ref[...].astype(F32))
    u = n_attn * gain_ref[0:1, :] + n_mlp * gain_ref[2:3, :]
    parts = [jnp.sum(v, axis=0, keepdims=True) for v in (n_attn * xhat, n_attn, n_mlp * xhat, n_mlp)]
    part = jnp.concatenate(parts + [jnp.zeros((4, u.shape[1]), F32)], axis=0)

    @pl.when(pl.program_id(0) == 0)
    def _():
        sum_ref[...] = part

    @pl.when(pl.program_id(0) > 0)
    def _():
        sum_ref[...] += part

    out_ref[...] = u.astype(out_ref.dtype)


def pull_back(terms, x, gains, first_row, dtype):
    rows, depth = x.shape
    br = min(256, rows)
    first = first_row // br
    block = lambda v: pl.BlockSpec((br, v.shape[1]), lambda i: (i + first, 0))
    specs, args = [], []
    for grad, weight in terms:
        specs += [block(grad), whole_spec(weight)]
        args += [grad, weight]
    tile = pl.BlockSpec((br, depth), lambda i: (i, 0))
    width = sum(grad.shape[1] for grad, _ in terms)
    return pl.pallas_call(
        pull_kernel,
        grid=(rows // br,),
        in_specs=specs + [tile, whole_spec(gains)],
        out_specs=[tile, pl.BlockSpec((8, depth), lambda i: (0, 0))],
        out_shape=[jax.ShapeDtypeStruct((rows, depth), dtype), jax.ShapeDtypeStruct((8, depth), F32)],
        compiler_params=pltpu.CompilerParams(vmem_limit_bytes=VMEM_BYTES),
        cost_estimate=pl.CostEstimate(
            flops=2 * rows * width * depth,
            bytes_accessed=2 * width * (rows + depth) + rows * depth * 8,
            transcendentals=rows,
        ),
        name="pull_back",
    )(*args, x, gains)


def out_kernel(*refs, own):
    att0, out0, att1, out1, act0, down0, act1, down1 = refs[:8]
    y = dot32(act0[...], down0[...], NT) + dot32(act1[...], down1[...], NT)
    y = y + dot32(att0[...], out0[...], NT) + dot32(att1[...], out1[...], NT)
    if not own:
        refs[-1][...] = y.astype(BF16)
        return
    x_ref, other_ref, bias_ref, dy_ref, pull_ref, other_pull_ref, y_ref, grad_ref = refs[8:]
    x = x_ref[...].astype(F32)
    y_ref[...] = (y + x + other_ref[...].astype(F32) + bias_ref[...]).astype(BF16)
    xhat, rstd = row_norm(x)
    u = pull_ref[...] + other_pull_ref[...].astype(F32)
    u = u - jnp.mean(u, axis=-1, keepdims=True) - xhat * jnp.mean(u * xhat, axis=-1, keepdims=True)
    grad_ref[...] = dy_ref[...].astype(F32) + rstd * u


def branch_out(terms, rows, last=None):
    own = last is not None
    depth = terms[0][1].shape[0]
    br = min(256, rows)
    first = 0 if own else rows // br
    tile = pl.BlockSpec((br, depth), lambda i: (i, 0))
    specs, args = [], []
    for value, weight in terms:
        specs += [pl.BlockSpec((br, value.shape[1]), lambda i: (i + first, 0)), whole_spec(weight)]
        args += [value, weight]
    if own:
        specs += [whole_spec(v) if v.shape[0] == 1 else tile for v in last]
        args += last
    width = sum(value.shape[1] for value, _ in terms)
    shapes = [jax.ShapeDtypeStruct((rows, depth), BF16)] + [jax.ShapeDtypeStruct((rows, depth), F32)] * own
    return pl.pallas_call(
        partial(out_kernel, own=own),
        grid=(rows // br,),
        in_specs=specs,
        out_specs=[tile] * len(shapes),
        out_shape=shapes,
        compiler_params=pltpu.CompilerParams(vmem_limit_bytes=VMEM_BYTES),
        cost_estimate=pl.CostEstimate(
            flops=2 * rows * width * depth,
            bytes_accessed=2 * width * (rows + depth) + rows * depth * (18 if own else 2),
            transcendentals=0,
        ),
        name="branch_out",
    )(*args)


class Links:
    def __init__(self):
        self.fsdp = lax.axis_size("fsdp")
        self.tp = lax.axis_size("tp")
        index = lax.axis_index("fsdp")
        self.core = index % 2
        self.place = index // 2
        self.lane = lax.axis_index("tp")
        self.places = self.fsdp // 2
        self.cores = [list(range(c, self.fsdp, 2)) for c in range(2)]
        self.bits = [1 << b for b in range((self.places - 1).bit_length())]

    def swap(self, value):
        return lax.ppermute(value, "fsdp", [(i, i ^ 1) for i in range(self.fsdp)])

    def hop(self, value, bit):
        return lax.ppermute(value, "fsdp", [(i, i ^ (2 * bit)) for i in range(self.fsdp)])

    def ring(self, value):
        return lax.ppermute(value, "tp", [(i, (i + 1) % self.tp) for i in range(self.tp)])

    def far_bit(self, slot):
        return 1 if slot % 2 == 0 else 2

    def near_places(self, piece):
        return {0: piece, 1: self.hop(piece, 1), 2: self.hop(piece, 2)}

    def far_place(self, pieces, slot):
        bit = self.far_bit(slot)
        return {**pieces, 3: self.hop(pieces[3 - bit], bit)}

    def scatter_far(self, blocks, slot):
        return self.hop(blocks[3], 3 - self.far_bit(slot))

    def scatter_near(self, blocks, far, slot):
        bit = self.far_bit(slot)
        near = {1: blocks[1], 2: blocks[2]}
        near[bit] = (near[bit].astype(F32) + far.astype(F32)).astype(BF16)
        return self.hop(near[1], 1), self.hop(near[2], 2)

    def gather_other(self, piece):
        return {0: lax.all_gather(piece, "fsdp", axis=0, tiled=True, axis_index_groups=self.cores)}

    def scatter_other(self, value):
        return lax.psum_scatter(
            value, "fsdp", scatter_dimension=0, tiled=True, axis_index_groups=self.cores
        )

    def scatter_lanes(self, slots):
        total = None
        for step in range(1, self.tp):
            total = slots[step]() if total is None else total + slots[step]()
            total = self.ring(total.astype(BF16)).astype(F32)
        return slots[0]() if total is None else total + slots[0]()

    def total(self, value):
        for bit in [1] + [2 * b for b in self.bits]:
            value = value + lax.ppermute(value, "fsdp", [(i, i ^ bit) for i in range(self.fsdp)])
        bit = 1
        while bit < self.tp:
            value = value + lax.ppermute(value, "tp", [(i, i ^ bit) for i in range(self.tp)])
            bit *= 2
        return value


def pick(value, index, axis):
    return lax.dynamic_index_in_dim(value, index, axis, keepdims=False)


def pair_rows(links, mine, other):
    got = links.swap(other)
    first = jnp.where(links.core == 0, mine, got)
    second = jnp.where(links.core == 0, got, mine)
    return jnp.concatenate([first, second], axis=0)


def unpair_rows(links, block):
    half = block.shape[0] // 2
    mine = lax.dynamic_slice_in_dim(block, links.core * half, half, 0)
    got = links.swap(lax.dynamic_slice_in_dim(block, (1 - links.core) * half, half, 0))
    return jnp.where(links.core == 0, mine, got), jnp.where(links.core == 0, got, mine)


sync = lax.optimization_barrier


def tables_of(segment_rows):
    seqs, length = segment_rows.shape
    width = 2 * HD
    starts = jnp.sum((segment_rows[:, None, :] < segment_rows[:, :, None]).astype(jnp.int32), axis=-1)
    places = (jnp.arange(length, dtype=jnp.int32)[None] - starts).reshape(-1).astype(F32)
    inverse_freq = jnp.power(10000.0, -jnp.arange(0, ROT, 2, dtype=F32) / ROT)
    angles = places[:, None] * jnp.tile(inverse_freq, width // (ROT // 2))[None, :]
    lane = jnp.arange(width, dtype=jnp.int32)[None, :]
    turn = lane % HD
    cos = jnp.where(turn < ROT, jnp.cos(angles), 1.0)
    sine = jnp.sin(angles)
    sa = jnp.where(turn < ROT // 2, -sine, 0.0)
    sb = jnp.where((turn >= ROT // 2) & (turn < ROT), sine, 0.0)
    same = segment_rows.reshape(-1, 1) == lane
    key_mark = jnp.where(same, 1.0, 0.0).astype(BF16)
    query_mark = jnp.where(same | (lane >= 8), 0.0, -MASKED).astype(BF16)
    return cos, sa, sb, query_mark, key_mark


def body(
    tokens,
    segments,
    attn_gain,
    attn_shift,
    mlp_gain,
    mlp_shift,
    qkv_weight,
    qkv_bias,
    out_weight,
    out_bias,
    up_weight,
    up_bias,
    down_weight,
    down_bias,
    cotangent,
):
    links = Links()
    tp = links.tp
    rows, depth = tokens.shape
    length = segments.shape[1]
    head_cols = qkv_weight.shape[2] // 2
    unit_cols = up_weight.shape[1] // 2

    def halves(shard, axis):
        size = shard.shape[axis] // 2
        return [lax.dynamic_slice_in_dim(shard, c * size, size, axis) for c in (links.core, 1 - links.core)]

    qkv_halves = [v.reshape(v.shape[0], -1) for v in halves(qkv_weight, 2)]
    out_halves = [v.T for v in halves(out_weight, 0)]
    up_halves = halves(up_weight, 1)
    down_halves = [v.T for v in halves(down_weight, 0)]
    attn_slots = [pair_rows(links, *[jnp.concatenate(v, axis=1) for v in zip(qkv_halves, out_halves)])]
    mlp_slots = [pair_rows(links, *[jnp.concatenate(v, axis=1) for v in zip(up_halves, down_halves)])]
    qkv_cols = 3 * head_cols

    half = tp // 2
    per = max(1, 2 * HD // head_cols)

    by_hops = links.places == 4 and per == 1
    place = jnp.full((1,), links.place if by_hops else 0, jnp.int32)

    def join_pair(slots):
        if per == 1:
            return slots[0]
        lead = slots[0].shape[0]
        return jnp.concatenate([v.reshape(lead, 4, head_cols) for v in slots], axis=2).reshape(lead, -1)

    def join_qkv(slots):
        if per == 1:
            return slots[0]
        lead = slots[0].shape[0]
        return jnp.concatenate([v.reshape(lead, 3, head_cols) for v in slots], axis=2).reshape(lead, -1)

    def split_pair(value, parts):
        if per == 1:
            return [value]
        lead = value.shape[0]
        blocks = value.reshape(lead, parts, per, head_cols)
        return [blocks[:, :, j].reshape(lead, -1) for j in range(per)]

    groups = [list(range(0, half)), list(range(half, tp))]

    lane_of = [(links.lane - s) % tp for s in range(tp)]
    qkv_bias_lanes = pick(qkv_bias.reshape(3, tp, 2, head_cols), links.core, 2)
    up_bias_lanes = pick(up_bias.reshape(tp, 2, unit_cols), links.core, 1)
    qkv_bias_groups = [
        jnp.concatenate(
            [
                join_qkv([pick(qkv_bias_lanes, lane_of[s], 1).reshape(1, -1) for s in g[i : i + per]])
                for i in range(0, half, per)
            ],
            axis=1,
        ).astype(F32)
        for g in groups
    ]
    up_bias_groups = [
        jnp.concatenate([pick(up_bias_lanes, lane_of[s], 0) for s in g]).astype(F32)[None] for g in groups
    ]

    gains = jnp.stack([v.astype(F32) for v in (attn_gain, attn_shift, mlp_gain, mlp_shift)])
    own_segments = lax.dynamic_slice_in_dim(segments, links.lane * rows // length, rows // length, 0)
    tables = tables_of(jnp.concatenate([own_segments, links.swap(own_segments)], axis=0))
    x_other = links.swap(tokens)
    normed = prepare(tokens, x_other, cotangent, links.swap(cotangent), gains)

    def start_gather(slots):
        return [links.near_places(v) if by_hops else links.gather_other(v) for v in slots]

    def end_gather(states):
        return [links.far_place(v, s) for s, v in enumerate(states)] if by_hops else states

    def pairs_of(states):
        if per == 1:
            return states
        return [{0: join_pair([v[0] for v in states[i : i + per]])} for i in range(0, half, per)]

    def attention_part(g, states, an, dy):
        return attention(pairs_of(states), place, an, dy, qkv_bias_groups[g], tables, length)

    def attention_grads(attended, dmixed, ant, dyt):
        blocks = weight_grads(place, links.places if by_hops else 1, ant, dmixed, dyt, attended, half // per)
        return blocks if per == 1 else [{0: v} for b in blocks for v in split_pair(b[0], 4)]

    def mlp_grads(active, dgate, mnt, dyt):
        return weight_grads(place, links.places if by_hops else 1, mnt, dgate, dyt, active, half)

    def start_scatter(slots):
        return slots, [links.scatter_far(v, s) for s, v in enumerate(slots)] if by_hops else []

    def next_scatter(state):
        slots, far = state
        if not by_hops:
            return [links.scatter_other(v[0]) for v in slots]
        return [(v[0], links.scatter_near(v, f, s)) for s, (v, f) in enumerate(zip(slots, far))]

    def end_scatter(states):
        def term(state):
            if not by_hops:
                return state.astype(F32)
            own, near = state
            return own.astype(F32) + near[0].astype(F32) + near[1].astype(F32)

        return [partial(term, state) for state in states]

    for s in range(1, half):
        attn_slots.append(links.ring(attn_slots[-1]))
        mlp_slots.append(links.ring(mlp_slots[-1]))
    gather_a = start_gather(attn_slots)
    gather_a, tables, normed = sync((gather_a, tables, normed))
    gather_a = end_gather(gather_a)
    gather_a, mlp_slots, attn_slots, normed = sync((gather_a, mlp_slots, attn_slots, normed))
    an, mn, dy2, ant, mnt, dyt = normed

    gather_b = start_gather(mlp_slots)
    for s in range(half, tp):
        mlp_slots.append(links.ring(mlp_slots[-1]))
        attn_slots.append(links.ring(attn_slots[-1]))
    att0, dmix0, qkv0, out0 = attention_part(0, gather_a, an, dy2)
    gather_b, att0, dmix0, mn = sync((gather_b, att0, dmix0, mn))
    gather_b = end_gather(gather_b)
    grad_a0 = attention_grads(att0, dmix0, ant, dyt)
    gather_b, grad_a0, mn, mlp_slots = sync((gather_b, grad_a0, mn, mlp_slots))

    gather_c = start_gather(mlp_slots[half:])
    act0, dgate0, gate_sum0, up0, down0 = mlp_front(gather_b, place, mn, dy2, up_bias_groups[0])
    gather_c, act0, dgate0 = sync((gather_c, act0, dgate0))
    gather_c = end_gather(gather_c)
    grad_m0 = mlp_grads(act0, dgate0, mnt, dyt)
    gather_c, grad_m0, mn, attn_slots = sync((gather_c, grad_m0, mn, attn_slots))

    gather_d = start_gather(attn_slots[half:])
    scatter_b = start_scatter(grad_m0)
    act1, dgate1, gate_sum1, up1, down1 = mlp_front(gather_c, place, mn, dy2, up_bias_groups[1])
    gather_d, scatter_b, act1, dgate1 = sync((gather_d, scatter_b, act1, dgate1))
    gather_d = end_gather(gather_d)
    scatter_b = next_scatter(scatter_b)
    grad_m1 = mlp_grads(act1, dgate1, mnt, dyt)
    gather_d, grad_m1, an = sync((gather_d, grad_m1, an))

    scatter_c = start_scatter(grad_m1)
    scatter_a = start_scatter(grad_a0)
    att1, dmix1, qkv1, out1 = attention_part(1, gather_d, an, dy2)
    scatter_b, scatter_c, scatter_a, att1, dmix1 = sync((scatter_b, scatter_c, scatter_a, att1, dmix1))
    sum_b = end_scatter(scatter_b)
    scatter_c = next_scatter(scatter_c)
    scatter_a = next_scatter(scatter_a)
    grad_a1 = attention_grads(att1, dmix1, ant, dyt)
    scatter_d = start_scatter(grad_a1)
    out_terms = ((att0, out0), (att1, out1), (act0, down0), (act1, down1))
    (sent_out,) = branch_out(out_terms, rows)
    other_out = links.swap(sent_out)
    scatter_d, sent_out, dgate1 = sync((scatter_d, sent_out, dgate1))
    scatter_d = next_scatter(scatter_d)
    terms = ((dgate0, up0), (dgate1, up1), (dmix0, qkv0), (dmix1, qkv1))
    sent_pull, sums_other = pull_back(terms, x_other, gains, rows, BF16)
    other_pull = links.swap(sent_pull)
    scatter_c, scatter_a, sums_other, act0 = sync((scatter_c, scatter_a, sums_other, act0))
    sum_c = end_scatter(scatter_c)
    sum_a = end_scatter(scatter_a)
    pulled, sums_own = pull_back(terms, tokens, gains, 0, F32)
    scatter_d, pulled, att0 = sync((scatter_d, pulled, att0))
    sum_d = end_scatter(scatter_d)
    end_bias = (out_bias.astype(F32) + down_bias.astype(F32))[None]
    out_terms = ((att0, out0), (att1, out1), (act0, down0), (act1, down1))
    output, input_grad = branch_out(
        out_terms, rows, [tokens, other_out, end_bias, cotangent, pulled, other_pull]
    )

    mlp_own = unpair_rows(links, links.scatter_lanes(sum_b + sum_c))
    attn_own = unpair_rows(links, links.scatter_lanes(sum_a + sum_d))
    up_grad = jnp.concatenate([v[:, :unit_cols] for v in mlp_own], axis=1)
    down_grad = jnp.concatenate([v[:, unit_cols:] for v in mlp_own], axis=1).T
    qkv_grad = jnp.concatenate([v[:, :qkv_cols].reshape(-1, 3, head_cols) for v in attn_own], axis=2)
    out_grad = jnp.concatenate([v[:, qkv_cols:] for v in attn_own], axis=1).T

    def spread(values):
        lead, cols = values[0].shape
        full = jnp.zeros((lead, tp, 2, cols), F32)
        for s, value in enumerate(values):
            full = lax.dynamic_update_slice(full, value.reshape(lead, 1, 1, cols), (0, lane_of[s], links.core, 0))
        return full.reshape(-1)

    qkv_sums = [jnp.sum(d.astype(F32), axis=0, keepdims=True) for d in (dmix0, dmix1)]
    pair_sums = [v for d in qkv_sums for v in jnp.split(d, half // per, axis=1)]
    qkv_bias_part = spread([v.reshape(3, head_cols) for d in pair_sums for v in split_pair(d, 3)])
    up_bias_part = spread([v for part in (gate_sum0, gate_sum1) for v in jnp.split(part, half, axis=1)])
    bias_part = jnp.sum(cotangent.astype(F32), axis=0)
    pieces = [
        *(sums_own + sums_other)[:4],
        qkv_bias_part,
        bias_part,
        up_bias_part,
    ]
    sizes = [v.shape[0] for v in pieces]
    summed = links.total(jnp.concatenate(pieces).reshape(-1, 128)).reshape(-1)
    sums = []
    at = 0
    for size in sizes:
        sums.append(summed[at : at + size])
        at += size
    return (
        output,
        input_grad,
        sums[0],
        sums[1],
        sums[2],
        sums[3],
        qkv_grad,
        sums[4].reshape(qkv_bias.shape),
        out_grad,
        sums[5],
        up_grad,
        sums[6],
        down_grad,
        sums[5],
    )


def solution(mesh):
    placed = (
        P(("fsdp", "tp"), None),
        P("fsdp", None),
        P(),
        P(),
        P(),
        P(),
        P("fsdp", None, "tp"),
        P(),
        P("tp", "fsdp"),
        P(),
        P("fsdp", "tp"),
        P(),
        P("tp", "fsdp"),
        P(),
        P(("fsdp", "tp"), None),
    )
    return jax.shard_map(
        body,
        mesh=mesh,
        in_specs=placed,
        out_specs=(
            P(("fsdp", "tp"), None),
            P(("fsdp", "tp"), None),
            P(),
            P(),
            P(),
            P(),
            P("fsdp", None, "tp"),
            P(),
            P("tp", "fsdp"),
            P(),
            P("fsdp", "tp"),
            P(),
            P("tp", "fsdp"),
            P(),
        ),
        check_vma=False,
    )
```

```python
from functools import partial
import math

import jax
import jax.numpy as jnp
from jax import lax
from jax.experimental import pallas as pl
from jax.experimental.pallas import tpu as pltpu
from jax.sharding import PartitionSpec as P

HD = 64
ROT = 16
EPS = 1e-05
MASKED = 1e30
F32 = jnp.float32
BF16 = jnp.bfloat16
VMEM_BYTES = 56 * 1024 * 1024
NT = (((1,), (1,)), ((), ()))
TN = (((0,), (0,)), ((), ()))
NN = (((1,), (0,)), ((), ()))

dot32 = partial(lax.dot_general, preferred_element_type=F32)


def whole_spec(value):
    return pl.BlockSpec(value.shape, lambda *_: (0,) * value.ndim)


def place_rows(piece, key, place_ref, whole):
    rows = piece.shape[0]
    if rows == whole.shape[0]:
        return slice(None)
    return pl.ds(pl.multiple_of((place_ref[0] ^ key) * rows, rows), rows)


def prepare_kernel(x_own, x_other, dy_own, dy_other, gain_ref, an_ref, mn_ref, dy_ref):
    step = pl.program_id(0)
    half = pl.num_programs(0) // 2

    def work(x_ref, grad_ref):
        xhat, _ = row_norm(x_ref[...].astype(F32))
        an = (xhat * gain_ref[0:1, :] + gain_ref[1:2, :]).astype(BF16)
        mn = (xhat * gain_ref[2:3, :] + gain_ref[3:4, :]).astype(BF16)
        dy = grad_ref[...]
        an_ref[...], mn_ref[...], dy_ref[...] = an, mn, dy

    @pl.when(step < half)
    def _():
        work(x_own, dy_own)

    @pl.when(step >= half)
    def _():
        work(x_other, dy_other)


def prepare(x_own, x_other, dy_own, dy_other, gains):
    rows, depth = x_own.shape
    br = min(512, rows)
    half = rows // br
    own = pl.BlockSpec((br, depth), lambda i: (jnp.minimum(i, half - 1), 0))
    other = pl.BlockSpec((br, depth), lambda i: (jnp.maximum(i - half, 0), 0))
    tall = pl.BlockSpec((br, depth), lambda i: (i, 0))
    return pl.pallas_call(
        prepare_kernel,
        grid=(2 * half,),
        in_specs=[own, other, own, other, whole_spec(gains)],
        out_specs=[tall] * 3,
        out_shape=[jax.ShapeDtypeStruct((2 * rows, depth), BF16)] * 3,
        compiler_params=pltpu.CompilerParams(vmem_limit_bytes=VMEM_BYTES),
        cost_estimate=pl.CostEstimate(
            flops=40 * rows * depth, bytes_accessed=32 * rows * depth, transcendentals=2 * rows
        ),
        name="prepare",
    )(x_own, x_other, dy_own, dy_other, gains)


def attention_kernel(place_ref, an_ref, dy_ref, bias_ref, cos_ref, sa_ref, sb_ref, qf_ref, kf_ref, *refs, keys, bq):
    length = an_ref.shape[0]
    width = 2 * HD
    count = len(keys)
    piece_refs, refs = refs[: sum(map(len, keys))], refs[sum(map(len, keys)) :]
    att_ref, dmix_ref, sum_ref, qkv_ref, out_ref, mixed_scr, do_scr, dk_scr, dv_scr = refs
    seq, pair = pl.program_id(0), pl.program_id(1)

    @pl.when((seq == 0) & (pair == 0))
    def _():
        at = 0
        for j, pair_keys in enumerate(keys):
            for ref, (key, lead) in zip(piece_refs[at : at + len(pair_keys)], pair_keys):
                into = place_rows(ref, key, place_ref, qkv_ref)
                qkv_ref[into, j * 3 * width : (j + 1) * 3 * width] = ref[:, lead : lead + 3 * width]
                out_ref[into, j * width : (j + 1) * width] = ref[:, lead + 3 * width : lead + 4 * width]
            at += len(pair_keys)

    @pl.when(pair == 0)
    def _():
        step = min(256, length)
        for r in range(0, length, step):
            mixed = dot32(an_ref[r : r + step, :], qkv_ref[...], NN) + bias_ref[...]
            do = dot32(dy_ref[r : r + step, :], out_ref[...], NN).astype(BF16)
            for j in range(count):
                mixed_scr[j, r : r + step, :] = mixed[:, j * 3 * width : (j + 1) * 3 * width]
                do_scr[j, r : r + step, :] = do[:, j * width : (j + 1) * width]

    mixed = mixed_scr.at[pair]
    cos, sa, sb = cos_ref[...], sa_ref[...], sb_ref[...]
    scale = 1.0 / math.sqrt(HD)
    half = ROT // 2

    def turn(v, c, a, b, sign):
        side = pltpu.roll(v, width - half, 1) * a + pltpu.roll(v, half, 1) * b
        return v * c + side if sign > 0 else v * c - side

    q = turn(mixed[:, 0:width], cos, sa, sb, 1).astype(BF16)
    k = turn(mixed[:, width : 2 * width], cos, sa, sb, 1).astype(BF16)
    v = mixed[:, 2 * width : 3 * width].astype(BF16)
    do = do_scr[pair]
    lane = lax.broadcasted_iota(jnp.int32, (length, width), 1)
    zero = jnp.zeros((), BF16)
    qs = (q.astype(F32) * scale).astype(BF16)
    qf = qf_ref[...]
    kaug = jnp.concatenate([k, kf_ref[...]], axis=1)
    heads = []
    for h in range(2):
        m = (lane // HD) == h
        qm = jnp.where(m, qs, zero)
        heads.append(
            (
                jnp.concatenate([qm, qf], axis=1),
                qm,
                jnp.where(m, k, zero),
                jnp.where(m, v, zero),
                jnp.where(m, do, zero),
            )
        )
    causal = lax.broadcasted_iota(jnp.int32, (bq, bq), 1) <= lax.broadcasted_iota(jnp.int32, (bq, bq), 0)
    blocks = length // bq
    for i in range(blocks):
        r0 = i * bq
        w = r0 + bq
        att = dq = dkp = dvp = None
        for qaug, qm, km, vm, dom in heads:
            s = dot32(qaug[r0:w], kaug[:w], NT)
            diagonal = jnp.where(causal, s[:, r0:], -MASKED)
            s = diagonal if i == 0 else jnp.concatenate([s[:, :r0], diagonal], axis=1)
            e = jnp.exp(s - jnp.max(s, axis=1, keepdims=True))
            p = e * (1.0 / jnp.sum(e, axis=1, keepdims=True))
            pb = p.astype(BF16)
            o = dot32(pb, vm[:w], NN)
            dp = dot32(dom[r0:w], v[:w], NT)
            delta = jnp.sum(p * dp, axis=1, keepdims=True)
            ds = (p * (dp - delta)).astype(BF16)
            x = dot32(ds, km[:w], NN)
            a = dot32(pb, dom[r0:w], TN)
            b = dot32(ds, qm[r0:w], TN)
            if att is None:
                att, dq, dvp, dkp = o, x, a, b
            else:
                att, dq, dvp, dkp = att + o, dq + x, dvp + a, dkp + b
        att_ref[r0:w, :] = att.astype(BF16)
        dmix_ref[r0:w, 0:width] = turn(dq * scale, cos[r0:w], sa[r0:w], sb[r0:w], -1).astype(BF16)
        if i > 0:
            dk_scr[:r0] += dkp[:r0]
            dv_scr[:r0] += dvp[:r0]
        dk_scr[r0:w] = dkp[r0:]
        dv_scr[r0:w] = dvp[r0:]
    dmix_ref[:, width : 2 * width] = turn(dk_scr[...], cos, sa, sb, -1).astype(BF16)
    dmix_ref[:, 2 * width : 3 * width] = dv_scr[...].astype(BF16)
    part = jnp.sum(dmix_ref[...].astype(F32), axis=0, keepdims=True)

    @pl.when(seq == 0)
    def _():
        sum_ref[pair] = part

    @pl.when(seq > 0)
    def _():
        sum_ref[pair] += part


def attention(pairs, place, an, dy, bias, tables, length):
    rows, depth = an.shape
    width = 2 * HD
    seqs = rows // length
    count = len(pairs)
    row = pl.BlockSpec((length, depth), lambda s, j, p: (s, 0))
    table = pl.BlockSpec((length, width), lambda s, j, p: (s, 0))
    pieces = [piece for pair in pairs for piece, _, _ in pair]
    units = seqs * count
    shapes = [
        jax.ShapeDtypeStruct((rows, count * width), BF16),
        jax.ShapeDtypeStruct((rows, count * 3 * width), BF16),
        jax.ShapeDtypeStruct((count, 1, 3 * width), F32),
        jax.ShapeDtypeStruct((depth, count * 3 * width), BF16),
        jax.ShapeDtypeStruct((depth, count * width), BF16),
    ]
    return pl.pallas_call(
        partial(attention_kernel, keys=[[v[1:] for v in pair] for pair in pairs], bq=min(512, length)),
        grid_spec=pltpu.PrefetchScalarGridSpec(
            num_scalar_prefetch=1,
            grid=(seqs, count),
            in_specs=[row, row, whole_spec(bias)] + [table] * 5 + [whole_spec(v) for v in pieces],
            out_specs=[
                pl.BlockSpec((length, width), lambda s, j, p: (s, j)),
                pl.BlockSpec((length, 3 * width), lambda s, j, p: (s, j)),
            ]
            + [whole_spec(v) for v in shapes[2:]],
            scratch_shapes=[
                pltpu.VMEM((count, length, 3 * width), F32),
                pltpu.VMEM((count, length, width), BF16),
                pltpu.VMEM((length, width), F32),
                pltpu.VMEM((length, width), F32),
            ],
        ),
        out_shape=shapes,
        compiler_params=pltpu.CompilerParams(vmem_limit_bytes=VMEM_BYTES),
        cost_estimate=pl.CostEstimate(
            flops=units * (32 * length * length * width + 8 * length * depth * width),
            bytes_accessed=units * length * (depth * 4 + width * 40),
            transcendentals=units * 2 * length * length,
        ),
        name="attention",
    )(place, an, dy, bias, *tables, *pieces)


def mlp_kernel(place_ref, mn_ref, dy_ref, bias_ref, *refs, keys):
    piece_refs, refs = refs[: sum(map(len, keys))], refs[sum(map(len, keys)) :]
    act_ref, dgate_ref, sum_ref, up_ref, down_ref = refs
    units = up_ref.shape[1] // len(keys)
    step = pl.program_id(0)

    @pl.when(step == 0)
    def _():
        at = 0
        for j, slot_keys in enumerate(keys):
            for ref, (key, lead) in zip(piece_refs[at : at + len(slot_keys)], slot_keys):
                into = place_rows(ref, key, place_ref, up_ref)
                up_ref[into, j * units : (j + 1) * units] = ref[:, lead : lead + units]
                down_ref[into, j * units : (j + 1) * units] = ref[:, lead + units : lead + 2 * units]
            at += len(slot_keys)

    part = []
    for c in range(0, up_ref.shape[1], units):
        col = slice(c, c + units)
        gate = dot32(mn_ref[...], up_ref[:, col], NN) + bias_ref[:, col]
        dact = dot32(dy_ref[...], down_ref[:, col], NN)
        e = jnp.exp(gate * gate * -0.5)
        pdf = e * (1.0 / math.sqrt(2.0 * math.pi))
        cdf = 0.5 + 0.5 * lax.erf(gate * math.sqrt(0.5))
        act_ref[:, col] = (gate * cdf).astype(BF16)
        dgate = (dact * (cdf + gate * pdf)).astype(BF16)
        dgate_ref[:, col] = dgate
        part.append(jnp.sum(dgate.astype(F32), axis=0, keepdims=True))
    part = jnp.concatenate(part, axis=1)

    @pl.when(step == 0)
    def _():
        sum_ref[...] = part

    @pl.when(step > 0)
    def _():
        sum_ref[...] += part


def mlp_front(slots, place, mn, dy, bias):
    rows, depth = mn.shape
    units = bias.shape[1] // len(slots)
    count = len(slots)
    br = min(512, rows)
    row = pl.BlockSpec((br, depth), lambda r, p: (r, 0))
    tile = pl.BlockSpec((br, count * units), lambda r, p: (r, 0))
    pieces = [piece for slot in slots for piece, _, _ in slot]
    shapes = [
        jax.ShapeDtypeStruct((rows, count * units), BF16),
        jax.ShapeDtypeStruct((rows, count * units), BF16),
        jax.ShapeDtypeStruct((1, count * units), F32),
        jax.ShapeDtypeStruct((depth, count * units), BF16),
        jax.ShapeDtypeStruct((depth, count * units), BF16),
    ]
    return pl.pallas_call(
        partial(mlp_kernel, keys=[[v[1:] for v in slot] for slot in slots]),
        grid_spec=pltpu.PrefetchScalarGridSpec(
            num_scalar_prefetch=1,
            grid=(rows // br,),
            in_specs=[row, row, whole_spec(bias)] + [whole_spec(v) for v in pieces],
            out_specs=[tile, tile] + [whole_spec(v) for v in shapes[2:]],
        ),
        out_shape=shapes,
        compiler_params=pltpu.CompilerParams(vmem_limit_bytes=VMEM_BYTES),
        cost_estimate=pl.CostEstimate(
            flops=4 * rows * depth * count * units,
            bytes_accessed=rows * depth * 4 + count * (units * depth * 8 + rows * units * 4),
            transcendentals=2 * rows * count * units,
        ),
        name="mlp_front",
    )(place, mn, dy, bias, *pieces)


def grads_kernel(place_ref, left_a, left_b, right_a, right_b, *refs, count, keys):
    outs, (sum_a, sum_b) = refs[:-2], refs[-2:]
    step = pl.program_id(0)

    @pl.when(step == 0)
    def _():
        sum_a[...] = dot32(left_a[...], right_a[...], TN)
        sum_b[...] = dot32(left_b[...], right_b[...], TN)

    @pl.when(step > 0)
    def _():
        sum_a[...] += dot32(left_a[...], right_a[...], TN)
        sum_b[...] += dot32(left_b[...], right_b[...], TN)

    @pl.when(step == pl.num_programs(0) - 1)
    def _():
        wa, wb = right_a.shape[1] // count, right_b.shape[1] // count
        width = wa + wb
        for j in range(count):
            for n, key in enumerate(keys):
                out = outs[j] if key == 3 else outs[n + count - 1 if len(keys) > 1 else 0]
                at = place_rows(out, key, place_ref, sum_a)
                first = 0 if key == 3 else j * width
                out[:, first : first + wa] = sum_a[at, j * wa : (j + 1) * wa].astype(BF16)
                out[:, first + wa : first + width] = sum_b[at, j * wb : (j + 1) * wb].astype(BF16)


def weight_grads(place, places, left_a, right_a, left_b, right_b, count):
    rows, depth = left_a.shape
    keys = (3, 1, 2, 0) if places == 4 else (0,)
    size = depth // len(keys)
    br = min(512, rows)
    wa, wb = right_a.shape[1], right_b.shape[1]
    block = lambda v: pl.BlockSpec((br, v.shape[1]), lambda i, p: (i, 0))
    far = jax.ShapeDtypeStruct((size, (wa + wb) // count), BF16)
    near = jax.ShapeDtypeStruct((size, wa + wb), BF16)
    shapes = [far] * count + [near] * 3 if places == 4 else [near]
    found = pl.pallas_call(
        partial(grads_kernel, count=count, keys=keys),
        grid_spec=pltpu.PrefetchScalarGridSpec(
            num_scalar_prefetch=1,
            grid=(rows // br,),
            in_specs=[block(v) for v in (left_a, left_b, right_a, right_b)],
            out_specs=[whole_spec(v) for v in shapes],
            scratch_shapes=[pltpu.VMEM((depth, wa), F32), pltpu.VMEM((depth, wb), F32)],
        ),
        out_shape=shapes,
        compiler_params=pltpu.CompilerParams(vmem_limit_bytes=VMEM_BYTES),
        cost_estimate=pl.CostEstimate(
            flops=2 * rows * depth * (wa + wb),
            bytes_accessed=4 * rows * depth + 2 * (wa + wb) * (rows + depth),
            transcendentals=0,
        ),
        name="weight_grads",
    )(place, left_a, left_b, right_a, right_b)
    return found


def row_norm(x):
    centre = x - jnp.mean(x, axis=-1, keepdims=True)
    rstd = lax.rsqrt(jnp.mean(centre * centre, axis=-1, keepdims=True) + EPS)
    return centre * rstd, rstd


def pull_kernel(*refs):
    dg0, up0, dg1, up1, dm0, qkv0, dm1, qkv1, x_ref, gain_ref = refs[:10]
    out_ref, sum_ref = refs[-2:]
    n_mlp = dot32(dg0[...], up0[...], NT) + dot32(dg1[...], up1[...], NT)
    n_attn = dot32(dm0[...], qkv0[...], NT) + dot32(dm1[...], qkv1[...], NT)
    xhat, rstd = row_norm(x_ref[...].astype(F32))
    u = n_attn * gain_ref[0:1, :] + n_mlp * gain_ref[2:3, :]
    parts = [jnp.sum(v, axis=0, keepdims=True) for v in (n_attn * xhat, n_attn, n_mlp * xhat, n_mlp)]
    part = jnp.concatenate(parts + [jnp.zeros((4, u.shape[1]), F32)], axis=0)

    @pl.when(pl.program_id(0) == 0)
    def _():
        sum_ref[...] = part

    @pl.when(pl.program_id(0) > 0)
    def _():
        sum_ref[...] += part

    out_ref[...] = u.astype(out_ref.dtype)


def pull_back(terms, x, gains, first_row, dtype):
    rows, depth = x.shape
    br = min(256, rows)
    first = first_row // br
    block = lambda v: pl.BlockSpec((br, v.shape[1]), lambda i: (i + first, 0))
    specs, args = [], []
    for grad, weight in terms:
        specs += [block(grad), whole_spec(weight)]
        args += [grad, weight]
    tile = pl.BlockSpec((br, depth), lambda i: (i, 0))
    width = sum(grad.shape[1] for grad, _ in terms)
    return pl.pallas_call(
        pull_kernel,
        grid=(rows // br,),
        in_specs=specs + [tile, whole_spec(gains)],
        out_specs=[tile, pl.BlockSpec((8, depth), lambda i: (0, 0))],
        out_shape=[jax.ShapeDtypeStruct((rows, depth), dtype), jax.ShapeDtypeStruct((8, depth), F32)],
        compiler_params=pltpu.CompilerParams(vmem_limit_bytes=VMEM_BYTES),
        cost_estimate=pl.CostEstimate(
            flops=2 * rows * width * depth,
            bytes_accessed=2 * width * (rows + depth) + rows * depth * 8,
            transcendentals=rows,
        ),
        name="pull_back",
    )(*args, x, gains)


def out_kernel(*refs, own):
    att0, out0, att1, out1, act0, down0, act1, down1 = refs[:8]
    y = dot32(act0[...], down0[...], NT) + dot32(act1[...], down1[...], NT)
    y = y + dot32(att0[...], out0[...], NT) + dot32(att1[...], out1[...], NT)
    if not own:
        refs[-1][...] = y.astype(BF16)
        return
    x_ref, other_ref, bias_ref, dy_ref, pull_ref, other_pull_ref, y_ref, grad_ref = refs[8:]
    x = x_ref[...].astype(F32)
    y_ref[...] = (y + x + other_ref[...].astype(F32) + bias_ref[...]).astype(BF16)
    xhat, rstd = row_norm(x)
    u = pull_ref[...] + other_pull_ref[...].astype(F32)
    u = u - jnp.mean(u, axis=-1, keepdims=True) - xhat * jnp.mean(u * xhat, axis=-1, keepdims=True)
    grad_ref[...] = dy_ref[...].astype(F32) + rstd * u


def branch_out(terms, rows, last=None):
    own = last is not None
    depth = terms[0][1].shape[0]
    br = min(256, rows)
    first = 0 if own else rows // br
    tile = pl.BlockSpec((br, depth), lambda i: (i, 0))
    specs, args = [], []
    for value, weight in terms:
        specs += [pl.BlockSpec((br, value.shape[1]), lambda i: (i + first, 0)), whole_spec(weight)]
        args += [value, weight]
    if own:
        specs += [whole_spec(v) if v.shape[0] == 1 else tile for v in last]
        args += last
    width = sum(value.shape[1] for value, _ in terms)
    shapes = [jax.ShapeDtypeStruct((rows, depth), BF16)] + [jax.ShapeDtypeStruct((rows, depth), F32)] * own
    return pl.pallas_call(
        partial(out_kernel, own=own),
        grid=(rows // br,),
        in_specs=specs,
        out_specs=[tile] * len(shapes),
        out_shape=shapes,
        compiler_params=pltpu.CompilerParams(vmem_limit_bytes=VMEM_BYTES),
        cost_estimate=pl.CostEstimate(
            flops=2 * rows * width * depth,
            bytes_accessed=2 * width * (rows + depth) + rows * depth * (18 if own else 2),
            transcendentals=0,
        ),
        name="branch_out",
    )(*args)


class Links:
    def __init__(self):
        self.fsdp = lax.axis_size("fsdp")
        self.tp = lax.axis_size("tp")
        index = lax.axis_index("fsdp")
        self.core = index % 2
        self.place = index // 2
        self.lane = lax.axis_index("tp")
        self.places = self.fsdp // 2
        self.cores = [list(range(c, self.fsdp, 2)) for c in range(2)]
        self.bits = [1 << b for b in range((self.places - 1).bit_length())]

    def swap(self, value):
        return lax.ppermute(value, "fsdp", [(i, i ^ 1) for i in range(self.fsdp)])

    def hop(self, value, bit):
        return lax.ppermute(value, "fsdp", [(i, i ^ (2 * bit)) for i in range(self.fsdp)])

    def ring(self, value):
        return lax.ppermute(value, "tp", [(i, (i + 1) % self.tp) for i in range(self.tp)])


    def near_places(self, piece):
        return self.hop(piece, 1), self.hop(piece, 2)

    def far_parts(self, near):
        cut = near[0].shape[1] // 2
        return near[1][:, :cut], near[0][:, cut:]

    def far_place(self, parts):
        return self.hop(parts[0], 1), self.hop(parts[1], 2)

    def scatter_far(self, far):
        return self.hop(far[0], 2), self.hop(far[1], 1)

    def add_far(self, one, two, far):
        cut = one.shape[1] // 2
        first = (one[:, :cut].astype(F32) + far[0].astype(F32)).astype(BF16)
        second = (two[:, cut:].astype(F32) + far[1].astype(F32)).astype(BF16)
        return lax.dynamic_update_slice(one, first, (0, 0)), lax.dynamic_update_slice(two, second, (0, cut))

    def scatter_near(self, one, two):
        return self.hop(one, 1), self.hop(two, 2)

    def gather_other(self, piece):
        return lax.all_gather(piece, "fsdp", axis=0, tiled=True, axis_index_groups=self.cores)

    def scatter_other(self, value):
        return lax.psum_scatter(
            value, "fsdp", scatter_dimension=0, tiled=True, axis_index_groups=self.cores
        )

    def ring_sum(self, total, terms):
        for term in terms:
            total = term if total is None else total + term
            total = self.ring(total.astype(BF16)).astype(F32)
        return total

    def sum_steps(self):
        steps = [("fsdp", self.fsdp, 1 << b) for b in range((self.fsdp - 1).bit_length())]
        return steps + [("tp", self.tp, 1 << b) for b in range((self.tp - 1).bit_length())]

    def sum_step(self, value, step):
        name, size, bit = step
        return value + lax.ppermute(value, name, [(i, i ^ bit) for i in range(size)])


def pick(value, index, axis):
    return lax.dynamic_index_in_dim(value, index, axis, keepdims=False)


def pair_rows(links, mine, other):
    got = links.swap(other)
    first = jnp.where(links.core == 0, mine, got)
    second = jnp.where(links.core == 0, got, mine)
    return jnp.concatenate([first, second], axis=0)


def unpair_rows(links, block):
    half = block.shape[0] // 2
    mine = lax.dynamic_slice_in_dim(block, links.core * half, half, 0)
    got = links.swap(lax.dynamic_slice_in_dim(block, (1 - links.core) * half, half, 0))
    return jnp.where(links.core == 0, mine, got), jnp.where(links.core == 0, got, mine)


sync = lax.optimization_barrier


def tables_of(segment_rows):
    seqs, length = segment_rows.shape
    width = 2 * HD
    starts = jnp.sum((segment_rows[:, None, :] < segment_rows[:, :, None]).astype(jnp.int32), axis=-1)
    places = (jnp.arange(length, dtype=jnp.int32)[None] - starts).reshape(-1).astype(F32)
    inverse_freq = jnp.power(10000.0, -jnp.arange(0, ROT, 2, dtype=F32) / ROT)
    angles = places[:, None] * jnp.tile(inverse_freq, width // (ROT // 2))[None, :]
    lane = jnp.arange(width, dtype=jnp.int32)[None, :]
    turn = lane % HD
    cos = jnp.where(turn < ROT, jnp.cos(angles), 1.0)
    sine = jnp.sin(angles)
    sa = jnp.where(turn < ROT // 2, -sine, 0.0)
    sb = jnp.where((turn >= ROT // 2) & (turn < ROT), sine, 0.0)
    same = segment_rows.reshape(-1, 1) == lane
    key_mark = jnp.where(same, 1.0, 0.0).astype(BF16)
    query_mark = jnp.where(same | (lane >= 8), 0.0, -MASKED).astype(BF16)
    return cos, sa, sb, query_mark, key_mark


def body(
    tokens,
    segments,
    attn_gain,
    attn_shift,
    mlp_gain,
    mlp_shift,
    qkv_weight,
    qkv_bias,
    out_weight,
    out_bias,
    up_weight,
    up_bias,
    down_weight,
    down_bias,
    cotangent,
):
    links = Links()
    tp = links.tp
    rows, depth = tokens.shape
    length = segments.shape[1]
    head_cols = qkv_weight.shape[2] // 2
    unit_cols = up_weight.shape[1] // 2

    def halves(shard, axis):
        size = shard.shape[axis] // 2
        return [lax.dynamic_slice_in_dim(shard, c * size, size, axis) for c in (links.core, 1 - links.core)]

    qkv_halves = [v.reshape(v.shape[0], -1) for v in halves(qkv_weight, 2)]
    out_halves = [v.T for v in halves(out_weight, 0)]
    up_halves = halves(up_weight, 1)
    down_halves = [v.T for v in halves(down_weight, 0)]
    attn_slots = [pair_rows(links, *[jnp.concatenate(v, axis=1) for v in zip(qkv_halves, out_halves)])]
    mlp_slots = [pair_rows(links, *[jnp.concatenate(v, axis=1) for v in zip(up_halves, down_halves)])]
    qkv_cols = 3 * head_cols

    half = tp // 2
    per = max(1, 2 * HD // head_cols)

    by_hops = links.places == 4 and per == 1
    place = jnp.full((1,), links.place if by_hops else 0, jnp.int32)

    def join_pair(slots):
        if per == 1:
            return slots[0]
        lead = slots[0].shape[0]
        return jnp.concatenate([v.reshape(lead, 4, head_cols) for v in slots], axis=2).reshape(lead, -1)

    def join_qkv(slots):
        if per == 1:
            return slots[0]
        lead = slots[0].shape[0]
        return jnp.concatenate([v.reshape(lead, 3, head_cols) for v in slots], axis=2).reshape(lead, -1)

    def split_pair(value, parts):
        if per == 1:
            return [value]
        lead = value.shape[0]
        blocks = value.reshape(lead, parts, per, head_cols)
        return [blocks[:, :, j].reshape(lead, -1) for j in range(per)]

    groups = [list(range(0, half)), list(range(half, tp))]

    lane_of = [(links.lane - s) % tp for s in range(tp)]
    qkv_bias_lanes = pick(qkv_bias.reshape(3, tp, 2, head_cols), links.core, 2)
    up_bias_lanes = pick(up_bias.reshape(tp, 2, unit_cols), links.core, 1)
    qkv_bias_groups = [
        jnp.concatenate(
            [
                join_qkv([pick(qkv_bias_lanes, lane_of[s], 1).reshape(1, -1) for s in g[i : i + per]])
                for i in range(0, half, per)
            ],
            axis=1,
        ).astype(F32)
        for g in groups
    ]
    up_bias_groups = [
        jnp.concatenate([pick(up_bias_lanes, lane_of[s], 0) for s in g]).astype(F32)[None] for g in groups
    ]

    gains = jnp.stack([v.astype(F32) for v in (attn_gain, attn_shift, mlp_gain, mlp_shift)])
    x_other, dy_other = links.swap(tokens), links.swap(cotangent)

    def group_piece(slots):
        return jnp.concatenate(slots, axis=1)

    def near(piece):
        return links.near_places(piece) if by_hops else links.gather_other(piece)

    def far_parts(got):
        return links.far_parts(got) if by_hops else ()

    def far(parts):
        return links.far_place(parts) if by_hops else ()

    def pieces_of(piece, got, last, width):
        if not by_hops:
            return [[(got, 0, j * width)] for j in range(half)]
        return [[(piece, 0, j * width), (got[0], 1, j * width), (got[1], 2, j * width), (last[j], 3, 0)] for j in (0, 1)]

    def pairs_of(slots):
        if per == 1:
            return slots
        columns = [v[0][0][:, v[0][2] : v[0][2] + 4 * head_cols] for v in slots]
        return [[(join_pair(columns[i : i + per]), 0, 0)] for i in range(0, half, per)]

    def attention_part(g, slots, an, dy):
        return attention(pairs_of(slots), place, an, dy, qkv_bias_groups[g], tables, length)

    def attention_grads(attended, dmixed):
        found = weight_grads(place, links.places if by_hops else 1, an, dmixed, dy2, attended, half // per)
        if per == 1:
            return found
        pairs = jnp.split(found[0], half // per, axis=1)
        return [jnp.concatenate([v for pair in pairs for v in split_pair(pair, 4)], axis=1)]

    def mlp_grads(active, dgate):
        return weight_grads(place, links.places if by_hops else 1, mn, dgate, dy2, active, half)

    def sum_far(blocks):
        return links.scatter_far(blocks[:2]) if by_hops else links.scatter_other(blocks[0])

    def add_far(blocks, got):
        return links.add_far(blocks[2], blocks[3], got) if by_hops else got

    def sum_near(sent):
        return links.scatter_near(*sent) if by_hops else sent

    def place_sum(blocks, got):
        if by_hops:
            got = blocks[4].astype(F32) + got[0].astype(F32) + got[1].astype(F32)
        return jnp.split(got.astype(F32), half, axis=1)

    def small_sums():
        def spread(values):
            lead, cols = values[0].shape
            full = jnp.zeros((lead, tp, 2, cols), F32)
            for s, value in enumerate(values):
                full = lax.dynamic_update_slice(full, value.reshape(lead, 1, 1, cols), (0, lane_of[s], links.core, 0))
            return full.reshape(-1)

        pair_sums = [v[i] for v in (qkv_sum0, qkv_sum1) for i in range(half // per)]
        qkv_bias_part = spread([v.reshape(3, head_cols) for d in pair_sums for v in split_pair(d, 3)])
        up_bias_part = spread([v for part in (gate_sum0, gate_sum1) for v in jnp.split(part, half, axis=1)])
        bias_part = jnp.sum(cotangent.astype(F32), axis=0)
        pieces = [
            *(sums_own + sums_other)[:4],
            qkv_bias_part,
            bias_part,
            up_bias_part,
        ]
        return jnp.concatenate(pieces).reshape(-1, 128)

    sizes = [depth] * 4 + [qkv_bias.size, depth, up_bias.size]

    attn_cols, mlp_cols = 4 * head_cols, 2 * unit_cols
    ring = links.ring
    own_segments = lax.dynamic_slice_in_dim(segments, links.lane * rows // length, rows // length, 0)
    pair_segments = jnp.concatenate([own_segments, links.swap(own_segments)], axis=0)
    attn_slots, pair_segments = sync((attn_slots, pair_segments))
    for s in range(1, half):
        attn_slots.append(ring(attn_slots[-1]))
    if by_hops:
        got = [links.near_places(attn_slots[0])]
        tables = tables_of(pair_segments)
        attn_slots, tables, x_other, dy_other = sync((attn_slots, tables, x_other, dy_other))
        got.append(links.near_places(attn_slots[1]))
        last = [links.hop(got[0][1], 1)]
        mlp_slots.append(ring(mlp_slots[0]))
        normed = prepare(tokens, x_other, cotangent, dy_other, gains)
        got, last, normed = sync((got, last, normed))
        last.append(links.hop(got[1][0], 2))
        group_a = [[(attn_slots[j], 0, 0), (got[j][0], 1, 0), (got[j][1], 2, 0), (last[j], 3, 0)] for j in (0, 1)]
    else:
        tables = tables_of(pair_segments)
        normed = prepare(tokens, x_other, cotangent, dy_other, gains)
        for s in range(1, half):
            mlp_slots.append(ring(mlp_slots[-1]))
        group_a = pieces_of(None, near(group_piece(attn_slots)), None, attn_cols)
    arrays = [[v[0] for v in slot] for slot in group_a]
    arrays, mlp_slots, attn_slots, normed = sync((arrays, mlp_slots, attn_slots, normed))
    group_a = [[(v, *w[1:]) for v, w in zip(vs, slot)] for vs, slot in zip(arrays, group_a)]
    an, mn, dy2 = normed
    piece_b = group_piece(mlp_slots)
    piece_b, an, attn_slots = sync((piece_b, an, attn_slots))

    def ring_on(slots, count):
        for _ in range(count):
            slots.append(ring(slots[-1]))
        return slots

    near_b = near(piece_b)
    mlp_slots = ring_on(mlp_slots, 1)
    attn_slots = ring_on(attn_slots, 1)
    att0, dmix0, qkv_sum0, qkv0, out0 = attention_part(0, group_a, an, dy2)
    near_b, mlp_slots, attn_slots, att0, dmix0 = sync((near_b, mlp_slots, attn_slots, att0, dmix0))
    parts_b = far_parts(near_b)
    parts_b, mlp_slots, attn_slots, att0 = sync((parts_b, mlp_slots, attn_slots, att0))

    far_b = far(parts_b)
    mlp_slots = ring_on(mlp_slots, half - 1)
    attn_slots = ring_on(attn_slots, half - 1)
    grad_a0 = attention_grads(att0, dmix0)
    far_b, mlp_slots, attn_slots, grad_a0 = sync((far_b, mlp_slots, attn_slots, grad_a0))
    piece_c = group_piece(mlp_slots[half:])
    piece_c, mn = sync((piece_c, mn))

    near_c = near(piece_c)
    group_b = pieces_of(piece_b, near_b, far_b, mlp_cols)
    act0, dgate0, gate_sum0, up0, down0 = mlp_front(group_b, place, mn, dy2, up_bias_groups[0])
    near_c, act0 = sync((near_c, act0))
    parts_c = far_parts(near_c)
    parts_c, act0 = sync((parts_c, act0))

    far_c = far(parts_c)
    far_a = sum_far(grad_a0)
    grad_b = mlp_grads(act0, dgate0)
    far_c, far_a, grad_b = sync((far_c, far_a, grad_b))
    piece_d = group_piece(attn_slots[half:])
    sent_a = add_far(grad_a0, far_a)
    piece_d, sent_a, mn = sync((piece_d, sent_a, mn))

    near_d = near(piece_d)
    near_a = sum_near(sent_a)
    group_c = pieces_of(piece_c, near_c, far_c, mlp_cols)
    act1, dgate1, gate_sum1, up1, down1 = mlp_front(group_c, place, mn, dy2, up_bias_groups[1])
    near_d, near_a, act1 = sync((near_d, near_a, act1))
    parts_d = far_parts(near_d)
    parts_d, act1 = sync((parts_d, act1))

    far_d = far(parts_d)
    back_b = sum_far(grad_b)
    grad_c = mlp_grads(act1, dgate1)
    far_d, back_b, grad_c = sync((far_d, back_b, grad_c))
    sent_b = add_far(grad_b, back_b)
    sum_a = place_sum(grad_a0, near_a)
    sent_b, sum_a, an = sync((sent_b, sum_a, an))

    back_near_b = sum_near(sent_b)
    back_c = sum_far(grad_c)
    ring_a = links.ring_sum(None, sum_a[1:])
    group_d = pieces_of(piece_d, near_d, far_d, attn_cols)
    att1, dmix1, qkv_sum1, qkv1, out1 = attention_part(1, group_d, an, dy2)
    back_near_b, back_c, ring_a, att1 = sync((back_near_b, back_c, ring_a, att1))
    sent_c = add_far(grad_c, back_c)
    sum_b = place_sum(grad_b, back_near_b)
    sent_c, sum_b, att1 = sync((sent_c, sum_b, att1))

    back_near_c = sum_near(sent_c)
    ring_m = links.ring_sum(None, sum_b[1:])
    grad_d = attention_grads(att1, dmix1)
    ring_m, grad_d, dgate1 = sync((ring_m, grad_d, dgate1))

    back_d = sum_far(grad_d)
    terms = ((dgate0, up0), (dgate1, up1), (dmix0, qkv0), (dmix1, qkv1))
    sent_pull, sums_other = pull_back(terms, x_other, gains, rows, BF16)
    back_near_c, back_d, sent_pull = sync((back_near_c, back_d, sent_pull))
    sum_c = place_sum(grad_c, back_near_c)
    sent_d = add_far(grad_d, back_d)
    term_m = ring_m + sum_c[0]
    sum_c, sent_d, term_m, dgate1 = sync((sum_c, sent_d, term_m, dgate1))

    near_e = sum_near(sent_d)
    ring_m = links.ring_sum(None, [term_m] + sum_c[1:-1])
    other_pull = links.swap(sent_pull)
    terms = ((dgate0, up0), (dgate1, up1), (dmix0, qkv0), (dmix1, qkv1))
    pulled, sums_own = pull_back(terms, tokens, gains, 0, F32)
    near_e, ring_m, other_pull, pulled = sync((near_e, ring_m, other_pull, pulled))
    sum_d = place_sum(grad_d, near_e)
    term_m = ring_m + sum_c[-1]
    term_a = ring_a + sum_d[0]
    small = small_sums()
    sum_d, term_m, term_a, small, att1 = sync((sum_d, term_m, term_a, small, att1))

    steps = links.sum_steps()
    ring_m = links.ring_sum(None, [term_m])
    ring_a = links.ring_sum(None, [term_a] + sum_d[1:-1])
    small = links.sum_step(small, steps[0])
    out_terms = ((att0, out0), (att1, out1), (act0, down0), (act1, down1))
    (sent_out,) = branch_out(out_terms, rows)
    ring_m, ring_a, small, sent_out = sync((ring_m, ring_a, small, sent_out))
    term_a = ring_a + sum_d[-1]
    sum_m = ring_m + sum_b[0]
    term_a, sum_m, small, sent_out = sync((term_a, sum_m, small, sent_out))

    other_out = links.swap(sent_out)
    ring_a = links.ring_sum(None, [term_a])
    mlp_own = unpair_rows(links, sum_m)
    small = links.sum_step(small, steps[1])
    other_out, small, att1, mlp_own, ring_a = sync((other_out, small, att1, mlp_own, ring_a))

    sum_e = ring_a + sum_a[0]
    sum_e, small, att1 = sync((sum_e, small, att1))
    attn_own = unpair_rows(links, sum_e)
    small = links.sum_step(small, steps[2])
    end_bias = (out_bias.astype(F32) + down_bias.astype(F32))[None]
    out_terms = ((att0, out0), (att1, out1), (act0, down0), (act1, down1))
    output, input_grad = branch_out(
        out_terms, rows, [tokens, other_out, end_bias, cotangent, pulled, other_pull]
    )
    small, attn_own, output, input_grad = sync((small, attn_own, output, input_grad))
    for step in steps[3:]:
        small = links.sum_step(small, step)
    up_grad = jnp.concatenate([v[:, :unit_cols] for v in mlp_own], axis=1)
    down_grad = jnp.concatenate([v[:, unit_cols:] for v in mlp_own], axis=1).T
    qkv_grad = jnp.concatenate([v[:, :qkv_cols].reshape(-1, 3, head_cols) for v in attn_own], axis=2)
    out_grad = jnp.concatenate([v[:, qkv_cols:] for v in attn_own], axis=1).T

    summed = small.reshape(-1)
    sums = []
    at = 0
    for size in sizes:
        sums.append(summed[at : at + size])
        at += size
    return (
        output,
        input_grad,
        sums[0],
        sums[1],
        sums[2],
        sums[3],
        qkv_grad,
        sums[4].reshape(qkv_bias.shape),
        out_grad,
        sums[5],
        up_grad,
        sums[6],
        down_grad,
        sums[5],
    )


def solution(mesh):
    placed = (
        P(("fsdp", "tp"), None),
        P("fsdp", None),
        P(),
        P(),
        P(),
        P(),
        P("fsdp", None, "tp"),
        P(),
        P("tp", "fsdp"),
        P(),
        P("fsdp", "tp"),
        P(),
        P("tp", "fsdp"),
        P(),
        P(("fsdp", "tp"), None),
    )
    return jax.shard_map(
        body,
        mesh=mesh,
        in_specs=placed,
        out_specs=(
            P(("fsdp", "tp"), None),
            P(("fsdp", "tp"), None),
            P(),
            P(),
            P(),
            P(),
            P("fsdp", None, "tp"),
            P(),
            P("tp", "fsdp"),
            P(),
            P("fsdp", "tp"),
            P(),
            P("tp", "fsdp"),
            P(),
        ),
        check_vma=False,
    )
```

```python
from functools import partial
import math

import jax
import jax.numpy as jnp
from jax import lax
from jax.experimental import pallas as pl
from jax.experimental.pallas import tpu as pltpu
from jax.sharding import PartitionSpec as P

HD = 64
ROT = 16
EPS = 1e-05
MASKED = 1e30
F32 = jnp.float32
BF16 = jnp.bfloat16
VMEM_BYTES = 56 * 1024 * 1024
NT = (((1,), (1,)), ((), ()))
TN = (((0,), (0,)), ((), ()))
NN = (((1,), (0,)), ((), ()))

dot32 = partial(lax.dot_general, preferred_element_type=F32)


def whole_spec(value):
    return pl.BlockSpec(value.shape, lambda *_: (0,) * value.ndim)


def place_rows(piece, key, place_ref, whole):
    rows = piece.shape[0]
    if rows == whole.shape[0]:
        return slice(None)
    return pl.ds(pl.multiple_of((place_ref[0] ^ key) * rows, rows), rows)


def prepare_kernel(x_own, x_other, dy_own, dy_other, gain_ref, an_ref, mn_ref, dy_ref):
    step = pl.program_id(0)
    half = pl.num_programs(0) // 2

    def work(x_ref, grad_ref):
        xhat, _ = row_norm(x_ref[...].astype(F32))
        an = (xhat * gain_ref[0:1, :] + gain_ref[1:2, :]).astype(BF16)
        mn = (xhat * gain_ref[2:3, :] + gain_ref[3:4, :]).astype(BF16)
        dy = grad_ref[...]
        an_ref[...], mn_ref[...], dy_ref[...] = an, mn, dy

    @pl.when(step < half)
    def _():
        work(x_own, dy_own)

    @pl.when(step >= half)
    def _():
        work(x_other, dy_other)


def prepare(x_own, x_other, dy_own, dy_other, gains):
    rows, depth = x_own.shape
    br = min(512, rows)
    half = rows // br
    own = pl.BlockSpec((br, depth), lambda i: (jnp.minimum(i, half - 1), 0))
    other = pl.BlockSpec((br, depth), lambda i: (jnp.maximum(i - half, 0), 0))
    tall = pl.BlockSpec((br, depth), lambda i: (i, 0))
    return pl.pallas_call(
        prepare_kernel,
        grid=(2 * half,),
        in_specs=[own, other, own, other, whole_spec(gains)],
        out_specs=[tall] * 3,
        out_shape=[jax.ShapeDtypeStruct((2 * rows, depth), BF16)] * 3,
        compiler_params=pltpu.CompilerParams(vmem_limit_bytes=VMEM_BYTES),
        cost_estimate=pl.CostEstimate(
            flops=40 * rows * depth, bytes_accessed=32 * rows * depth, transcendentals=2 * rows
        ),
        name="prepare",
    )(x_own, x_other, dy_own, dy_other, gains)


def attention_kernel(place_ref, an_ref, dy_ref, bias_ref, turn_ref, mark_ref, *refs, keys, bq):
    length = an_ref.shape[0]
    width = 2 * HD
    piece_refs, refs = refs[: len(keys)], refs[len(keys) :]
    att_ref, dmix_ref, sum_ref, qkv_ref, out_ref, mixed_scr, do_scr, dk_scr, dv_scr = refs
    count = mixed_scr.shape[0]
    seq, pair = pl.program_id(0), pl.program_id(1)

    @pl.when((seq == 0) & (pair == 0))
    def _():
        for ref, (key, parts) in zip(piece_refs, keys):
            into = place_rows(ref, key, place_ref, qkv_ref)
            for j, lead in parts:
                qkv_ref[into, j * 3 * width : (j + 1) * 3 * width] = ref[:, lead : lead + 3 * width]
                out_ref[into, j * width : (j + 1) * width] = ref[:, lead + 3 * width : lead + 4 * width]

    @pl.when(pair == 0)
    def _():
        step = min(256, length)
        for r in range(0, length, step):
            mixed = dot32(an_ref[r : r + step, :], qkv_ref[...], NN) + bias_ref[...]
            do = dot32(dy_ref[r : r + step, :], out_ref[...], NN).astype(BF16)
            for j in range(count):
                mixed_scr[j, r : r + step, :] = mixed[:, j * 3 * width : (j + 1) * 3 * width]
                do_scr[j, r : r + step, :] = do[:, j * width : (j + 1) * width]

    mixed = mixed_scr.at[pair]
    scale = 1.0 / math.sqrt(HD)
    half = ROT // 2
    lane = lax.broadcasted_iota(jnp.int32, (length, width), 1)
    dim = lane % HD
    table = turn_ref[...]
    cos = jnp.where(dim < half, table, jnp.where(dim < ROT, pltpu.roll(table, half, 1), 1.0))
    sa = jnp.where(dim < half, -pltpu.roll(table, width - half, 1), 0.0)
    sb = jnp.where((dim >= half) & (dim < ROT), table, 0.0)

    def turn(v, c, a, b, sign):
        side = pltpu.roll(v, width - half, 1) * a + pltpu.roll(v, half, 1) * b
        return v * c + side if sign > 0 else v * c - side

    q = turn(mixed[:, 0:width], cos, sa, sb, 1).astype(BF16)
    k = turn(mixed[:, width : 2 * width], cos, sa, sb, 1).astype(BF16)
    v = mixed[:, 2 * width : 3 * width].astype(BF16)
    do = do_scr[pair]
    zero = jnp.zeros((), BF16)
    qs = (q.astype(F32) * scale).astype(BF16)
    qf = jnp.where((mark_ref[...].astype(F32) > 0.5) | (lane >= 8), 0.0, -MASKED).astype(BF16)
    kaug = jnp.concatenate([k, mark_ref[...]], axis=1)
    heads = []
    for h in range(2):
        m = (lane // HD) == h
        qm = jnp.where(m, qs, zero)
        heads.append(
            (
                jnp.concatenate([qm, qf], axis=1),
                qm,
                jnp.where(m, k, zero),
                jnp.where(m, v, zero),
                jnp.where(m, do, zero),
            )
        )
    causal = lax.broadcasted_iota(jnp.int32, (bq, bq), 1) <= lax.broadcasted_iota(jnp.int32, (bq, bq), 0)
    blocks = length // bq
    for i in range(blocks):
        r0 = i * bq
        w = r0 + bq
        att = dq = dkp = dvp = 0.0
        staged = []
        for qaug, qm, km, vm, dom in heads:
            s = dot32(qaug[r0:w], kaug[:w], NT)
            diagonal = jnp.where(causal, s[:, r0:], -MASKED)
            s = diagonal if i == 0 else jnp.concatenate([s[:, :r0], diagonal], axis=1)
            staged.append((s, dot32(dom[r0:w], v[:w], NT)))
        for (s, dp), (qaug, qm, km, vm, dom) in zip(staged, heads):
            e = jnp.exp(s - jnp.max(s, axis=1, keepdims=True))
            p = e * (1.0 / jnp.sum(e, axis=1, keepdims=True))
            pb = p.astype(BF16)
            o = dot32(pb, vm[:w], NN)
            delta = jnp.sum(o * dom[r0:w].astype(F32), axis=1, keepdims=True)
            ds = (p * (dp - delta)).astype(BF16)
            att, dq = att + o, dq + dot32(ds, km[:w], NN)
            dvp, dkp = dvp + dot32(pb, dom[r0:w], TN), dkp + dot32(ds, qm[r0:w], TN)
        att_ref[r0:w, :] = att.astype(BF16)
        dmix_ref[r0:w, 0:width] = turn(dq * scale, cos[r0:w], sa[r0:w], sb[r0:w], -1).astype(BF16)
        if i > 0:
            dk_scr[:r0] += dkp[:r0]
            dv_scr[:r0] += dvp[:r0]
        dk_scr[r0:w] = dkp[r0:]
        dv_scr[r0:w] = dvp[r0:]
    dmix_ref[:, width : 2 * width] = turn(dk_scr[...], cos, sa, sb, -1).astype(BF16)
    dmix_ref[:, 2 * width : 3 * width] = dv_scr[...].astype(BF16)
    part = jnp.sum(dmix_ref[...].astype(F32), axis=0, keepdims=True)

    @pl.when(seq == 0)
    def _():
        sum_ref[pair] = part

    @pl.when(seq > 0)
    def _():
        sum_ref[pair] += part


def attention(pieces, place, an, dy, bias, tables, length):
    rows, depth = an.shape
    width = 2 * HD
    seqs = rows // length
    count = bias.shape[1] // (3 * width)
    row = pl.BlockSpec((length, depth), lambda s, j, p: (s, 0))
    table = pl.BlockSpec((length, width), lambda s, j, p: (s, 0))
    arrays = [v[0] for v in pieces]
    units = seqs * count
    shapes = [
        jax.ShapeDtypeStruct((rows, count * width), BF16),
        jax.ShapeDtypeStruct((rows, count * 3 * width), BF16),
        jax.ShapeDtypeStruct((count, 1, 3 * width), F32),
        jax.ShapeDtypeStruct((depth, count * 3 * width), BF16),
        jax.ShapeDtypeStruct((depth, count * width), BF16),
    ]
    return pl.pallas_call(
        partial(attention_kernel, keys=[v[1:] for v in pieces], bq=min(512, length)),
        grid_spec=pltpu.PrefetchScalarGridSpec(
            num_scalar_prefetch=1,
            grid=(seqs, count),
            in_specs=[row, row, whole_spec(bias), table, table] + [whole_spec(v) for v in arrays],
            out_specs=[
                pl.BlockSpec((length, width), lambda s, j, p: (s, j)),
                pl.BlockSpec((length, 3 * width), lambda s, j, p: (s, j)),
            ]
            + [whole_spec(v) for v in shapes[2:]],
            scratch_shapes=[
                pltpu.VMEM((count, length, 3 * width), F32),
                pltpu.VMEM((count, length, width), BF16),
                pltpu.VMEM((length, width), F32),
                pltpu.VMEM((length, width), F32),
            ],
        ),
        out_shape=shapes,
        compiler_params=pltpu.CompilerParams(vmem_limit_bytes=VMEM_BYTES),
        cost_estimate=pl.CostEstimate(
            flops=units * (32 * length * length * width + 8 * length * depth * width),
            bytes_accessed=units * length * (depth * 4 + width * 40),
            transcendentals=units * 2 * length * length,
        ),
        name="attention",
    )(place, an, dy, bias, *tables, *arrays)


def mlp_kernel(place_ref, mn_ref, dy_ref, bias_ref, *refs, keys, count):
    piece_refs, refs = refs[: len(keys)], refs[len(keys) :]
    act_ref, dgate_ref, sum_ref, up_ref, down_ref = refs
    units = up_ref.shape[1] // count
    step = pl.program_id(0)

    @pl.when(step == 0)
    def _():
        sum_ref[...] = jnp.zeros_like(sum_ref)
        for ref, (key, parts) in zip(piece_refs, keys):
            into = place_rows(ref, key, place_ref, up_ref)
            for j, lead in parts:
                up_ref[into, j * units : (j + 1) * units] = ref[:, lead : lead + units]
                down_ref[into, j * units : (j + 1) * units] = ref[:, lead + units : lead + 2 * units]

    for c in range(0, up_ref.shape[1], units):
        col = slice(c, c + units)
        gate = dot32(mn_ref[...], up_ref[:, col], NN) + bias_ref[:, col]
        dact = dot32(dy_ref[...], down_ref[:, col], NN)
        cdf = 0.5 + 0.5 * lax.erf(gate * math.sqrt(0.5))
        pdf = jnp.exp(gate * gate * -0.5) * (1.0 / math.sqrt(2.0 * math.pi))
        act_ref[:, col] = (gate * cdf).astype(BF16)
        dgate = (dact * (cdf + gate * pdf)).astype(BF16)
        dgate_ref[:, col] = dgate
        sum_ref[:, col] += jnp.sum(dgate.astype(F32), axis=0, keepdims=True)


def mlp(pieces, place, mn, dy, bias, count):
    rows, depth = mn.shape
    units = bias.shape[1]
    br = min(512, rows)
    row = pl.BlockSpec((br, depth), lambda r, p: (r, 0))
    tile = pl.BlockSpec((br, units), lambda r, p: (r, 0))
    arrays = [v[0] for v in pieces]
    shapes = [
        jax.ShapeDtypeStruct((rows, units), BF16),
        jax.ShapeDtypeStruct((rows, units), BF16),
        jax.ShapeDtypeStruct((1, units), F32),
        jax.ShapeDtypeStruct((depth, units), BF16),
        jax.ShapeDtypeStruct((depth, units), BF16),
    ]
    return pl.pallas_call(
        partial(mlp_kernel, keys=[v[1:] for v in pieces], count=count),
        grid_spec=pltpu.PrefetchScalarGridSpec(
            num_scalar_prefetch=1,
            grid=(rows // br,),
            in_specs=[row, row, whole_spec(bias)] + [whole_spec(v) for v in arrays],
            out_specs=[tile, tile] + [whole_spec(v) for v in shapes[2:]],
        ),
        out_shape=shapes,
        compiler_params=pltpu.CompilerParams(vmem_limit_bytes=VMEM_BYTES),
        cost_estimate=pl.CostEstimate(
            flops=4 * rows * depth * units,
            bytes_accessed=rows * depth * 4 + units * depth * 8 + rows * units * 4,
            transcendentals=2 * rows * units,
        ),
        name="mlp",
    )(place, mn, dy, bias, *arrays)


def block_shapes(places, depth, wa, wb, count):
    if places != 4:
        return (0,), [jax.ShapeDtypeStruct((depth, wa + wb), BF16)]
    far = jax.ShapeDtypeStruct((depth // 4, (wa + wb) // count), BF16)
    near = jax.ShapeDtypeStruct((depth // 4, wa + wb), BF16)
    return (3, 1, 2, 0), [far] * count + [near] * 3


def put_blocks(outs, sum_a, sum_b, place_ref, count, keys):
    wa, wb = sum_a.shape[1] // count, sum_b.shape[1] // count
    width = wa + wb
    for j in range(count):
        for n, key in enumerate(keys):
            out = outs[j] if key == 3 else outs[n + count - 1 if len(keys) > 1 else 0]
            at = place_rows(out, key, place_ref, sum_a)
            first = 0 if key == 3 else j * width
            out[:, first : first + wa] = sum_a[at, j * wa : (j + 1) * wa].astype(BF16)
            out[:, first + wa : first + width] = sum_b[at, j * wb : (j + 1) * wb].astype(BF16)


def grads_kernel(place_ref, left_a, left_b, right_a, right_b, *refs, count, keys):
    outs, (sum_a, sum_b) = refs[:-2], refs[-2:]
    step = pl.program_id(0)

    @pl.when(step == 0)
    def _():
        sum_a[...] = dot32(left_a[...], right_a[...], TN)
        sum_b[...] = dot32(left_b[...], right_b[...], TN)

    @pl.when(step > 0)
    def _():
        sum_a[...] += dot32(left_a[...], right_a[...], TN)
        sum_b[...] += dot32(left_b[...], right_b[...], TN)

    @pl.when(step == pl.num_programs(0) - 1)
    def _():
        put_blocks(outs, sum_a, sum_b, place_ref, count, keys)


def weight_grads(place, places, left_a, right_a, left_b, right_b, count):
    rows, depth = left_a.shape
    br = min(512, rows)
    wa, wb = right_a.shape[1], right_b.shape[1]
    block = lambda v: pl.BlockSpec((br, v.shape[1]), lambda i, p: (i, 0))
    keys, shapes = block_shapes(places, depth, wa, wb, count)
    found = pl.pallas_call(
        partial(grads_kernel, count=count, keys=keys),
        grid_spec=pltpu.PrefetchScalarGridSpec(
            num_scalar_prefetch=1,
            grid=(rows // br,),
            in_specs=[block(v) for v in (left_a, left_b, right_a, right_b)],
            out_specs=[whole_spec(v) for v in shapes],
            scratch_shapes=[pltpu.VMEM((depth, wa), F32), pltpu.VMEM((depth, wb), F32)],
        ),
        out_shape=shapes,
        compiler_params=pltpu.CompilerParams(vmem_limit_bytes=VMEM_BYTES),
        cost_estimate=pl.CostEstimate(
            flops=2 * rows * depth * (wa + wb),
            bytes_accessed=4 * rows * depth + 2 * (wa + wb) * (rows + depth),
            transcendentals=0,
        ),
        name="weight_grads",
    )(place, left_a, left_b, right_a, right_b)
    return found


def row_norm(x):
    centre = x - jnp.mean(x, axis=-1, keepdims=True)
    rstd = lax.rsqrt(jnp.mean(centre * centre, axis=-1, keepdims=True) + EPS)
    return centre * rstd, rstd


def pull_kernel(*refs):
    dg0, up0, dg1, up1, dm0, qkv0, dm1, qkv1, x_ref, gain_ref = refs[:10]
    out_ref, sum_ref = refs[-2:]
    n_mlp = dot32(dg0[...], up0[...], NT) + dot32(dg1[...], up1[...], NT)
    n_attn = dot32(dm0[...], qkv0[...], NT) + dot32(dm1[...], qkv1[...], NT)
    xhat, rstd = row_norm(x_ref[...].astype(F32))
    u = n_attn * gain_ref[0:1, :] + n_mlp * gain_ref[2:3, :]
    parts = [jnp.sum(v, axis=0, keepdims=True) for v in (n_attn * xhat, n_attn, n_mlp * xhat, n_mlp)]
    part = jnp.concatenate(parts + [jnp.zeros((4, u.shape[1]), F32)], axis=0)

    @pl.when(pl.program_id(0) == 0)
    def _():
        sum_ref[...] = part

    @pl.when(pl.program_id(0) > 0)
    def _():
        sum_ref[...] += part

    out_ref[...] = u.astype(out_ref.dtype)


def pull_back(terms, x, gains, first_row, dtype):
    rows, depth = x.shape
    br = min(256, rows)
    first = first_row // br
    block = lambda v: pl.BlockSpec((br, v.shape[1]), lambda i: (i + first, 0))
    specs, args = [], []
    for grad, weight in terms:
        specs += [block(grad), whole_spec(weight)]
        args += [grad, weight]
    tile = pl.BlockSpec((br, depth), lambda i: (i, 0))
    width = sum(grad.shape[1] for grad, _ in terms)
    return pl.pallas_call(
        pull_kernel,
        grid=(rows // br,),
        in_specs=specs + [tile, whole_spec(gains)],
        out_specs=[tile, pl.BlockSpec((8, depth), lambda i: (0, 0))],
        out_shape=[jax.ShapeDtypeStruct((rows, depth), dtype), jax.ShapeDtypeStruct((8, depth), F32)],
        compiler_params=pltpu.CompilerParams(vmem_limit_bytes=VMEM_BYTES),
        cost_estimate=pl.CostEstimate(
            flops=2 * rows * width * depth,
            bytes_accessed=2 * width * (rows + depth) + rows * depth * 8,
            transcendentals=rows,
        ),
        name="pull_back",
    )(*args, x, gains)


def out_kernel(*refs, own):
    att0, out0, att1, out1, act0, down0, act1, down1 = refs[:8]
    y = dot32(act0[...], down0[...], NT) + dot32(act1[...], down1[...], NT)
    y = y + dot32(att0[...], out0[...], NT) + dot32(att1[...], out1[...], NT)
    if not own:
        refs[-1][...] = y.astype(BF16)
        return
    x_ref, other_ref, bias_ref, dy_ref, pull_ref, other_pull_ref, y_ref, grad_ref = refs[8:]
    x = x_ref[...].astype(F32)
    y_ref[...] = (y + x + other_ref[...].astype(F32) + bias_ref[...]).astype(BF16)
    xhat, rstd = row_norm(x)
    u = pull_ref[...] + other_pull_ref[...].astype(F32)
    u = u - jnp.mean(u, axis=-1, keepdims=True) - xhat * jnp.mean(u * xhat, axis=-1, keepdims=True)
    grad_ref[...] = dy_ref[...].astype(F32) + rstd * u


def branch_out(terms, rows, last=None):
    own = last is not None
    depth = terms[0][1].shape[0]
    br = min(256, rows)
    first = 0 if own else rows // br
    tile = pl.BlockSpec((br, depth), lambda i: (i, 0))
    specs, args = [], []
    for value, weight in terms:
        specs += [pl.BlockSpec((br, value.shape[1]), lambda i: (i + first, 0)), whole_spec(weight)]
        args += [value, weight]
    if own:
        specs += [whole_spec(v) if v.shape[0] == 1 else tile for v in last]
        args += last
    width = sum(value.shape[1] for value, _ in terms)
    shapes = [jax.ShapeDtypeStruct((rows, depth), BF16)] + [jax.ShapeDtypeStruct((rows, depth), F32)] * own
    return pl.pallas_call(
        partial(out_kernel, own=own),
        grid=(rows // br,),
        in_specs=specs,
        out_specs=[tile] * len(shapes),
        out_shape=shapes,
        compiler_params=pltpu.CompilerParams(vmem_limit_bytes=VMEM_BYTES),
        cost_estimate=pl.CostEstimate(
            flops=2 * rows * width * depth,
            bytes_accessed=2 * width * (rows + depth) + rows * depth * (18 if own else 2),
            transcendentals=0,
        ),
        name="branch_out",
    )(*args)


class Links:
    def __init__(self):
        self.fsdp = lax.axis_size("fsdp")
        self.tp = lax.axis_size("tp")
        index = lax.axis_index("fsdp")
        self.core = index % 2
        self.place = index // 2
        self.lane = lax.axis_index("tp")
        self.places = self.fsdp // 2
        self.cores = [list(range(c, self.fsdp, 2)) for c in range(2)]
        self.bits = [1 << b for b in range((self.places - 1).bit_length())]

    def swap(self, value):
        return lax.ppermute(value, "fsdp", [(i, i ^ 1) for i in range(self.fsdp)])

    def hop(self, value, bit):
        return lax.ppermute(value, "fsdp", [(i, i ^ (2 * bit)) for i in range(self.fsdp)])

    def ring(self, value):
        return lax.ppermute(value, "tp", [(i, (i + 1) % self.tp) for i in range(self.tp)])


    def near_places(self, piece):
        return self.hop(piece, 1), self.hop(piece, 2)

    def far_parts(self, near):
        cut = near[0].shape[1] // 2
        return near[1][:, :cut], near[0][:, cut:]

    def far_place(self, parts):
        return self.hop(parts[0], 1), self.hop(parts[1], 2)

    def scatter_far(self, far):
        return self.hop(far[0], 2), self.hop(far[1], 1)

    def add_far(self, one, two, far):
        cut = one.shape[1] // 2
        first = (one[:, :cut].astype(F32) + far[0].astype(F32)).astype(BF16)
        second = (two[:, cut:].astype(F32) + far[1].astype(F32)).astype(BF16)
        return lax.dynamic_update_slice(one, first, (0, 0)), lax.dynamic_update_slice(two, second, (0, cut))

    def scatter_near(self, one, two):
        return self.hop(one, 1), self.hop(two, 2)

    def gather_other(self, piece):
        return lax.all_gather(piece, "fsdp", axis=0, tiled=True, axis_index_groups=self.cores)

    def scatter_other(self, value):
        return lax.psum_scatter(
            value, "fsdp", scatter_dimension=0, tiled=True, axis_index_groups=self.cores
        )

    def back(self, value):
        return lax.ppermute(value, "tp", [(i, (i - 1) % self.tp) for i in range(self.tp)])

    def across(self, value):
        return lax.ppermute(value, "tp", [(i, (i + 2) % self.tp) for i in range(self.tp)])

    def ring_sum(self, total, terms):
        for term in terms:
            total = term if total is None else total + term
            total = self.ring(total.astype(BF16)).astype(F32)
        return total

    def sum_steps(self):
        steps = [("fsdp", self.fsdp, 1 << b) for b in range((self.fsdp - 1).bit_length())]
        return steps + [("tp", self.tp, 1 << b) for b in range((self.tp - 1).bit_length())]

    def sum_step(self, value, step):
        name, size, bit = step
        return value + lax.ppermute(value, name, [(i, i ^ bit) for i in range(size)])


def pick(value, index, axis):
    return lax.dynamic_index_in_dim(value, index, axis, keepdims=False)


def pair_rows(links, mine, other):
    got = links.swap(other)
    first = jnp.where(links.core == 0, mine, got)
    second = jnp.where(links.core == 0, got, mine)
    return jnp.concatenate([first, second], axis=0)


def unpair_rows(links, block):
    half = block.shape[0] // 2
    mine = lax.dynamic_slice_in_dim(block, links.core * half, half, 0)
    got = links.swap(lax.dynamic_slice_in_dim(block, (1 - links.core) * half, half, 0))
    return jnp.where(links.core == 0, mine, got), jnp.where(links.core == 0, got, mine)


sync = lax.optimization_barrier


def tables_of(segment_rows):
    length = segment_rows.shape[1]
    starts = jnp.sum((segment_rows[:, None, :] < segment_rows[:, :, None]).astype(jnp.int32), axis=-1)
    places = (jnp.arange(length, dtype=jnp.int32)[None] - starts).reshape(-1).astype(F32)
    inverse_freq = jnp.power(10000.0, -jnp.arange(0, ROT, 2, dtype=F32) / ROT)
    angles = inverse_freq[:, None] * places[None, :]
    turns = jnp.concatenate([jnp.cos(angles), jnp.sin(angles)], axis=0)
    marks = segment_rows.reshape(-1, 1) == jnp.arange(2 * HD, dtype=jnp.int32)[None, :]
    return jnp.tile(turns.T, (1, 2 * HD // ROT)), marks.astype(BF16)


def body(
    tokens,
    segments,
    attn_gain,
    attn_shift,
    mlp_gain,
    mlp_shift,
    qkv_weight,
    qkv_bias,
    out_weight,
    out_bias,
    up_weight,
    up_bias,
    down_weight,
    down_bias,
    cotangent,
):
    links = Links()
    tp = links.tp
    rows, depth = tokens.shape
    length = segments.shape[1]
    head_cols = qkv_weight.shape[2] // 2
    unit_cols = up_weight.shape[1] // 2

    def halves(shard, axis):
        size = shard.shape[axis] // 2
        return [lax.dynamic_slice_in_dim(shard, c * size, size, axis) for c in (links.core, 1 - links.core)]

    qkv_halves = [v.reshape(v.shape[0], -1) for v in halves(qkv_weight, 2)]
    out_halves = [v.T for v in halves(out_weight, 0)]
    up_halves = halves(up_weight, 1)
    down_halves = [v.T for v in halves(down_weight, 0)]
    attn_slots = [pair_rows(links, *[jnp.concatenate(v, axis=1) for v in zip(qkv_halves, out_halves)])]
    mlp_slots = [pair_rows(links, *[jnp.concatenate(v, axis=1) for v in zip(up_halves, down_halves)])]
    qkv_cols = 3 * head_cols

    half = tp // 2
    per = max(1, 2 * HD // head_cols)

    by_hops = links.places == 4 and per == 1 and tp == 4
    place = jnp.full((1,), links.place if by_hops else 0, jnp.int32)

    def join_pair(slots):
        if per == 1:
            return slots[0]
        lead = slots[0].shape[0]
        return jnp.concatenate([v.reshape(lead, 4, head_cols) for v in slots], axis=2).reshape(lead, -1)

    def join_qkv(slots):
        if per == 1:
            return slots[0]
        lead = slots[0].shape[0]
        return jnp.concatenate([v.reshape(lead, 3, head_cols) for v in slots], axis=2).reshape(lead, -1)

    def split_pair(value, parts):
        if per == 1:
            return [value]
        lead = value.shape[0]
        blocks = value.reshape(lead, parts, per, head_cols)
        return [blocks[:, :, j].reshape(lead, -1) for j in range(per)]

    groups = [list(range(0, half)), list(range(half, tp))]
    mlp_groups = [[1, 3], [0, 2]] if by_hops else groups

    lane_of = [(links.lane - s) % tp for s in range(tp)]
    qkv_bias_lanes = pick(qkv_bias.reshape(3, tp, 2, head_cols), links.core, 2)
    up_bias_lanes = pick(up_bias.reshape(tp, 2, unit_cols), links.core, 1)
    qkv_bias_groups = [
        jnp.concatenate(
            [
                join_qkv([pick(qkv_bias_lanes, lane_of[s], 1).reshape(1, -1) for s in g[i : i + per]])
                for i in range(0, half, per)
            ],
            axis=1,
        ).astype(F32)
        for g in groups
    ]
    up_bias_groups = [
        jnp.concatenate([pick(up_bias_lanes, lane_of[s], 0) for s in g]).astype(F32)[None] for g in mlp_groups
    ]

    gains = jnp.stack([v.astype(F32) for v in (attn_gain, attn_shift, mlp_gain, mlp_shift)])
    x_other, dy_other = links.swap(tokens), links.swap(cotangent)

    def group_piece(slots):
        return jnp.concatenate(slots, axis=1)

    def near(piece):
        return links.near_places(piece) if by_hops else links.gather_other(piece)

    def far_parts(got):
        return links.far_parts(got) if by_hops else ()

    def far(parts):
        return links.far_place(parts) if by_hops else ()

    def pieces_of(piece, got, last, width):
        both = tuple((j, j * width) for j in range(half))
        if not by_hops:
            return [(got, 0, both)]
        return [(piece, 0, both), (got[0], 1, both), (got[1], 2, both), (last[0], 3, ((0, 0),)), (last[1], 3, ((1, 0),))]

    def attention_part(g, pieces, an, dy):
        if per > 1:
            slots = jnp.split(pieces[0][0], half, axis=1)
            whole = jnp.concatenate([join_pair(slots[i : i + per]) for i in range(0, half, per)], axis=1)
            pieces = [(whole, 0, tuple((j, j * 8 * HD) for j in range(half // per)))]
        return attention(pieces, place, an, dy, qkv_bias_groups[g], tables, length)

    def attention_grads(attended, dmixed):
        found = weight_grads(place, links.places if by_hops else 1, an, dmixed, dy2, attended, half // per)
        if per == 1:
            return found
        pairs = jnp.split(found[0], half // per, axis=1)
        return [jnp.concatenate([v for pair in pairs for v in split_pair(pair, 4)], axis=1)]

    def mlp_part(g, pieces, mn, dy):
        return mlp(pieces, place, mn, dy, up_bias_groups[g], half)

    def mlp_grads(active, dgate):
        return weight_grads(place, links.places if by_hops else 1, mn, dgate, dy2, active, half)

    def sum_far(blocks):
        return links.scatter_far(blocks[:2]) if by_hops else links.scatter_other(blocks[0])

    def add_far(blocks, got):
        return links.add_far(blocks[2], blocks[3], got) if by_hops else got

    def sum_near(sent):
        return links.scatter_near(*sent) if by_hops else sent

    def place_sum(blocks, got):
        if by_hops:
            got = blocks[4].astype(F32) + got[0].astype(F32) + got[1].astype(F32)
        return jnp.split(got.astype(F32), half, axis=1)

    def small_sums():
        def spread(values):
            lead, cols = values[0].shape
            full = jnp.zeros((lead, tp, 2, cols), F32)
            for s, value in enumerate(values):
                full = lax.dynamic_update_slice(full, value.reshape(lead, 1, 1, cols), (0, lane_of[s], links.core, 0))
            return full.reshape(-1)

        pair_sums = [v[i] for v in (qkv_sum0, qkv_sum1) for i in range(half // per)]
        qkv_bias_part = spread([v.reshape(3, head_cols) for d in pair_sums for v in split_pair(d, 3)])
        gate_sums = [v for part in (gate_sum0, gate_sum1) for v in jnp.split(part, half, axis=1)]
        order = mlp_groups[0] + mlp_groups[1]
        up_bias_part = spread([gate_sums[order.index(s)] for s in range(tp)])
        bias_part = jnp.sum(cotangent.astype(F32), axis=0)
        pieces = [
            *(sums_own + sums_other)[:4],
            qkv_bias_part,
            bias_part,
            up_bias_part,
        ]
        return jnp.concatenate(pieces).reshape(-1, 128)

    sizes = [depth] * 4 + [qkv_bias.size, depth, up_bias.size]

    attn_cols, mlp_cols = 4 * head_cols, 2 * unit_cols
    ring, back = links.ring, links.back
    own_segments = lax.dynamic_slice_in_dim(segments, links.lane * rows // length, rows // length, 0)
    pair_segments = jnp.concatenate([own_segments, links.swap(own_segments)], axis=0)
    attn_slots, pair_segments = sync((attn_slots, pair_segments))
    if by_hops:
        attn = {0: attn_slots[0], 1: ring(attn_slots[0])}
        units = {0: mlp_slots[0]}
        got = [links.near_places(attn[0])]
        attn, units, pair_segments = sync((attn, units, pair_segments))
        got.append(links.near_places(attn[1]))
        units[1], units[3] = ring(units[0]), back(units[0])
        tables = tables_of(pair_segments)
        got, x_other, dy_other = sync((got, x_other, dy_other))
        last = [links.hop(got[0][1], 1), links.hop(got[1][0], 2)]
        normed = prepare(tokens, x_other, cotangent, dy_other, gains)
        units, last, normed, tables = sync((units, last, normed, tables))
        piece_b = group_piece([units[1], units[3]])
        piece_b, normed = sync((piece_b, normed))
        group_a = [
            (v, key, ((j, 0),))
            for j in (0, 1)
            for v, key in ((attn[j], 0), (got[j][0], 1), (got[j][1], 2), (last[j], 3))
        ]
    else:
        attn, units = {0: attn_slots[0]}, {0: mlp_slots[0]}
        for s in range(1, tp):
            attn[s] = ring(attn[s - 1])
            units[s] = ring(units[s - 1])
        tables = tables_of(pair_segments)
        normed = prepare(tokens, x_other, cotangent, dy_other, gains)
        group_a = pieces_of(None, near(group_piece([attn[s] for s in groups[0]])), None, attn_cols)
    an, mn, dy2 = normed
    if not by_hops:
        piece_b, piece_c, piece_d = [
            group_piece([v[s] for s in g]) for v, g in ((units, groups[0]), (units, groups[1]), (attn, groups[1]))
        ]
    piece_b, an = sync((piece_b, an))

    near_b = near(piece_b)
    if by_hops:
        units[2], attn[2], attn[3] = ring(units[1]), ring(attn[1]), back(attn[0])
    att0, dmix0, qkv_sum0, qkv0, out0 = attention_part(0, group_a, an, dy2)
    near_b, attn, units, att0 = sync((near_b, attn, units, att0))
    parts_b = far_parts(near_b)
    if by_hops:
        piece_c = group_piece([units[0], units[2]])
    parts_b, piece_c, att0 = sync((parts_b, piece_c, att0))

    far_b = far(parts_b)
    grad_a = attention_grads(att0, dmix0)
    far_b, grad_a, attn, mn = sync((far_b, grad_a, attn, mn))

    near_c = near(piece_c)
    act0, dgate0, gate_sum0, up0, down0 = mlp_part(0, pieces_of(piece_b, near_b, far_b, mlp_cols), mn, dy2)
    near_c, act0 = sync((near_c, act0))
    parts_c = far_parts(near_c)
    parts_c, act0 = sync((parts_c, act0))

    far_c = far(parts_c)
    back_a = sum_far(grad_a)
    grad_b = mlp_grads(act0, dgate0)
    far_c, back_a, grad_b, mn = sync((far_c, back_a, grad_b, mn))
    if by_hops:
        piece_d = group_piece([attn[2], attn[3]])
    sent_a = add_far(grad_a, back_a)
    piece_d, sent_a, mn = sync((piece_d, sent_a, mn))

    near_d = near(piece_d)
    near_a = sum_near(sent_a)
    act1, dgate1, gate_sum1, up1, down1 = mlp_part(1, pieces_of(piece_c, near_c, far_c, mlp_cols), mn, dy2)
    near_d, near_a, act1 = sync((near_d, near_a, act1))
    parts_d = far_parts(near_d)
    parts_d, act1 = sync((parts_d, act1))

    far_d = far(parts_d)
    back_b = sum_far(grad_b)
    grad_c = mlp_grads(act1, dgate1)
    far_d, back_b, grad_c, an = sync((far_d, back_b, grad_c, an))
    sent_b = add_far(grad_b, back_b)
    sum_a = place_sum(grad_a, near_a)
    sent_b, sum_a, grad_c, an = sync((sent_b, sum_a, grad_c, an))

    back_near_b = sum_near(sent_b)
    back_c = sum_far(grad_c)
    att1, dmix1, qkv_sum1, qkv1, out1 = attention_part(1, pieces_of(piece_d, near_d, far_d, attn_cols), an, dy2)
    back_near_b, back_c, att1 = sync((back_near_b, back_c, att1))
    sent_c = add_far(grad_c, back_c)
    sum_b = place_sum(grad_b, back_near_b)
    sent_c, sum_b, att1 = sync((sent_c, sum_b, att1))

    back_near_c = sum_near(sent_c)
    lanes_m = ring(sum_b[1].astype(BF16)) if by_hops else ()
    grad_d = attention_grads(att1, dmix1)
    grad_d, dgate1 = sync((grad_d, dgate1))

    back_d = sum_far(grad_d)
    terms = ((dgate0, up0), (dgate1, up1), (dmix0, qkv0), (dmix1, qkv1))
    sent_pull, sums_other = pull_back(terms, x_other, gains, rows, BF16)
    back_near_c, back_d, lanes_m, sent_pull, att1 = sync((back_near_c, back_d, lanes_m, sent_pull, att1))
    sum_c = place_sum(grad_c, back_near_c)
    last_m = sum_c[1].astype(BF16) if by_hops else ()
    sent_d = add_far(grad_d, back_d)
    sent_d, last_m, sent_pull, att1 = sync((sent_d, last_m, sent_pull, att1))

    back_near_d = sum_near(sent_d)
    last_m = back(last_m) if by_hops else ()
    other_pull = links.swap(sent_pull)
    out_terms = ((att0, out0), (att1, out1), (act0, down0), (act1, down1))
    (sent_out,) = branch_out(out_terms, rows)
    back_near_d, other_pull, last_m, sent_out, dgate1 = sync((back_near_d, other_pull, last_m, sent_out, dgate1))
    sum_d = place_sum(grad_d, back_near_d)
    lanes_a = [v.astype(BF16) for v in sum_d]
    if by_hops:
        last_m = (sum_b[0] + last_m.astype(F32)).astype(BF16)
    lanes_a, last_m, sent_out, dgate1 = sync((lanes_a, last_m, sent_out, dgate1))

    other_out = links.swap(sent_out)
    if by_hops:
        lanes_a = [back(lanes_a[0]), ring(lanes_a[1])]
        last_m = back(last_m)
    terms = ((dgate0, up0), (dgate1, up1), (dmix0, qkv0), (dmix1, qkv1))
    pulled, sums_own = pull_back(terms, tokens, gains, 0, F32)
    lanes_a, last_m, other_out, sums_own, att1 = sync((lanes_a, last_m, other_out, sums_own, att1))
    small = small_sums()
    steps = links.sum_steps()
    if by_hops:
        last_a = (sum_a[1] + lanes_a[0].astype(F32)).astype(BF16)
        sum_m = sum_c[0] + lanes_m.astype(F32) + last_m.astype(F32)
    else:
        last_a = ()
        sum_m = links.ring_sum(None, sum_b[1:] + sum_c) + sum_b[0]
    small, last_a, sum_m, att1 = sync((small, last_a, sum_m, att1))

    if by_hops:
        last_a = back(last_a)
    mlp_own = unpair_rows(links, sum_m)
    small = links.sum_step(small, steps[0])
    end_bias = (out_bias.astype(F32) + down_bias.astype(F32))[None]
    out_terms = ((att0, out0), (att1, out1), (act0, down0), (act1, down1))
    output, input_grad = branch_out(
        out_terms, rows, [tokens, other_out, end_bias, cotangent, pulled, other_pull]
    )
    small, last_a, mlp_own, output, input_grad = sync((small, last_a, mlp_own, output, input_grad))
    if by_hops:
        sum_e = sum_a[0] + lanes_a[1].astype(F32) + last_a.astype(F32)
    else:
        sum_e = links.ring_sum(None, sum_a[1:] + sum_d) + sum_a[0]
    attn_own = unpair_rows(links, sum_e)
    small = links.sum_step(links.sum_step(small, steps[1]), steps[2])
    if tp == 4 and links.fsdp == 8:
        a, b, c = [lax.ppermute(small, "tp", [(i, i ^ bit) for i in range(tp)]) for bit in (1, 2, 3)]
        small = (small + a) + (b + c)
    else:
        for step in steps[3:]:
            small = links.sum_step(small, step)
    up_grad = jnp.concatenate([v[:, :unit_cols] for v in mlp_own], axis=1)
    down_grad = jnp.concatenate([v[:, unit_cols:] for v in mlp_own], axis=1).T
    qkv_grad = jnp.concatenate([v[:, :qkv_cols].reshape(-1, 3, head_cols) for v in attn_own], axis=2)
    out_grad = jnp.concatenate([v[:, qkv_cols:] for v in attn_own], axis=1).T

    summed = small.reshape(-1)
    sums = []
    at = 0
    for size in sizes:
        sums.append(summed[at : at + size])
        at += size
    return (
        output,
        input_grad,
        sums[0],
        sums[1],
        sums[2],
        sums[3],
        qkv_grad,
        sums[4].reshape(qkv_bias.shape),
        out_grad,
        sums[5],
        up_grad,
        sums[6],
        down_grad,
        sums[5],
    )


def solution(mesh):
    placed = (
        P(("fsdp", "tp"), None),
        P("fsdp", None),
        P(),
        P(),
        P(),
        P(),
        P("fsdp", None, "tp"),
        P(),
        P("tp", "fsdp"),
        P(),
        P("fsdp", "tp"),
        P(),
        P("tp", "fsdp"),
        P(),
        P(("fsdp", "tp"), None),
    )
    return jax.shard_map(
        body,
        mesh=mesh,
        in_specs=placed,
        out_specs=(
            P(("fsdp", "tp"), None),
            P(("fsdp", "tp"), None),
            P(),
            P(),
            P(),
            P(),
            P("fsdp", None, "tp"),
            P(),
            P("tp", "fsdp"),
            P(),
            P("fsdp", "tp"),
            P(),
            P("tp", "fsdp"),
            P(),
        ),
        check_vma=False,
    )
```

```python
from functools import partial
import math

import jax
import jax.numpy as jnp
from jax import lax
from jax.experimental import pallas as pl
from jax.experimental.pallas import tpu as pltpu
from jax.sharding import PartitionSpec as P

HD = 64
ROT = 16
EPS = 1e-05
MASKED = 1e30
F32 = jnp.float32
BF16 = jnp.bfloat16
VMEM_BYTES = 56 * 1024 * 1024
NT = (((1,), (1,)), ((), ()))
TN = (((0,), (0,)), ((), ()))
NN = (((1,), (0,)), ((), ()))

dot32 = partial(lax.dot_general, preferred_element_type=F32)


def whole_spec(value):
    return pl.BlockSpec(value.shape, lambda *_: (0,) * value.ndim)


def place_rows(piece, key, place_ref, whole):
    rows = piece.shape[0]
    if rows == whole.shape[0]:
        return slice(None)
    return pl.ds(pl.multiple_of((place_ref[0] ^ key) * rows, rows), rows)


def prepare_kernel(x_own, x_other, dy_own, dy_other, gain_ref, an_ref, mn_ref, dy_ref):
    step = pl.program_id(0)
    half = pl.num_programs(0) // 2

    def work(x_ref, grad_ref):
        xhat, _ = row_norm(x_ref[...].astype(F32))
        an = (xhat * gain_ref[0:1, :] + gain_ref[1:2, :]).astype(BF16)
        mn = (xhat * gain_ref[2:3, :] + gain_ref[3:4, :]).astype(BF16)
        dy = grad_ref[...]
        an_ref[...], mn_ref[...], dy_ref[...] = an, mn, dy

    @pl.when(step < half)
    def _():
        work(x_own, dy_own)

    @pl.when(step >= half)
    def _():
        work(x_other, dy_other)


def prepare(x_own, x_other, dy_own, dy_other, gains):
    rows, depth = x_own.shape
    br = min(512, rows)
    half = rows // br
    own = pl.BlockSpec((br, depth), lambda i: (jnp.minimum(i, half - 1), 0))
    other = pl.BlockSpec((br, depth), lambda i: (jnp.maximum(i - half, 0), 0))
    tall = pl.BlockSpec((br, depth), lambda i: (i, 0))
    return pl.pallas_call(
        prepare_kernel,
        grid=(2 * half,),
        in_specs=[own, other, own, other, whole_spec(gains)],
        out_specs=[tall] * 3,
        out_shape=[jax.ShapeDtypeStruct((2 * rows, depth), BF16)] * 3,
        compiler_params=pltpu.CompilerParams(vmem_limit_bytes=VMEM_BYTES),
        cost_estimate=pl.CostEstimate(
            flops=40 * rows * depth, bytes_accessed=32 * rows * depth, transcendentals=2 * rows
        ),
        name="prepare",
    )(x_own, x_other, dy_own, dy_other, gains)


def attention_kernel(place_ref, an_ref, dy_ref, bias_ref, turn_ref, mark_ref, *refs, keys, bq):
    length = an_ref.shape[0]
    width = 2 * HD
    piece_refs, refs = refs[: len(keys)], refs[len(keys) :]
    att_ref, dmix_ref, sum_ref, qkv_ref, out_ref, mixed_scr, do_scr, dk_scr, dv_scr = refs
    count = mixed_scr.shape[0]
    seq, pair = pl.program_id(0), pl.program_id(1)

    @pl.when((seq == 0) & (pair == 0))
    def _():
        for ref, (key, parts) in zip(piece_refs, keys):
            into = place_rows(ref, key, place_ref, qkv_ref)
            for j, lead in parts:
                qkv_ref[into, j * 3 * width : (j + 1) * 3 * width] = ref[:, lead : lead + 3 * width]
                out_ref[into, j * width : (j + 1) * width] = ref[:, lead + 3 * width : lead + 4 * width]

    @pl.when(pair == 0)
    def _():
        step = min(256, length)
        for r in range(0, length, step):
            mixed = dot32(an_ref[r : r + step, :], qkv_ref[...], NN) + bias_ref[...]
            do = dot32(dy_ref[r : r + step, :], out_ref[...], NN).astype(BF16)
            for j in range(count):
                mixed_scr[j, r : r + step, :] = mixed[:, j * 3 * width : (j + 1) * 3 * width]
                do_scr[j, r : r + step, :] = do[:, j * width : (j + 1) * width]

    mixed = mixed_scr.at[pair]
    scale = 1.0 / math.sqrt(HD)
    half = ROT // 2
    lane = lax.broadcasted_iota(jnp.int32, (length, width), 1)
    dim = lane % HD
    table = turn_ref[...]
    cos = jnp.where(dim < half, table, jnp.where(dim < ROT, pltpu.roll(table, half, 1), 1.0))
    sa = jnp.where(dim < half, -pltpu.roll(table, width - half, 1), 0.0)
    sb = jnp.where((dim >= half) & (dim < ROT), table, 0.0)

    def turn(v, c, a, b, sign):
        side = pltpu.roll(v, width - half, 1) * a + pltpu.roll(v, half, 1) * b
        return v * c + side if sign > 0 else v * c - side

    q = turn(mixed[:, 0:width], cos, sa, sb, 1).astype(BF16)
    k = turn(mixed[:, width : 2 * width], cos, sa, sb, 1).astype(BF16)
    v = mixed[:, 2 * width : 3 * width].astype(BF16)
    do = do_scr[pair]
    zero = jnp.zeros((), BF16)
    qs = (q.astype(F32) * scale).astype(BF16)
    qf = jnp.where((mark_ref[...].astype(F32) > 0.5) | (lane >= 8), 0.0, -MASKED).astype(BF16)
    kaug = jnp.concatenate([k, mark_ref[...]], axis=1)
    heads = []
    for h in range(2):
        m = (lane // HD) == h
        qm = jnp.where(m, qs, zero)
        heads.append(
            (
                jnp.concatenate([qm, qf], axis=1),
                qm,
                jnp.where(m, k, zero),
                jnp.where(m, v, zero),
                jnp.where(m, do, zero),
            )
        )
    causal = lax.broadcasted_iota(jnp.int32, (bq, bq), 1) <= lax.broadcasted_iota(jnp.int32, (bq, bq), 0)
    blocks = length // bq
    for i in range(blocks):
        r0 = i * bq
        w = r0 + bq
        att = dq = dkp = dvp = 0.0
        staged = []
        for qaug, qm, km, vm, dom in heads:
            s = dot32(qaug[r0:w], kaug[:w], NT)
            diagonal = jnp.where(causal, s[:, r0:], -MASKED)
            s = diagonal if i == 0 else jnp.concatenate([s[:, :r0], diagonal], axis=1)
            staged.append((s, dot32(dom[r0:w], v[:w], NT)))
        for (s, dp), (qaug, qm, km, vm, dom) in zip(staged, heads):
            e = jnp.exp(s - jnp.max(s, axis=1, keepdims=True))
            p = e * (1.0 / jnp.sum(e, axis=1, keepdims=True))
            pb = p.astype(BF16)
            o = dot32(pb, vm[:w], NN)
            delta = jnp.sum(o * dom[r0:w].astype(F32), axis=1, keepdims=True)
            ds = (p * (dp - delta)).astype(BF16)
            att, dq = att + o, dq + dot32(ds, km[:w], NN)
            dvp, dkp = dvp + dot32(pb, dom[r0:w], TN), dkp + dot32(ds, qm[r0:w], TN)
        att_ref[r0:w, :] = att.astype(BF16)
        dmix_ref[r0:w, 0:width] = turn(dq * scale, cos[r0:w], sa[r0:w], sb[r0:w], -1).astype(BF16)
        if i > 0:
            dk_scr[:r0] += dkp[:r0]
            dv_scr[:r0] += dvp[:r0]
        dk_scr[r0:w] = dkp[r0:]
        dv_scr[r0:w] = dvp[r0:]
    dmix_ref[:, width : 2 * width] = turn(dk_scr[...], cos, sa, sb, -1).astype(BF16)
    dmix_ref[:, 2 * width : 3 * width] = dv_scr[...].astype(BF16)
    part = jnp.sum(dmix_ref[...].astype(F32), axis=0, keepdims=True)

    @pl.when(seq == 0)
    def _():
        sum_ref[pair] = part

    @pl.when(seq > 0)
    def _():
        sum_ref[pair] += part


def attention(pieces, place, an, dy, bias, tables, length):
    rows, depth = an.shape
    width = 2 * HD
    seqs = rows // length
    count = bias.shape[1] // (3 * width)
    row = pl.BlockSpec((length, depth), lambda s, j, p: (s, 0))
    table = pl.BlockSpec((length, width), lambda s, j, p: (s, 0))
    arrays = [v[0] for v in pieces]
    units = seqs * count
    shapes = [
        jax.ShapeDtypeStruct((rows, count * width), BF16),
        jax.ShapeDtypeStruct((rows, count * 3 * width), BF16),
        jax.ShapeDtypeStruct((count, 1, 3 * width), F32),
        jax.ShapeDtypeStruct((depth, count * 3 * width), BF16),
        jax.ShapeDtypeStruct((depth, count * width), BF16),
    ]
    return pl.pallas_call(
        partial(attention_kernel, keys=[v[1:] for v in pieces], bq=min(512, length)),
        grid_spec=pltpu.PrefetchScalarGridSpec(
            num_scalar_prefetch=1,
            grid=(seqs, count),
            in_specs=[row, row, whole_spec(bias), table, table] + [whole_spec(v) for v in arrays],
            out_specs=[
                pl.BlockSpec((length, width), lambda s, j, p: (s, j)),
                pl.BlockSpec((length, 3 * width), lambda s, j, p: (s, j)),
            ]
            + [whole_spec(v) for v in shapes[2:]],
            scratch_shapes=[
                pltpu.VMEM((count, length, 3 * width), F32),
                pltpu.VMEM((count, length, width), BF16),
                pltpu.VMEM((length, width), F32),
                pltpu.VMEM((length, width), F32),
            ],
        ),
        out_shape=shapes,
        compiler_params=pltpu.CompilerParams(vmem_limit_bytes=VMEM_BYTES),
        cost_estimate=pl.CostEstimate(
            flops=units * (32 * length * length * width + 8 * length * depth * width),
            bytes_accessed=units * length * (depth * 4 + width * 40),
            transcendentals=units * 2 * length * length,
        ),
        name="attention",
    )(place, an, dy, bias, *tables, *arrays)


def mlp_kernel(place_ref, mn_ref, dy_ref, bias_ref, *refs, keys, count):
    piece_refs, refs = refs[: len(keys)], refs[len(keys) :]
    act_ref, dgate_ref, sum_ref, up_ref, down_ref = refs
    units = up_ref.shape[1] // count
    step = pl.program_id(0)

    @pl.when(step == 0)
    def _():
        sum_ref[...] = jnp.zeros_like(sum_ref)
        for ref, (key, parts) in zip(piece_refs, keys):
            into = place_rows(ref, key, place_ref, up_ref)
            for j, lead in parts:
                up_ref[into, j * units : (j + 1) * units] = ref[:, lead : lead + units]
                down_ref[into, j * units : (j + 1) * units] = ref[:, lead + units : lead + 2 * units]

    for c in range(0, up_ref.shape[1], units):
        col = slice(c, c + units)
        gate = dot32(mn_ref[...], up_ref[:, col], NN) + bias_ref[:, col]
        dact = dot32(dy_ref[...], down_ref[:, col], NN)
        cdf = 0.5 + 0.5 * lax.erf(gate * math.sqrt(0.5))
        pdf = jnp.exp(gate * gate * -0.5) * (1.0 / math.sqrt(2.0 * math.pi))
        act_ref[:, col] = (gate * cdf).astype(BF16)
        dgate = (dact * (cdf + gate * pdf)).astype(BF16)
        dgate_ref[:, col] = dgate
        sum_ref[:, col] += jnp.sum(dgate.astype(F32), axis=0, keepdims=True)


def mlp(pieces, place, mn, dy, bias, count):
    rows, depth = mn.shape
    units = bias.shape[1]
    br = min(512, rows)
    row = pl.BlockSpec((br, depth), lambda r, p: (r, 0))
    tile = pl.BlockSpec((br, units), lambda r, p: (r, 0))
    arrays = [v[0] for v in pieces]
    shapes = [
        jax.ShapeDtypeStruct((rows, units), BF16),
        jax.ShapeDtypeStruct((rows, units), BF16),
        jax.ShapeDtypeStruct((1, units), F32),
        jax.ShapeDtypeStruct((depth, units), BF16),
        jax.ShapeDtypeStruct((depth, units), BF16),
    ]
    return pl.pallas_call(
        partial(mlp_kernel, keys=[v[1:] for v in pieces], count=count),
        grid_spec=pltpu.PrefetchScalarGridSpec(
            num_scalar_prefetch=1,
            grid=(rows // br,),
            in_specs=[row, row, whole_spec(bias)] + [whole_spec(v) for v in arrays],
            out_specs=[tile, tile] + [whole_spec(v) for v in shapes[2:]],
        ),
        out_shape=shapes,
        compiler_params=pltpu.CompilerParams(vmem_limit_bytes=VMEM_BYTES),
        cost_estimate=pl.CostEstimate(
            flops=4 * rows * depth * units,
            bytes_accessed=rows * depth * 4 + units * depth * 8 + rows * units * 4,
            transcendentals=2 * rows * units,
        ),
        name="mlp",
    )(place, mn, dy, bias, *arrays)


def block_shapes(places, depth, wa, wb, count):
    if places != 4:
        return (0,), [jax.ShapeDtypeStruct((depth, wa + wb), BF16)]
    far = jax.ShapeDtypeStruct((depth // 4, (wa + wb) // count), BF16)
    near = jax.ShapeDtypeStruct((depth // 4, wa + wb), BF16)
    return (3, 1, 2, 0), [far] * count + [near] * 3


def put_blocks(outs, sum_a, sum_b, place_ref, count, keys):
    wa, wb = sum_a.shape[1] // count, sum_b.shape[1] // count
    width = wa + wb
    for j in range(count):
        for n, key in enumerate(keys):
            out = outs[j] if key == 3 else outs[n + count - 1 if len(keys) > 1 else 0]
            at = place_rows(out, key, place_ref, sum_a)
            first = 0 if key == 3 else j * width
            out[:, first : first + wa] = sum_a[at, j * wa : (j + 1) * wa].astype(BF16)
            out[:, first + wa : first + width] = sum_b[at, j * wb : (j + 1) * wb].astype(BF16)


def grads_kernel(place_ref, left_a, left_b, right_a, right_b, *refs, count, keys):
    outs, (sum_a, sum_b) = refs[:-2], refs[-2:]
    step = pl.program_id(0)

    @pl.when(step == 0)
    def _():
        sum_a[...] = dot32(left_a[...], right_a[...], TN)
        sum_b[...] = dot32(left_b[...], right_b[...], TN)

    @pl.when(step > 0)
    def _():
        sum_a[...] += dot32(left_a[...], right_a[...], TN)
        sum_b[...] += dot32(left_b[...], right_b[...], TN)

    @pl.when(step == pl.num_programs(0) - 1)
    def _():
        put_blocks(outs, sum_a, sum_b, place_ref, count, keys)


def weight_grads(place, places, left_a, right_a, left_b, right_b, count):
    rows, depth = left_a.shape
    br = min(512, rows)
    wa, wb = right_a.shape[1], right_b.shape[1]
    block = lambda v: pl.BlockSpec((br, v.shape[1]), lambda i, p: (i, 0))
    keys, shapes = block_shapes(places, depth, wa, wb, count)
    found = pl.pallas_call(
        partial(grads_kernel, count=count, keys=keys),
        grid_spec=pltpu.PrefetchScalarGridSpec(
            num_scalar_prefetch=1,
            grid=(rows // br,),
            in_specs=[block(v) for v in (left_a, left_b, right_a, right_b)],
            out_specs=[whole_spec(v) for v in shapes],
            scratch_shapes=[pltpu.VMEM((depth, wa), F32), pltpu.VMEM((depth, wb), F32)],
        ),
        out_shape=shapes,
        compiler_params=pltpu.CompilerParams(vmem_limit_bytes=VMEM_BYTES),
        cost_estimate=pl.CostEstimate(
            flops=2 * rows * depth * (wa + wb),
            bytes_accessed=4 * rows * depth + 2 * (wa + wb) * (rows + depth),
            transcendentals=0,
        ),
        name="weight_grads",
    )(place, left_a, left_b, right_a, right_b)
    return found


def row_norm(x):
    centre = x - jnp.mean(x, axis=-1, keepdims=True)
    rstd = lax.rsqrt(jnp.mean(centre * centre, axis=-1, keepdims=True) + EPS)
    return centre * rstd, rstd


def pull_kernel(*refs):
    dg0, up0, dg1, up1, dm0, qkv0, dm1, qkv1, x_ref, gain_ref = refs[:10]
    out_ref, sum_ref = refs[-2:]
    n_mlp = dot32(dg0[...], up0[...], NT) + dot32(dg1[...], up1[...], NT)
    n_attn = dot32(dm0[...], qkv0[...], NT) + dot32(dm1[...], qkv1[...], NT)
    xhat, rstd = row_norm(x_ref[...].astype(F32))
    u = n_attn * gain_ref[0:1, :] + n_mlp * gain_ref[2:3, :]
    parts = [jnp.sum(v, axis=0, keepdims=True) for v in (n_attn * xhat, n_attn, n_mlp * xhat, n_mlp)]
    part = jnp.concatenate(parts + [jnp.zeros((4, u.shape[1]), F32)], axis=0)

    @pl.when(pl.program_id(0) == 0)
    def _():
        sum_ref[...] = part

    @pl.when(pl.program_id(0) > 0)
    def _():
        sum_ref[...] += part

    out_ref[...] = u.astype(out_ref.dtype)


def pull_back(terms, x, gains, first_row, dtype):
    rows, depth = x.shape
    br = min(256, rows)
    first = first_row // br
    block = lambda v: pl.BlockSpec((br, v.shape[1]), lambda i: (i + first, 0))
    specs, args = [], []
    for grad, weight in terms:
        specs += [block(grad), whole_spec(weight)]
        args += [grad, weight]
    tile = pl.BlockSpec((br, depth), lambda i: (i, 0))
    width = sum(grad.shape[1] for grad, _ in terms)
    return pl.pallas_call(
        pull_kernel,
        grid=(rows // br,),
        in_specs=specs + [tile, whole_spec(gains)],
        out_specs=[tile, pl.BlockSpec((8, depth), lambda i: (0, 0))],
        out_shape=[jax.ShapeDtypeStruct((rows, depth), dtype), jax.ShapeDtypeStruct((8, depth), F32)],
        compiler_params=pltpu.CompilerParams(vmem_limit_bytes=VMEM_BYTES),
        cost_estimate=pl.CostEstimate(
            flops=2 * rows * width * depth,
            bytes_accessed=2 * width * (rows + depth) + rows * depth * 8,
            transcendentals=rows,
        ),
        name="pull_back",
    )(*args, x, gains)


def out_kernel(*refs, own):
    att0, out0, att1, out1, act0, down0, act1, down1 = refs[:8]
    y = dot32(act0[...], down0[...], NT) + dot32(act1[...], down1[...], NT)
    y = y + dot32(att0[...], out0[...], NT) + dot32(att1[...], out1[...], NT)
    if not own:
        refs[-1][...] = y.astype(BF16)
        return
    x_ref, other_ref, bias_ref, dy_ref, pull_ref, other_pull_ref, y_ref, grad_ref = refs[8:]
    x = x_ref[...].astype(F32)
    y_ref[...] = (y + x + other_ref[...].astype(F32) + bias_ref[...]).astype(BF16)
    xhat, rstd = row_norm(x)
    u = pull_ref[...] + other_pull_ref[...].astype(F32)
    u = u - jnp.mean(u, axis=-1, keepdims=True) - xhat * jnp.mean(u * xhat, axis=-1, keepdims=True)
    grad_ref[...] = dy_ref[...].astype(F32) + rstd * u


def branch_out(terms, rows, last=None):
    own = last is not None
    depth = terms[0][1].shape[0]
    br = min(256, rows)
    first = 0 if own else rows // br
    tile = pl.BlockSpec((br, depth), lambda i: (i, 0))
    specs, args = [], []
    for value, weight in terms:
        specs += [pl.BlockSpec((br, value.shape[1]), lambda i: (i + first, 0)), whole_spec(weight)]
        args += [value, weight]
    if own:
        specs += [whole_spec(v) if v.shape[0] == 1 else tile for v in last]
        args += last
    width = sum(value.shape[1] for value, _ in terms)
    shapes = [jax.ShapeDtypeStruct((rows, depth), BF16)] + [jax.ShapeDtypeStruct((rows, depth), F32)] * own
    return pl.pallas_call(
        partial(out_kernel, own=own),
        grid=(rows // br,),
        in_specs=specs,
        out_specs=[tile] * len(shapes),
        out_shape=shapes,
        compiler_params=pltpu.CompilerParams(vmem_limit_bytes=VMEM_BYTES),
        cost_estimate=pl.CostEstimate(
            flops=2 * rows * width * depth,
            bytes_accessed=2 * width * (rows + depth) + rows * depth * (18 if own else 2),
            transcendentals=0,
        ),
        name="branch_out",
    )(*args)


class Links:
    def __init__(self):
        self.fsdp = lax.axis_size("fsdp")
        self.tp = lax.axis_size("tp")
        index = lax.axis_index("fsdp")
        self.core = index % 2
        self.place = index // 2
        self.lane = lax.axis_index("tp")
        self.places = self.fsdp // 2
        self.cores = [list(range(c, self.fsdp, 2)) for c in range(2)]
        self.bits = [1 << b for b in range((self.places - 1).bit_length())]

    def swap(self, value):
        return lax.ppermute(value, "fsdp", [(i, i ^ 1) for i in range(self.fsdp)])

    def hop(self, value, bit):
        return lax.ppermute(value, "fsdp", [(i, i ^ (2 * bit)) for i in range(self.fsdp)])

    def ring(self, value):
        return lax.ppermute(value, "tp", [(i, (i + 1) % self.tp) for i in range(self.tp)])


    def near_places(self, piece):
        return self.hop(piece, 1), self.hop(piece, 2)

    def far_parts(self, near):
        cut = near[0].shape[1] // 2
        return near[1][:, :cut], near[0][:, cut:]

    def far_place(self, parts):
        return self.hop(parts[0], 1), self.hop(parts[1], 2)

    def scatter_far(self, far):
        return self.hop(far[0], 2), self.hop(far[1], 1)

    def add_far(self, one, two, far):
        cut = one.shape[1] // 2
        first = (one[:, :cut].astype(F32) + far[0].astype(F32)).astype(BF16)
        second = (two[:, cut:].astype(F32) + far[1].astype(F32)).astype(BF16)
        return lax.dynamic_update_slice(one, first, (0, 0)), lax.dynamic_update_slice(two, second, (0, cut))

    def scatter_near(self, one, two):
        return self.hop(one, 1), self.hop(two, 2)

    def gather_other(self, piece):
        return lax.all_gather(piece, "fsdp", axis=0, tiled=True, axis_index_groups=self.cores)

    def scatter_other(self, value):
        return lax.psum_scatter(
            value, "fsdp", scatter_dimension=0, tiled=True, axis_index_groups=self.cores
        )

    def back(self, value):
        return lax.ppermute(value, "tp", [(i, (i - 1) % self.tp) for i in range(self.tp)])

    def across(self, value):
        return lax.ppermute(value, "tp", [(i, (i + 2) % self.tp) for i in range(self.tp)])

    def ring_sum(self, total, terms):
        for term in terms:
            total = term if total is None else total + term
            total = self.ring(total.astype(BF16)).astype(F32)
        return total

    def sum_steps(self):
        steps = [("fsdp", self.fsdp, 1 << b) for b in range((self.fsdp - 1).bit_length())]
        return steps + [("tp", self.tp, 1 << b) for b in range((self.tp - 1).bit_length())]

    def sum_step(self, value, step):
        name, size, bit = step
        return value + lax.ppermute(value, name, [(i, i ^ bit) for i in range(size)])


def pick(value, index, axis):
    return lax.dynamic_index_in_dim(value, index, axis, keepdims=False)


def pair_rows(links, mine, other):
    got = links.swap(other)
    first = jnp.where(links.core == 0, mine, got)
    second = jnp.where(links.core == 0, got, mine)
    return jnp.concatenate([first, second], axis=0)


def unpair_rows(links, block):
    half = block.shape[0] // 2
    mine = lax.dynamic_slice_in_dim(block, links.core * half, half, 0)
    got = links.swap(lax.dynamic_slice_in_dim(block, (1 - links.core) * half, half, 0))
    return jnp.where(links.core == 0, mine, got), jnp.where(links.core == 0, got, mine)


sync = lax.optimization_barrier


def tables_of(segment_rows):
    length = segment_rows.shape[1]
    starts = jnp.sum((segment_rows[:, None, :] < segment_rows[:, :, None]).astype(jnp.int32), axis=-1)
    places = (jnp.arange(length, dtype=jnp.int32)[None] - starts).reshape(-1).astype(F32)
    inverse_freq = jnp.power(10000.0, -jnp.arange(0, ROT, 2, dtype=F32) / ROT)
    angles = inverse_freq[:, None] * places[None, :]
    turns = jnp.concatenate([jnp.cos(angles), jnp.sin(angles)], axis=0)
    marks = segment_rows.reshape(-1, 1) == jnp.arange(2 * HD, dtype=jnp.int32)[None, :]
    return jnp.tile(turns.T, (1, 2 * HD // ROT)), marks.astype(BF16)


def body(
    tokens,
    segments,
    attn_gain,
    attn_shift,
    mlp_gain,
    mlp_shift,
    qkv_weight,
    qkv_bias,
    out_weight,
    out_bias,
    up_weight,
    up_bias,
    down_weight,
    down_bias,
    cotangent,
):
    links = Links()
    tp = links.tp
    rows, depth = tokens.shape
    length = segments.shape[1]
    head_cols = qkv_weight.shape[2] // 2
    unit_cols = up_weight.shape[1] // 2

    def halves(shard, axis):
        size = shard.shape[axis] // 2
        return [lax.dynamic_slice_in_dim(shard, c * size, size, axis) for c in (links.core, 1 - links.core)]

    qkv_halves = [v.reshape(v.shape[0], -1) for v in halves(qkv_weight, 2)]
    out_halves = [v.T for v in halves(out_weight, 0)]
    up_halves = halves(up_weight, 1)
    down_halves = [v.T for v in halves(down_weight, 0)]
    attn_slots = [pair_rows(links, *[jnp.concatenate(v, axis=1) for v in zip(qkv_halves, out_halves)])]
    mlp_slots = [pair_rows(links, *[jnp.concatenate(v, axis=1) for v in zip(up_halves, down_halves)])]
    qkv_cols = 3 * head_cols

    half = tp // 2
    per = max(1, 2 * HD // head_cols)

    by_hops = links.places == 4 and per == 1 and tp == 4
    place = jnp.full((1,), links.place if by_hops else 0, jnp.int32)

    def join_pair(slots):
        if per == 1:
            return slots[0]
        lead = slots[0].shape[0]
        return jnp.concatenate([v.reshape(lead, 4, head_cols) for v in slots], axis=2).reshape(lead, -1)

    def join_qkv(slots):
        if per == 1:
            return slots[0]
        lead = slots[0].shape[0]
        return jnp.concatenate([v.reshape(lead, 3, head_cols) for v in slots], axis=2).reshape(lead, -1)

    def split_pair(value, parts):
        if per == 1:
            return [value]
        lead = value.shape[0]
        blocks = value.reshape(lead, parts, per, head_cols)
        return [blocks[:, :, j].reshape(lead, -1) for j in range(per)]

    groups = [list(range(0, half)), list(range(half, tp))]
    mlp_groups = [[1, 3], [0, 2]] if by_hops else groups

    lane_of = [(links.lane - s) % tp for s in range(tp)]
    qkv_bias_lanes = pick(qkv_bias.reshape(3, tp, 2, head_cols), links.core, 2)
    up_bias_lanes = pick(up_bias.reshape(tp, 2, unit_cols), links.core, 1)
    qkv_bias_groups = [
        jnp.concatenate(
            [
                join_qkv([pick(qkv_bias_lanes, lane_of[s], 1).reshape(1, -1) for s in g[i : i + per]])
                for i in range(0, half, per)
            ],
            axis=1,
        ).astype(F32)
        for g in groups
    ]
    up_bias_groups = [
        jnp.concatenate([pick(up_bias_lanes, lane_of[s], 0) for s in g]).astype(F32)[None] for g in mlp_groups
    ]

    gains = jnp.stack([v.astype(F32) for v in (attn_gain, attn_shift, mlp_gain, mlp_shift)])
    x_other, dy_other = links.swap(tokens), links.swap(cotangent)

    def group_piece(slots):
        return jnp.concatenate(slots, axis=1)

    def near(piece):
        return links.near_places(piece) if by_hops else links.gather_other(piece)

    def far_parts(got):
        return links.far_parts(got) if by_hops else ()

    def far(parts):
        return links.far_place(parts) if by_hops else ()

    def pieces_of(piece, got, last, width):
        both = tuple((j, j * width) for j in range(half))
        if not by_hops:
            return [(got, 0, both)]
        return [(piece, 0, both), (got[0], 1, both), (got[1], 2, both), (last[0], 3, ((0, 0),)), (last[1], 3, ((1, 0),))]

    def attention_part(g, pieces, an, dy):
        if per > 1:
            slots = jnp.split(pieces[0][0], half, axis=1)
            whole = jnp.concatenate([join_pair(slots[i : i + per]) for i in range(0, half, per)], axis=1)
            pieces = [(whole, 0, tuple((j, j * 8 * HD) for j in range(half // per)))]
        return attention(pieces, place, an, dy, qkv_bias_groups[g], tables, length)

    def attention_grads(attended, dmixed):
        found = weight_grads(place, links.places if by_hops else 1, an, dmixed, dy2, attended, half // per)
        if per == 1:
            return found
        pairs = jnp.split(found[0], half // per, axis=1)
        return [jnp.concatenate([v for pair in pairs for v in split_pair(pair, 4)], axis=1)]

    def mlp_part(g, pieces, mn, dy):
        return mlp(pieces, place, mn, dy, up_bias_groups[g], half)

    def mlp_grads(active, dgate):
        return weight_grads(place, links.places if by_hops else 1, mn, dgate, dy2, active, half)

    def sum_far(blocks):
        return links.scatter_far(blocks[:2]) if by_hops else links.scatter_other(blocks[0])

    def add_far(blocks, got):
        return links.add_far(blocks[2], blocks[3], got) if by_hops else got

    def sum_near(sent):
        return links.scatter_near(*sent) if by_hops else sent

    def place_sum(blocks, got):
        if by_hops:
            got = blocks[4].astype(F32) + got[0].astype(F32) + got[1].astype(F32)
        return jnp.split(got.astype(F32), half, axis=1)

    def small_sums():
        def spread(values):
            lead, cols = values[0].shape
            full = jnp.zeros((lead, tp, 2, cols), F32)
            for s, value in enumerate(values):
                full = lax.dynamic_update_slice(full, value.reshape(lead, 1, 1, cols), (0, lane_of[s], links.core, 0))
            return full.reshape(-1)

        pair_sums = [v[i] for v in (qkv_sum0, qkv_sum1) for i in range(half // per)]
        qkv_bias_part = spread([v.reshape(3, head_cols) for d in pair_sums for v in split_pair(d, 3)])
        gate_sums = [v for part in (gate_sum0, gate_sum1) for v in jnp.split(part, half, axis=1)]
        order = mlp_groups[0] + mlp_groups[1]
        up_bias_part = spread([gate_sums[order.index(s)] for s in range(tp)])
        bias_part = jnp.sum(cotangent.astype(F32), axis=0)
        pieces = [
            *(sums_own + sums_other)[:4],
            qkv_bias_part,
            bias_part,
            up_bias_part,
        ]
        return jnp.concatenate(pieces).reshape(-1, 128)

    sizes = [depth] * 4 + [qkv_bias.size, depth, up_bias.size]

    attn_cols, mlp_cols = 4 * head_cols, 2 * unit_cols
    ring, back = links.ring, links.back
    own_segments = lax.dynamic_slice_in_dim(segments, links.lane * rows // length, rows // length, 0)
    pair_segments = jnp.concatenate([own_segments, links.swap(own_segments)], axis=0)
    attn_slots, pair_segments = sync((attn_slots, pair_segments))
    if by_hops:
        attn = {0: attn_slots[0], 1: ring(attn_slots[0])}
        units = {0: mlp_slots[0]}
        got = [links.near_places(attn[0])]
        attn, units, pair_segments = sync((attn, units, pair_segments))
        got.append(links.near_places(attn[1]))
        units[1], units[3] = ring(units[0]), back(units[0])
        tables = tables_of(pair_segments)
        got, x_other, dy_other = sync((got, x_other, dy_other))
        last = [links.hop(got[0][1], 1), links.hop(got[1][0], 2)]
        normed = prepare(tokens, x_other, cotangent, dy_other, gains)
        units, last, normed, tables = sync((units, last, normed, tables))
        piece_b = group_piece([units[1], units[3]])
        piece_b, normed = sync((piece_b, normed))
        group_a = [
            (v, key, ((j, 0),))
            for j in (0, 1)
            for v, key in ((attn[j], 0), (got[j][0], 1), (got[j][1], 2), (last[j], 3))
        ]
    else:
        attn, units = {0: attn_slots[0]}, {0: mlp_slots[0]}
        for s in range(1, tp):
            attn[s] = ring(attn[s - 1])
            units[s] = ring(units[s - 1])
        tables = tables_of(pair_segments)
        normed = prepare(tokens, x_other, cotangent, dy_other, gains)
        group_a = pieces_of(None, near(group_piece([attn[s] for s in groups[0]])), None, attn_cols)
    an, mn, dy2 = normed
    if not by_hops:
        piece_b, piece_c, piece_d = [
            group_piece([v[s] for s in g]) for v, g in ((units, groups[0]), (units, groups[1]), (attn, groups[1]))
        ]
    piece_b, an = sync((piece_b, an))

    near_b = near(piece_b)
    if by_hops:
        units[2] = ring(units[1])
    att0, dmix0, qkv_sum0, qkv0, out0 = attention_part(0, group_a, an, dy2)
    near_b, attn, units, att0 = sync((near_b, attn, units, att0))
    parts_b = far_parts(near_b)
    if by_hops:
        piece_c = group_piece([units[0], units[2]])
    parts_b, piece_c, att0 = sync((parts_b, piece_c, att0))

    far_b = far(parts_b)
    if by_hops:
        attn[2], attn[3] = ring(attn[1]), back(attn[0])
    grad_a = attention_grads(att0, dmix0)
    far_b, grad_a, mn = sync((far_b, grad_a, mn))

    near_c = near(piece_c)
    act0, dgate0, gate_sum0, up0, down0 = mlp_part(0, pieces_of(piece_b, near_b, far_b, mlp_cols), mn, dy2)
    near_c, attn, act0 = sync((near_c, attn, act0))
    parts_c = far_parts(near_c)
    parts_c, act0 = sync((parts_c, act0))

    far_c = far(parts_c)
    back_a = sum_far(grad_a)
    grad_b = mlp_grads(act0, dgate0)
    far_c, back_a, grad_b, mn = sync((far_c, back_a, grad_b, mn))
    if by_hops:
        piece_d = group_piece([attn[2], attn[3]])
    sent_a = add_far(grad_a, back_a)
    piece_d, sent_a, mn = sync((piece_d, sent_a, mn))

    near_d = near(piece_d)
    near_a = sum_near(sent_a)
    act1, dgate1, gate_sum1, up1, down1 = mlp_part(1, pieces_of(piece_c, near_c, far_c, mlp_cols), mn, dy2)
    near_d, near_a, act1 = sync((near_d, near_a, act1))
    parts_d = far_parts(near_d)
    parts_d, act1 = sync((parts_d, act1))

    far_d = far(parts_d)
    back_b = sum_far(grad_b)
    grad_c = mlp_grads(act1, dgate1)
    far_d, back_b, grad_c, an = sync((far_d, back_b, grad_c, an))
    sent_b = add_far(grad_b, back_b)
    sum_a = place_sum(grad_a, near_a)
    sent_b, sum_a, grad_c, an = sync((sent_b, sum_a, grad_c, an))

    back_near_b = sum_near(sent_b)
    back_c = sum_far(grad_c)
    att1, dmix1, qkv_sum1, qkv1, out1 = attention_part(1, pieces_of(piece_d, near_d, far_d, attn_cols), an, dy2)
    back_near_b, back_c, att1 = sync((back_near_b, back_c, att1))
    sent_c = add_far(grad_c, back_c)
    sum_b = place_sum(grad_b, back_near_b)
    sent_c, sum_b, att1 = sync((sent_c, sum_b, att1))

    back_near_c = sum_near(sent_c)
    lanes_m = ring(sum_b[1].astype(BF16)) if by_hops else ()
    grad_d = attention_grads(att1, dmix1)
    grad_d, dgate1 = sync((grad_d, dgate1))

    back_d = sum_far(grad_d)
    terms = ((dgate0, up0), (dgate1, up1), (dmix0, qkv0), (dmix1, qkv1))
    sent_pull, sums_other = pull_back(terms, x_other, gains, rows, BF16)
    back_near_c, back_d, lanes_m, sent_pull, att1 = sync((back_near_c, back_d, lanes_m, sent_pull, att1))
    sum_c = place_sum(grad_c, back_near_c)
    last_m = sum_c[1].astype(BF16) if by_hops else ()
    sent_d = add_far(grad_d, back_d)
    sent_d, last_m, sent_pull, att1 = sync((sent_d, last_m, sent_pull, att1))

    back_near_d = sum_near(sent_d)
    last_m = back(last_m) if by_hops else ()
    other_pull = links.swap(sent_pull)
    out_terms = ((att0, out0), (att1, out1), (act0, down0), (act1, down1))
    (sent_out,) = branch_out(out_terms, rows)
    back_near_d, other_pull, last_m, sent_out, dgate1 = sync((back_near_d, other_pull, last_m, sent_out, dgate1))
    sum_d = place_sum(grad_d, back_near_d)
    lanes_a = [v.astype(BF16) for v in sum_d]
    if by_hops:
        last_m = (sum_b[0] + last_m.astype(F32)).astype(BF16)
    lanes_a, last_m, sent_out, dgate1 = sync((lanes_a, last_m, sent_out, dgate1))

    other_out = links.swap(sent_out)
    if by_hops:
        lanes_a = [back(lanes_a[0]), ring(lanes_a[1])]
        last_m = back(last_m)
    terms = ((dgate0, up0), (dgate1, up1), (dmix0, qkv0), (dmix1, qkv1))
    pulled, sums_own = pull_back(terms, tokens, gains, 0, F32)
    lanes_a, last_m, other_out, sums_own, att1 = sync((lanes_a, last_m, other_out, sums_own, att1))
    small = small_sums()
    steps = links.sum_steps()
    if by_hops:
        last_a = (sum_a[1] + lanes_a[0].astype(F32)).astype(BF16)
        sum_m = sum_c[0] + lanes_m.astype(F32) + last_m.astype(F32)
    else:
        last_a = ()
        sum_m = links.ring_sum(None, sum_b[1:] + sum_c) + sum_b[0]
    small, last_a, sum_m, att1 = sync((small, last_a, sum_m, att1))

    if by_hops:
        last_a = back(last_a)
    mlp_own = unpair_rows(links, sum_m)
    small = links.sum_step(small, steps[0])
    end_bias = (out_bias.astype(F32) + down_bias.astype(F32))[None]
    out_terms = ((att0, out0), (att1, out1), (act0, down0), (act1, down1))
    output, input_grad = branch_out(
        out_terms, rows, [tokens, other_out, end_bias, cotangent, pulled, other_pull]
    )
    small, last_a, mlp_own, output, input_grad = sync((small, last_a, mlp_own, output, input_grad))
    if by_hops:
        sum_e = sum_a[0] + lanes_a[1].astype(F32) + last_a.astype(F32)
    else:
        sum_e = links.ring_sum(None, sum_a[1:] + sum_d) + sum_a[0]
    attn_own = unpair_rows(links, sum_e)
    small = links.sum_step(links.sum_step(small, steps[1]), steps[2])
    if tp == 4 and links.fsdp == 8:
        a, b, c = [lax.ppermute(small, "tp", [(i, i ^ bit) for i in range(tp)]) for bit in (1, 2, 3)]
        small = (small + a) + (b + c)
    else:
        for step in steps[3:]:
            small = links.sum_step(small, step)
    up_grad = jnp.concatenate([v[:, :unit_cols] for v in mlp_own], axis=1)
    down_grad = jnp.concatenate([v[:, unit_cols:] for v in mlp_own], axis=1).T
    qkv_grad = jnp.concatenate([v[:, :qkv_cols].reshape(-1, 3, head_cols) for v in attn_own], axis=2)
    out_grad = jnp.concatenate([v[:, qkv_cols:] for v in attn_own], axis=1).T

    summed = small.reshape(-1)
    sums = []
    at = 0
    for size in sizes:
        sums.append(summed[at : at + size])
        at += size
    return (
        output,
        input_grad,
        sums[0],
        sums[1],
        sums[2],
        sums[3],
        qkv_grad,
        sums[4].reshape(qkv_bias.shape),
        out_grad,
        sums[5],
        up_grad,
        sums[6],
        down_grad,
        sums[5],
    )


def solution(mesh):
    placed = (
        P(("fsdp", "tp"), None),
        P("fsdp", None),
        P(),
        P(),
        P(),
        P(),
        P("fsdp", None, "tp"),
        P(),
        P("tp", "fsdp"),
        P(),
        P("fsdp", "tp"),
        P(),
        P("tp", "fsdp"),
        P(),
        P(("fsdp", "tp"), None),
    )
    return jax.shard_map(
        body,
        mesh=mesh,
        in_specs=placed,
        out_specs=(
            P(("fsdp", "tp"), None),
            P(("fsdp", "tp"), None),
            P(),
            P(),
            P(),
            P(),
            P("fsdp", None, "tp"),
            P(),
            P("tp", "fsdp"),
            P(),
            P("fsdp", "tp"),
            P(),
            P("tp", "fsdp"),
            P(),
        ),
        check_vma=False,
    )
```

```python
from functools import partial
import math

import jax
import jax.numpy as jnp
from jax import lax
from jax.experimental import pallas as pl
from jax.experimental.pallas import tpu as pltpu
from jax.sharding import PartitionSpec as P

HD = 64
ROT = 16
EPS = 1e-05
MASKED = 1e30
F32 = jnp.float32
BF16 = jnp.bfloat16
VMEM_BYTES = 56 * 1024 * 1024
NT = (((1,), (1,)), ((), ()))
TN = (((0,), (0,)), ((), ()))
NN = (((1,), (0,)), ((), ()))

dot32 = partial(lax.dot_general, preferred_element_type=F32)


def whole_spec(value):
    return pl.BlockSpec(value.shape, lambda *_: (0,) * value.ndim)


def place_rows(piece, key, place_ref, whole):
    rows = piece.shape[0]
    if rows == whole.shape[0]:
        return slice(None)
    return pl.ds(pl.multiple_of((place_ref[0] ^ key) * rows, rows), rows)


def prepare_kernel(x_own, x_other, dy_own, dy_other, gain_ref, an_ref, mn_ref, dy_ref):
    step = pl.program_id(0)
    half = pl.num_programs(0) // 2

    def work(x_ref, grad_ref):
        xhat, _ = row_norm(x_ref[...].astype(F32))
        an = (xhat * gain_ref[0:1, :] + gain_ref[1:2, :]).astype(BF16)
        mn = (xhat * gain_ref[2:3, :] + gain_ref[3:4, :]).astype(BF16)
        dy = grad_ref[...]
        an_ref[...], mn_ref[...], dy_ref[...] = an, mn, dy

    @pl.when(step < half)
    def _():
        work(x_own, dy_own)

    @pl.when(step >= half)
    def _():
        work(x_other, dy_other)


def prepare(x_own, x_other, dy_own, dy_other, gains):
    rows, depth = x_own.shape
    br = min(1024, rows)
    half = rows // br
    own = pl.BlockSpec((br, depth), lambda i: (jnp.minimum(i, half - 1), 0))
    other = pl.BlockSpec((br, depth), lambda i: (jnp.maximum(i - half, 0), 0))
    tall = pl.BlockSpec((br, depth), lambda i: (i, 0))
    return pl.pallas_call(
        prepare_kernel,
        grid=(2 * half,),
        in_specs=[own, other, own, other, whole_spec(gains)],
        out_specs=[tall] * 3,
        out_shape=[jax.ShapeDtypeStruct((2 * rows, depth), BF16)] * 3,
        compiler_params=pltpu.CompilerParams(vmem_limit_bytes=VMEM_BYTES),
        cost_estimate=pl.CostEstimate(
            flops=40 * rows * depth, bytes_accessed=32 * rows * depth, transcendentals=2 * rows
        ),
        name="prepare",
    )(x_own, x_other, dy_own, dy_other, gains)


def attention_kernel(place_ref, an_ref, dy_ref, bias_ref, turn_ref, mark_ref, *refs, keys, bq):
    length = an_ref.shape[0]
    width = 2 * HD
    piece_refs, refs = refs[: len(keys)], refs[len(keys) :]
    att_ref, dmix_ref, sum_ref, qkv_ref, out_ref, mixed_scr, do_scr, dk_scr, dv_scr = refs
    count = mixed_scr.shape[0]
    seq, pair = pl.program_id(0), pl.program_id(1)

    @pl.when((seq == 0) & (pair == 0))
    def _():
        for ref, (key, parts) in zip(piece_refs, keys):
            into = place_rows(ref, key, place_ref, qkv_ref)
            for j, lead in parts:
                qkv_ref[into, j * 3 * width : (j + 1) * 3 * width] = ref[:, lead : lead + 3 * width]
                out_ref[into, j * width : (j + 1) * width] = ref[:, lead + 3 * width : lead + 4 * width]

    @pl.when(pair == 0)
    def _():
        step = min(256, length)
        for r in range(0, length, step):
            mixed = dot32(an_ref[r : r + step, :], qkv_ref[...], NN) + bias_ref[...]
            do = dot32(dy_ref[r : r + step, :], out_ref[...], NN).astype(BF16)
            for j in range(count):
                mixed_scr[j, r : r + step, :] = mixed[:, j * 3 * width : (j + 1) * 3 * width]
                do_scr[j, r : r + step, :] = do[:, j * width : (j + 1) * width]

    mixed = mixed_scr.at[pair]
    scale = 1.0 / math.sqrt(HD)
    half = ROT // 2
    lane = lax.broadcasted_iota(jnp.int32, (length, width), 1)
    dim = lane % HD
    table = turn_ref[...]
    cos = jnp.where(dim < half, table, jnp.where(dim < ROT, pltpu.roll(table, half, 1), 1.0))
    sa = jnp.where(dim < half, -pltpu.roll(table, width - half, 1), 0.0)
    sb = jnp.where((dim >= half) & (dim < ROT), table, 0.0)

    def turn(v, c, a, b, sign):
        side = pltpu.roll(v, width - half, 1) * a + pltpu.roll(v, half, 1) * b
        return v * c + side if sign > 0 else v * c - side

    q = turn(mixed[:, 0:width], cos, sa, sb, 1).astype(BF16)
    k = turn(mixed[:, width : 2 * width], cos, sa, sb, 1).astype(BF16)
    v = mixed[:, 2 * width : 3 * width].astype(BF16)
    do = do_scr[pair]
    zero = jnp.zeros((), BF16)
    qs = (q.astype(F32) * scale).astype(BF16)
    qf = jnp.where((mark_ref[...].astype(F32) > 0.5) | (lane >= 8), 0.0, -MASKED).astype(BF16)
    kaug = jnp.concatenate([k, mark_ref[...]], axis=1)
    heads = []
    for h in range(2):
        m = (lane // HD) == h
        qm = jnp.where(m, qs, zero)
        heads.append(
            (
                jnp.concatenate([qm, qf], axis=1),
                qm,
                jnp.where(m, k, zero),
                jnp.where(m, v, zero),
                jnp.where(m, do, zero),
            )
        )
    causal = lax.broadcasted_iota(jnp.int32, (bq, bq), 1) <= lax.broadcasted_iota(jnp.int32, (bq, bq), 0)
    blocks = length // bq
    for i in range(blocks):
        r0 = i * bq
        w = r0 + bq
        att = dq = dkp = dvp = 0.0
        staged = []
        for qaug, qm, km, vm, dom in heads:
            s = dot32(qaug[r0:w], kaug[:w], NT)
            diagonal = jnp.where(causal, s[:, r0:], -MASKED)
            s = diagonal if i == 0 else jnp.concatenate([s[:, :r0], diagonal], axis=1)
            staged.append((s, dot32(dom[r0:w], v[:w], NT)))
        for (s, dp), (qaug, qm, km, vm, dom) in zip(staged, heads):
            e = jnp.exp(s - jnp.max(s, axis=1, keepdims=True))
            p = e * (1.0 / jnp.sum(e, axis=1, keepdims=True))
            pb = p.astype(BF16)
            o = dot32(pb, vm[:w], NN)
            delta = jnp.sum(o * dom[r0:w].astype(F32), axis=1, keepdims=True)
            ds = (p * (dp - delta)).astype(BF16)
            att, dq = att + o, dq + dot32(ds, km[:w], NN)
            dvp, dkp = dvp + dot32(pb, dom[r0:w], TN), dkp + dot32(ds, qm[r0:w], TN)
        att_ref[r0:w, :] = att.astype(BF16)
        dmix_ref[r0:w, 0:width] = turn(dq * scale, cos[r0:w], sa[r0:w], sb[r0:w], -1).astype(BF16)
        if i > 0:
            dk_scr[:r0] += dkp[:r0]
            dv_scr[:r0] += dvp[:r0]
        dk_scr[r0:w] = dkp[r0:]
        dv_scr[r0:w] = dvp[r0:]
    dmix_ref[:, width : 2 * width] = turn(dk_scr[...], cos, sa, sb, -1).astype(BF16)
    dmix_ref[:, 2 * width : 3 * width] = dv_scr[...].astype(BF16)
    part = jnp.sum(dmix_ref[...].astype(F32), axis=0, keepdims=True)

    @pl.when(seq == 0)
    def _():
        sum_ref[pair] = part

    @pl.when(seq > 0)
    def _():
        sum_ref[pair] += part


def attention(pieces, place, an, dy, bias, tables, length):
    rows, depth = an.shape
    width = 2 * HD
    seqs = rows // length
    count = bias.shape[1] // (3 * width)
    row = pl.BlockSpec((length, depth), lambda s, j, p: (s, 0))
    table = pl.BlockSpec((length, width), lambda s, j, p: (s, 0))
    arrays = [v[0] for v in pieces]
    units = seqs * count
    shapes = [
        jax.ShapeDtypeStruct((rows, count * width), BF16),
        jax.ShapeDtypeStruct((rows, count * 3 * width), BF16),
        jax.ShapeDtypeStruct((count, 1, 3 * width), F32),
        jax.ShapeDtypeStruct((depth, count * 3 * width), BF16),
        jax.ShapeDtypeStruct((depth, count * width), BF16),
    ]
    return pl.pallas_call(
        partial(attention_kernel, keys=[v[1:] for v in pieces], bq=min(512, length)),
        grid_spec=pltpu.PrefetchScalarGridSpec(
            num_scalar_prefetch=1,
            grid=(seqs, count),
            in_specs=[row, row, whole_spec(bias), table, table] + [whole_spec(v) for v in arrays],
            out_specs=[
                pl.BlockSpec((length, width), lambda s, j, p: (s, j)),
                pl.BlockSpec((length, 3 * width), lambda s, j, p: (s, j)),
            ]
            + [whole_spec(v) for v in shapes[2:]],
            scratch_shapes=[
                pltpu.VMEM((count, length, 3 * width), F32),
                pltpu.VMEM((count, length, width), BF16),
                pltpu.VMEM((length, width), F32),
                pltpu.VMEM((length, width), F32),
            ],
        ),
        out_shape=shapes,
        compiler_params=pltpu.CompilerParams(vmem_limit_bytes=VMEM_BYTES),
        cost_estimate=pl.CostEstimate(
            flops=units * (32 * length * length * width + 8 * length * depth * width),
            bytes_accessed=units * length * (depth * 4 + width * 40),
            transcendentals=units * 2 * length * length,
        ),
        name="attention",
    )(place, an, dy, bias, *tables, *arrays)


def mlp_kernel(place_ref, mn_ref, dy_ref, bias_ref, *refs, keys, count):
    piece_refs, refs = refs[: len(keys)], refs[len(keys) :]
    act_ref, dgate_ref, sum_ref, up_ref, down_ref = refs
    units = up_ref.shape[1] // count
    step = pl.program_id(0)

    @pl.when(step == 0)
    def _():
        sum_ref[...] = jnp.zeros_like(sum_ref)
        for ref, (key, parts) in zip(piece_refs, keys):
            into = place_rows(ref, key, place_ref, up_ref)
            for j, lead in parts:
                up_ref[into, j * units : (j + 1) * units] = ref[:, lead : lead + units]
                down_ref[into, j * units : (j + 1) * units] = ref[:, lead + units : lead + 2 * units]

    for c in range(0, up_ref.shape[1], units):
        col = slice(c, c + units)
        gate = dot32(mn_ref[...], up_ref[:, col], NN) + bias_ref[:, col]
        dact = dot32(dy_ref[...], down_ref[:, col], NN)
        cdf = 0.5 + 0.5 * lax.erf(gate * math.sqrt(0.5))
        pdf = jnp.exp(gate * gate * -0.5) * (1.0 / math.sqrt(2.0 * math.pi))
        act_ref[:, col] = (gate * cdf).astype(BF16)
        dgate = (dact * (cdf + gate * pdf)).astype(BF16)
        dgate_ref[:, col] = dgate
        sum_ref[:, col] += jnp.sum(dgate.astype(F32), axis=0, keepdims=True)


def mlp(pieces, place, mn, dy, bias, count):
    rows, depth = mn.shape
    units = bias.shape[1]
    br = min(512, rows)
    row = pl.BlockSpec((br, depth), lambda r, p: (r, 0))
    tile = pl.BlockSpec((br, units), lambda r, p: (r, 0))
    arrays = [v[0] for v in pieces]
    shapes = [
        jax.ShapeDtypeStruct((rows, units), BF16),
        jax.ShapeDtypeStruct((rows, units), BF16),
        jax.ShapeDtypeStruct((1, units), F32),
        jax.ShapeDtypeStruct((depth, units), BF16),
        jax.ShapeDtypeStruct((depth, units), BF16),
    ]
    return pl.pallas_call(
        partial(mlp_kernel, keys=[v[1:] for v in pieces], count=count),
        grid_spec=pltpu.PrefetchScalarGridSpec(
            num_scalar_prefetch=1,
            grid=(rows // br,),
            in_specs=[row, row, whole_spec(bias)] + [whole_spec(v) for v in arrays],
            out_specs=[tile, tile] + [whole_spec(v) for v in shapes[2:]],
        ),
        out_shape=shapes,
        compiler_params=pltpu.CompilerParams(vmem_limit_bytes=VMEM_BYTES),
        cost_estimate=pl.CostEstimate(
            flops=4 * rows * depth * units,
            bytes_accessed=rows * depth * 4 + units * depth * 8 + rows * units * 4,
            transcendentals=2 * rows * units,
        ),
        name="mlp",
    )(place, mn, dy, bias, *arrays)


def block_shapes(places, depth, wa, wb, count):
    if places != 4:
        return (0,), [jax.ShapeDtypeStruct((depth, wa + wb), BF16)]
    far = jax.ShapeDtypeStruct((depth // 4, (wa + wb) // count), BF16)
    near = jax.ShapeDtypeStruct((depth // 4, wa + wb), BF16)
    return (3, 1, 2, 0), [far] * count + [near] * 3


def put_blocks(outs, sum_a, sum_b, place_ref, count, keys):
    wa, wb = sum_a.shape[1] // count, sum_b.shape[1] // count
    width = wa + wb
    for j in range(count):
        for n, key in enumerate(keys):
            out = outs[j] if key == 3 else outs[n + count - 1 if len(keys) > 1 else 0]
            at = place_rows(out, key, place_ref, sum_a)
            first = 0 if key == 3 else j * width
            out[:, first : first + wa] = sum_a[at, j * wa : (j + 1) * wa].astype(BF16)
            out[:, first + wa : first + width] = sum_b[at, j * wb : (j + 1) * wb].astype(BF16)


def grads_kernel(place_ref, left_a, left_b, right_a, right_b, *refs, count, keys):
    outs, (sum_a, sum_b) = refs[:-2], refs[-2:]
    step = pl.program_id(0)

    @pl.when(step == 0)
    def _():
        sum_a[...] = dot32(left_a[...], right_a[...], TN)
        sum_b[...] = dot32(left_b[...], right_b[...], TN)

    @pl.when(step > 0)
    def _():
        sum_a[...] += dot32(left_a[...], right_a[...], TN)
        sum_b[...] += dot32(left_b[...], right_b[...], TN)

    @pl.when(step == pl.num_programs(0) - 1)
    def _():
        put_blocks(outs, sum_a, sum_b, place_ref, count, keys)


def weight_grads(place, places, left_a, right_a, left_b, right_b, count):
    rows, depth = left_a.shape
    br = min(512 if right_a.shape[1] == right_b.shape[1] else 1024, rows)
    wa, wb = right_a.shape[1], right_b.shape[1]
    block = lambda v: pl.BlockSpec((br, v.shape[1]), lambda i, p: (i, 0))
    keys, shapes = block_shapes(places, depth, wa, wb, count)
    found = pl.pallas_call(
        partial(grads_kernel, count=count, keys=keys),
        grid_spec=pltpu.PrefetchScalarGridSpec(
            num_scalar_prefetch=1,
            grid=(rows // br,),
            in_specs=[block(v) for v in (left_a, left_b, right_a, right_b)],
            out_specs=[whole_spec(v) for v in shapes],
            scratch_shapes=[pltpu.VMEM((depth, wa), F32), pltpu.VMEM((depth, wb), F32)],
        ),
        out_shape=shapes,
        compiler_params=pltpu.CompilerParams(vmem_limit_bytes=VMEM_BYTES),
        cost_estimate=pl.CostEstimate(
            flops=2 * rows * depth * (wa + wb),
            bytes_accessed=4 * rows * depth + 2 * (wa + wb) * (rows + depth),
            transcendentals=0,
        ),
        name="weight_grads",
    )(place, left_a, left_b, right_a, right_b)
    return found


def row_norm(x):
    centre = x - jnp.mean(x, axis=-1, keepdims=True)
    rstd = lax.rsqrt(jnp.mean(centre * centre, axis=-1, keepdims=True) + EPS)
    return centre * rstd, rstd


def pull_kernel(*refs):
    dg0, up0, dg1, up1, dm0, qkv0, dm1, qkv1, x_ref, gain_ref = refs[:10]
    out_ref, sum_ref = refs[-2:]
    n_mlp = dot32(dg0[...], up0[...], NT) + dot32(dg1[...], up1[...], NT)
    n_attn = dot32(dm0[...], qkv0[...], NT) + dot32(dm1[...], qkv1[...], NT)
    xhat, rstd = row_norm(x_ref[...].astype(F32))
    u = n_attn * gain_ref[0:1, :] + n_mlp * gain_ref[2:3, :]
    parts = [jnp.sum(v, axis=0, keepdims=True) for v in (n_attn * xhat, n_attn, n_mlp * xhat, n_mlp)]
    part = jnp.concatenate(parts + [jnp.zeros((4, u.shape[1]), F32)], axis=0)

    @pl.when(pl.program_id(0) == 0)
    def _():
        sum_ref[...] = part

    @pl.when(pl.program_id(0) > 0)
    def _():
        sum_ref[...] += part

    out_ref[...] = u.astype(out_ref.dtype)


def pull_back(terms, x, gains, first_row, dtype):
    rows, depth = x.shape
    br = min(256, rows)
    first = first_row // br
    block = lambda v: pl.BlockSpec((br, v.shape[1]), lambda i: (i + first, 0))
    specs, args = [], []
    for grad, weight in terms:
        specs += [block(grad), whole_spec(weight)]
        args += [grad, weight]
    tile = pl.BlockSpec((br, depth), lambda i: (i, 0))
    width = sum(grad.shape[1] for grad, _ in terms)
    return pl.pallas_call(
        pull_kernel,
        grid=(rows // br,),
        in_specs=specs + [tile, whole_spec(gains)],
        out_specs=[tile, pl.BlockSpec((8, depth), lambda i: (0, 0))],
        out_shape=[jax.ShapeDtypeStruct((rows, depth), dtype), jax.ShapeDtypeStruct((8, depth), F32)],
        compiler_params=pltpu.CompilerParams(vmem_limit_bytes=VMEM_BYTES),
        cost_estimate=pl.CostEstimate(
            flops=2 * rows * width * depth,
            bytes_accessed=2 * width * (rows + depth) + rows * depth * 8,
            transcendentals=rows,
        ),
        name="pull_back",
    )(*args, x, gains)


def out_kernel(*refs, own):
    att0, out0, att1, out1, act0, down0, act1, down1 = refs[:8]
    y = dot32(act0[...], down0[...], NT) + dot32(act1[...], down1[...], NT)
    y = y + dot32(att0[...], out0[...], NT) + dot32(att1[...], out1[...], NT)
    if not own:
        refs[-1][...] = y.astype(BF16)
        return
    x_ref, other_ref, bias_ref, dy_ref, pull_ref, other_pull_ref, y_ref, grad_ref = refs[8:]
    x = x_ref[...].astype(F32)
    y_ref[...] = (y + x + other_ref[...].astype(F32) + bias_ref[...]).astype(BF16)
    xhat, rstd = row_norm(x)
    u = pull_ref[...] + other_pull_ref[...].astype(F32)
    u = u - jnp.mean(u, axis=-1, keepdims=True) - xhat * jnp.mean(u * xhat, axis=-1, keepdims=True)
    grad_ref[...] = dy_ref[...].astype(F32) + rstd * u


def branch_out(terms, rows, last=None):
    own = last is not None
    depth = terms[0][1].shape[0]
    br = min(256, rows)
    first = 0 if own else rows // br
    tile = pl.BlockSpec((br, depth), lambda i: (i, 0))
    specs, args = [], []
    for value, weight in terms:
        specs += [pl.BlockSpec((br, value.shape[1]), lambda i: (i + first, 0)), whole_spec(weight)]
        args += [value, weight]
    if own:
        specs += [whole_spec(v) if v.shape[0] == 1 else tile for v in last]
        args += last
    width = sum(value.shape[1] for value, _ in terms)
    shapes = [jax.ShapeDtypeStruct((rows, depth), BF16)] + [jax.ShapeDtypeStruct((rows, depth), F32)] * own
    return pl.pallas_call(
        partial(out_kernel, own=own),
        grid=(rows // br,),
        in_specs=specs,
        out_specs=[tile] * len(shapes),
        out_shape=shapes,
        compiler_params=pltpu.CompilerParams(vmem_limit_bytes=VMEM_BYTES),
        cost_estimate=pl.CostEstimate(
            flops=2 * rows * width * depth,
            bytes_accessed=2 * width * (rows + depth) + rows * depth * (18 if own else 2),
            transcendentals=0,
        ),
        name="branch_out",
    )(*args)


class Links:
    def __init__(self):
        self.fsdp = lax.axis_size("fsdp")
        self.tp = lax.axis_size("tp")
        index = lax.axis_index("fsdp")
        self.core = index % 2
        self.place = index // 2
        self.lane = lax.axis_index("tp")
        self.places = self.fsdp // 2
        self.cores = [list(range(c, self.fsdp, 2)) for c in range(2)]
        self.bits = [1 << b for b in range((self.places - 1).bit_length())]

    def swap(self, value):
        return lax.ppermute(value, "fsdp", [(i, i ^ 1) for i in range(self.fsdp)])

    def hop(self, value, bit):
        return lax.ppermute(value, "fsdp", [(i, i ^ (2 * bit)) for i in range(self.fsdp)])

    def ring(self, value):
        return lax.ppermute(value, "tp", [(i, (i + 1) % self.tp) for i in range(self.tp)])


    def near_places(self, piece):
        return self.hop(piece, 1), self.hop(piece, 2)

    def far_parts(self, near):
        cut = near[0].shape[1] // 2
        return near[1][:, :cut], near[0][:, cut:]

    def far_place(self, parts):
        return self.hop(parts[0], 1), self.hop(parts[1], 2)

    def scatter_far(self, far):
        return self.hop(far[0], 2), self.hop(far[1], 1)

    def add_far(self, one, two, far):
        cut = one.shape[1] // 2
        first = (one[:, :cut].astype(F32) + far[0].astype(F32)).astype(BF16)
        second = (two[:, cut:].astype(F32) + far[1].astype(F32)).astype(BF16)
        return lax.dynamic_update_slice(one, first, (0, 0)), lax.dynamic_update_slice(two, second, (0, cut))

    def scatter_near(self, one, two):
        return self.hop(one, 1), self.hop(two, 2)

    def gather_other(self, piece):
        return lax.all_gather(piece, "fsdp", axis=0, tiled=True, axis_index_groups=self.cores)

    def scatter_other(self, value):
        return lax.psum_scatter(
            value, "fsdp", scatter_dimension=0, tiled=True, axis_index_groups=self.cores
        )

    def back(self, value):
        return lax.ppermute(value, "tp", [(i, (i - 1) % self.tp) for i in range(self.tp)])

    def across(self, value):
        return lax.ppermute(value, "tp", [(i, (i + 2) % self.tp) for i in range(self.tp)])

    def ring_sum(self, total, terms):
        for term in terms:
            total = term if total is None else total + term
            total = self.ring(total.astype(BF16)).astype(F32)
        return total

    def sum_steps(self):
        steps = [("fsdp", self.fsdp, 1 << b) for b in range((self.fsdp - 1).bit_length())]
        return steps + [("tp", self.tp, 1 << b) for b in range((self.tp - 1).bit_length())]

    def sum_step(self, value, step):
        name, size, bit = step
        return value + lax.ppermute(value, name, [(i, i ^ bit) for i in range(size)])


def pick(value, index, axis):
    return lax.dynamic_index_in_dim(value, index, axis, keepdims=False)


def pair_rows(links, mine, other):
    got = links.swap(other)
    first = jnp.where(links.core == 0, mine, got)
    second = jnp.where(links.core == 0, got, mine)
    return jnp.concatenate([first, second], axis=0)


def unpair_rows(links, block):
    half = block.shape[0] // 2
    mine = lax.dynamic_slice_in_dim(block, links.core * half, half, 0)
    got = links.swap(lax.dynamic_slice_in_dim(block, (1 - links.core) * half, half, 0))
    return jnp.where(links.core == 0, mine, got), jnp.where(links.core == 0, got, mine)


sync = lax.optimization_barrier


def tables_of(segment_rows):
    length = segment_rows.shape[1]
    starts = jnp.sum((segment_rows[:, None, :] < segment_rows[:, :, None]).astype(jnp.int32), axis=-1)
    places = (jnp.arange(length, dtype=jnp.int32)[None] - starts).reshape(-1).astype(F32)
    inverse_freq = jnp.power(10000.0, -jnp.arange(0, ROT, 2, dtype=F32) / ROT)
    angles = inverse_freq[:, None] * places[None, :]
    turns = jnp.concatenate([jnp.cos(angles), jnp.sin(angles)], axis=0)
    marks = segment_rows.reshape(-1, 1) == jnp.arange(2 * HD, dtype=jnp.int32)[None, :]
    return jnp.tile(turns.T, (1, 2 * HD // ROT)), marks.astype(BF16)


def body(
    tokens,
    segments,
    attn_gain,
    attn_shift,
    mlp_gain,
    mlp_shift,
    qkv_weight,
    qkv_bias,
    out_weight,
    out_bias,
    up_weight,
    up_bias,
    down_weight,
    down_bias,
    cotangent,
):
    links = Links()
    tp = links.tp
    rows, depth = tokens.shape
    length = segments.shape[1]
    head_cols = qkv_weight.shape[2] // 2
    unit_cols = up_weight.shape[1] // 2

    def halves(shard, axis):
        size = shard.shape[axis] // 2
        return [lax.dynamic_slice_in_dim(shard, c * size, size, axis) for c in (links.core, 1 - links.core)]

    qkv_halves = [v.reshape(v.shape[0], -1) for v in halves(qkv_weight, 2)]
    out_halves = [v.T for v in halves(out_weight, 0)]
    up_halves = halves(up_weight, 1)
    down_halves = [v.T for v in halves(down_weight, 0)]
    attn_slots = [pair_rows(links, *[jnp.concatenate(v, axis=1) for v in zip(qkv_halves, out_halves)])]
    mlp_slots = [pair_rows(links, *[jnp.concatenate(v, axis=1) for v in zip(up_halves, down_halves)])]
    qkv_cols = 3 * head_cols

    half = tp // 2
    per = max(1, 2 * HD // head_cols)

    by_hops = links.places == 4 and per == 1 and tp == 4
    place = jnp.full((1,), links.place if by_hops else 0, jnp.int32)

    def join_pair(slots):
        if per == 1:
            return slots[0]
        lead = slots[0].shape[0]
        return jnp.concatenate([v.reshape(lead, 4, head_cols) for v in slots], axis=2).reshape(lead, -1)

    def join_qkv(slots):
        if per == 1:
            return slots[0]
        lead = slots[0].shape[0]
        return jnp.concatenate([v.reshape(lead, 3, head_cols) for v in slots], axis=2).reshape(lead, -1)

    def split_pair(value, parts):
        if per == 1:
            return [value]
        lead = value.shape[0]
        blocks = value.reshape(lead, parts, per, head_cols)
        return [blocks[:, :, j].reshape(lead, -1) for j in range(per)]

    groups = [list(range(0, half)), list(range(half, tp))]
    mlp_groups = [[1, 3], [0, 2]] if by_hops else groups

    lane_of = [(links.lane - s) % tp for s in range(tp)]
    qkv_bias_lanes = pick(qkv_bias.reshape(3, tp, 2, head_cols), links.core, 2)
    up_bias_lanes = pick(up_bias.reshape(tp, 2, unit_cols), links.core, 1)
    qkv_bias_groups = [
        jnp.concatenate(
            [
                join_qkv([pick(qkv_bias_lanes, lane_of[s], 1).reshape(1, -1) for s in g[i : i + per]])
                for i in range(0, half, per)
            ],
            axis=1,
        ).astype(F32)
        for g in groups
    ]
    up_bias_groups = [
        jnp.concatenate([pick(up_bias_lanes, lane_of[s], 0) for s in g]).astype(F32)[None] for g in mlp_groups
    ]

    gains = jnp.stack([v.astype(F32) for v in (attn_gain, attn_shift, mlp_gain, mlp_shift)])
    x_other, dy_other = links.swap(tokens), links.swap(cotangent)

    def group_piece(slots):
        return jnp.concatenate(slots, axis=1)

    def near(piece):
        return links.near_places(piece) if by_hops else links.gather_other(piece)

    def far_parts(got):
        return links.far_parts(got) if by_hops else ()

    def far(parts):
        return links.far_place(parts) if by_hops else ()

    def pieces_of(piece, got, last, width):
        both = tuple((j, j * width) for j in range(half))
        if not by_hops:
            return [(got, 0, both)]
        return [(piece, 0, both), (got[0], 1, both), (got[1], 2, both), (last[0], 3, ((0, 0),)), (last[1], 3, ((1, 0),))]

    def attention_part(g, pieces, an, dy):
        if per > 1:
            slots = jnp.split(pieces[0][0], half, axis=1)
            whole = jnp.concatenate([join_pair(slots[i : i + per]) for i in range(0, half, per)], axis=1)
            pieces = [(whole, 0, tuple((j, j * 8 * HD) for j in range(half // per)))]
        return attention(pieces, place, an, dy, qkv_bias_groups[g], tables, length)

    def attention_grads(attended, dmixed):
        found = weight_grads(place, links.places if by_hops else 1, an, dmixed, dy2, attended, half // per)
        if per == 1:
            return found
        pairs = jnp.split(found[0], half // per, axis=1)
        return [jnp.concatenate([v for pair in pairs for v in split_pair(pair, 4)], axis=1)]

    def mlp_part(g, pieces, mn, dy):
        return mlp(pieces, place, mn, dy, up_bias_groups[g], half)

    def mlp_grads(active, dgate):
        return weight_grads(place, links.places if by_hops else 1, mn, dgate, dy2, active, half)

    def sum_far(blocks):
        return links.scatter_far(blocks[:2]) if by_hops else links.scatter_other(blocks[0])

    def add_far(blocks, got):
        return links.add_far(blocks[2], blocks[3], got) if by_hops else got

    def sum_near(sent):
        return links.scatter_near(*sent) if by_hops else sent

    def place_sum(blocks, got):
        if by_hops:
            got = blocks[4].astype(F32) + got[0].astype(F32) + got[1].astype(F32)
        return jnp.split(got.astype(F32), half, axis=1)

    def small_sums():
        def spread(values):
            lead, cols = values[0].shape
            full = jnp.zeros((lead, tp, 2, cols), F32)
            for s, value in enumerate(values):
                full = lax.dynamic_update_slice(full, value.reshape(lead, 1, 1, cols), (0, lane_of[s], links.core, 0))
            return full.reshape(-1)

        pair_sums = [v[i] for v in (qkv_sum0, qkv_sum1) for i in range(half // per)]
        qkv_bias_part = spread([v.reshape(3, head_cols) for d in pair_sums for v in split_pair(d, 3)])
        gate_sums = [v for part in (gate_sum0, gate_sum1) for v in jnp.split(part, half, axis=1)]
        order = mlp_groups[0] + mlp_groups[1]
        up_bias_part = spread([gate_sums[order.index(s)] for s in range(tp)])
        bias_part = jnp.sum(cotangent.astype(F32), axis=0)
        pieces = [
            *(sums_own + sums_other)[:4],
            qkv_bias_part,
            bias_part,
            up_bias_part,
        ]
        return jnp.concatenate(pieces).reshape(-1, 128)

    sizes = [depth] * 4 + [qkv_bias.size, depth, up_bias.size]

    attn_cols, mlp_cols = 4 * head_cols, 2 * unit_cols
    ring, back = links.ring, links.back
    own_segments = lax.dynamic_slice_in_dim(segments, links.lane * rows // length, rows // length, 0)
    pair_segments = jnp.concatenate([own_segments, links.swap(own_segments)], axis=0)
    attn_slots, pair_segments = sync((attn_slots, pair_segments))
    if by_hops:
        attn = {0: attn_slots[0], 1: ring(attn_slots[0])}
        units = {0: mlp_slots[0]}
        got = [links.near_places(attn[0])]
        attn, units, pair_segments = sync((attn, units, pair_segments))
        got.append(links.near_places(attn[1]))
        units[1], units[3] = ring(units[0]), back(units[0])
        tables = tables_of(pair_segments)
        got, x_other, dy_other = sync((got, x_other, dy_other))
        last = [links.hop(got[0][1], 1), links.hop(got[1][0], 2)]
        normed = prepare(tokens, x_other, cotangent, dy_other, gains)
        units, last, normed, tables = sync((units, last, normed, tables))
        piece_b = group_piece([units[1], units[3]])
        piece_b, normed = sync((piece_b, normed))
        group_a = [
            (v, key, ((j, 0),))
            for j in (0, 1)
            for v, key in ((attn[j], 0), (got[j][0], 1), (got[j][1], 2), (last[j], 3))
        ]
    else:
        attn, units = {0: attn_slots[0]}, {0: mlp_slots[0]}
        for s in range(1, tp):
            attn[s] = ring(attn[s - 1])
            units[s] = ring(units[s - 1])
        tables = tables_of(pair_segments)
        normed = prepare(tokens, x_other, cotangent, dy_other, gains)
        group_a = pieces_of(None, near(group_piece([attn[s] for s in groups[0]])), None, attn_cols)
    an, mn, dy2 = normed
    if not by_hops:
        piece_b, piece_c, piece_d = [
            group_piece([v[s] for s in g]) for v, g in ((units, groups[0]), (units, groups[1]), (attn, groups[1]))
        ]
    piece_b, an = sync((piece_b, an))

    near_b = near(piece_b)
    if by_hops:
        units[2] = ring(units[1])
    att0, dmix0, qkv_sum0, qkv0, out0 = attention_part(0, group_a, an, dy2)
    near_b, attn, units, att0 = sync((near_b, attn, units, att0))
    parts_b = far_parts(near_b)
    if by_hops:
        piece_c = group_piece([units[0], units[2]])
    parts_b, piece_c, att0 = sync((parts_b, piece_c, att0))

    far_b = far(parts_b)
    if by_hops:
        attn[2], attn[3] = ring(attn[1]), back(attn[0])
    grad_a = attention_grads(att0, dmix0)
    far_b, grad_a, mn = sync((far_b, grad_a, mn))

    near_c = near(piece_c)
    act0, dgate0, gate_sum0, up0, down0 = mlp_part(0, pieces_of(piece_b, near_b, far_b, mlp_cols), mn, dy2)
    near_c, attn, act0 = sync((near_c, attn, act0))
    parts_c = far_parts(near_c)
    parts_c, act0 = sync((parts_c, act0))

    far_c = far(parts_c)
    back_a = sum_far(grad_a)
    grad_b = mlp_grads(act0, dgate0)
    far_c, back_a, grad_b, mn = sync((far_c, back_a, grad_b, mn))
    if by_hops:
        piece_d = group_piece([attn[2], attn[3]])
    sent_a = add_far(grad_a, back_a)
    piece_d, sent_a, mn = sync((piece_d, sent_a, mn))

    near_d = near(piece_d)
    near_a = sum_near(sent_a)
    act1, dgate1, gate_sum1, up1, down1 = mlp_part(1, pieces_of(piece_c, near_c, far_c, mlp_cols), mn, dy2)
    near_d, near_a, act1 = sync((near_d, near_a, act1))
    parts_d = far_parts(near_d)
    parts_d, act1 = sync((parts_d, act1))

    far_d = far(parts_d)
    back_b = sum_far(grad_b)
    grad_c = mlp_grads(act1, dgate1)
    far_d, back_b, grad_c, an = sync((far_d, back_b, grad_c, an))
    sent_b = add_far(grad_b, back_b)
    sum_a = place_sum(grad_a, near_a)
    sent_b, sum_a, grad_c, an = sync((sent_b, sum_a, grad_c, an))

    back_near_b = sum_near(sent_b)
    back_c = sum_far(grad_c)
    att1, dmix1, qkv_sum1, qkv1, out1 = attention_part(1, pieces_of(piece_d, near_d, far_d, attn_cols), an, dy2)
    back_near_b, back_c, att1 = sync((back_near_b, back_c, att1))
    sent_c = add_far(grad_c, back_c)
    sum_b = place_sum(grad_b, back_near_b)
    sent_c, sum_b, att1 = sync((sent_c, sum_b, att1))

    back_near_c = sum_near(sent_c)
    lanes_m = ring(sum_b[1].astype(BF16)) if by_hops else ()
    grad_d = attention_grads(att1, dmix1)
    grad_d, dgate1 = sync((grad_d, dgate1))

    back_d = sum_far(grad_d)
    terms = ((dgate0, up0), (dgate1, up1), (dmix0, qkv0), (dmix1, qkv1))
    sent_pull, sums_other = pull_back(terms, x_other, gains, rows, BF16)
    back_near_c, back_d, lanes_m, sent_pull, att1 = sync((back_near_c, back_d, lanes_m, sent_pull, att1))
    sum_c = place_sum(grad_c, back_near_c)
    last_m = sum_c[1].astype(BF16) if by_hops else ()
    sent_d = add_far(grad_d, back_d)
    sent_d, last_m, sent_pull, att1 = sync((sent_d, last_m, sent_pull, att1))

    back_near_d = sum_near(sent_d)
    last_m = back(last_m) if by_hops else ()
    other_pull = links.swap(sent_pull)
    out_terms = ((att0, out0), (att1, out1), (act0, down0), (act1, down1))
    (sent_out,) = branch_out(out_terms, rows)
    back_near_d, other_pull, last_m, sent_out, dgate1 = sync((back_near_d, other_pull, last_m, sent_out, dgate1))
    sum_d = place_sum(grad_d, back_near_d)
    lanes_a = [v.astype(BF16) for v in sum_d]
    if by_hops:
        last_m = (sum_b[0] + last_m.astype(F32)).astype(BF16)
    lanes_a, last_m, sent_out, dgate1 = sync((lanes_a, last_m, sent_out, dgate1))

    other_out = links.swap(sent_out)
    if by_hops:
        lanes_a = [back(lanes_a[0]), ring(lanes_a[1])]
        last_m = back(last_m)
    terms = ((dgate0, up0), (dgate1, up1), (dmix0, qkv0), (dmix1, qkv1))
    pulled, sums_own = pull_back(terms, tokens, gains, 0, F32)
    lanes_a, last_m, other_out, sums_own, att1 = sync((lanes_a, last_m, other_out, sums_own, att1))
    small = small_sums()
    steps = links.sum_steps()
    if by_hops:
        last_a = (sum_a[1] + lanes_a[0].astype(F32)).astype(BF16)
        sum_m = sum_c[0] + lanes_m.astype(F32) + last_m.astype(F32)
    else:
        last_a = ()
        sum_m = links.ring_sum(None, sum_b[1:] + sum_c) + sum_b[0]
    small, last_a, sum_m, att1 = sync((small, last_a, sum_m, att1))

    if by_hops:
        last_a = back(last_a)
    mlp_own = unpair_rows(links, sum_m)
    small = links.sum_step(small, steps[0])
    end_bias = (out_bias.astype(F32) + down_bias.astype(F32))[None]
    out_terms = ((att0, out0), (att1, out1), (act0, down0), (act1, down1))
    output, input_grad = branch_out(
        out_terms, rows, [tokens, other_out, end_bias, cotangent, pulled, other_pull]
    )
    small, last_a, mlp_own, output, input_grad = sync((small, last_a, mlp_own, output, input_grad))
    if by_hops:
        sum_e = sum_a[0] + lanes_a[1].astype(F32) + last_a.astype(F32)
    else:
        sum_e = links.ring_sum(None, sum_a[1:] + sum_d) + sum_a[0]
    attn_own = unpair_rows(links, sum_e)
    small = links.sum_step(links.sum_step(small, steps[1]), steps[2])
    if tp == 4 and links.fsdp == 8:
        a, b, c = [lax.ppermute(small, "tp", [(i, i ^ bit) for i in range(tp)]) for bit in (1, 2, 3)]
        small = (small + a) + (b + c)
    else:
        for step in steps[3:]:
            small = links.sum_step(small, step)
    up_grad = jnp.concatenate([v[:, :unit_cols] for v in mlp_own], axis=1)
    down_grad = jnp.concatenate([v[:, unit_cols:] for v in mlp_own], axis=1).T
    qkv_grad = jnp.concatenate([v[:, :qkv_cols].reshape(-1, 3, head_cols) for v in attn_own], axis=2)
    out_grad = jnp.concatenate([v[:, qkv_cols:] for v in attn_own], axis=1).T

    summed = small.reshape(-1)
    sums = []
    at = 0
    for size in sizes:
        sums.append(summed[at : at + size])
        at += size
    return (
        output,
        input_grad,
        sums[0],
        sums[1],
        sums[2],
        sums[3],
        qkv_grad,
        sums[4].reshape(qkv_bias.shape),
        out_grad,
        sums[5],
        up_grad,
        sums[6],
        down_grad,
        sums[5],
    )


def solution(mesh):
    placed = (
        P(("fsdp", "tp"), None),
        P("fsdp", None),
        P(),
        P(),
        P(),
        P(),
        P("fsdp", None, "tp"),
        P(),
        P("tp", "fsdp"),
        P(),
        P("fsdp", "tp"),
        P(),
        P("tp", "fsdp"),
        P(),
        P(("fsdp", "tp"), None),
    )
    return jax.shard_map(
        body,
        mesh=mesh,
        in_specs=placed,
        out_specs=(
            P(("fsdp", "tp"), None),
            P(("fsdp", "tp"), None),
            P(),
            P(),
            P(),
            P(),
            P("fsdp", None, "tp"),
            P(),
            P("tp", "fsdp"),
            P(),
            P("fsdp", "tp"),
            P(),
            P("tp", "fsdp"),
            P(),
        ),
        check_vma=False,
    )
```
